32 devices in a mesh: dp: 8 (over z, x), seq: 4 (over y, core).
Axes of the slice: x: 2, y: 2, z: 4, core: 2. Of those that a mesh axis runs over, the one named last changes fastest.
Arguments:
- frames: bfloat16 [12288, 768], P(('dp', 'seq')), may hold values from -6 to 6
- cotangent: bfloat16 [12288, 768], P(('dp', 'seq')), may hold values from -6 to 6
- lengths: int32 [8, 3], P('dp'), may hold values from 48 to 1440, as said below
- input_weight: bfloat16 [768, 2304], replicated, may hold values from -0.21875 to 0.21875
- output_weight: bfloat16 [768, 768], replicated, may hold values from -0.21875 to 0.21875
- expand_weight: bfloat16 [768, 3072], replicated, may hold values from -0.21875 to 0.21875
- reduce_weight: bfloat16 [3072, 768], replicated, may hold values from -0.109375 to 0.109375
- vector_copy: bfloat16 [12, 768], replicated, may hold values from -0.6 to 2.6
- input_master: float32 [768, 2304], P('dp', 'seq'), may hold values from -0.21875 to 0.21875
- output_master: float32 [768, 768], P('seq', 'dp'), may hold values from -0.21875 to 0.21875
- expand_master: float32 [768, 3072], P('seq', 'dp'), may hold values from -0.21875 to 0.21875
- reduce_master: float32 [3072, 768], P('seq', 'dp'), may hold values from -0.109375 to 0.109375
- vector_master: float32 [12, 768], P('seq', 'dp'), may hold values from -0.6 to 2.6
- input_first: float32 [768, 2304], P('dp', 'seq'), may hold values from -0.00024414062 to 0.00024414062
- output_first: float32 [768, 768], P('seq', 'dp'), may hold values from -0.00024414062 to 0.00024414062
- expand_first: float32 [768, 3072], P('seq', 'dp'), may hold values from -0.00024414062 to 0.00024414062
- reduce_first: float32 [3072, 768], P('seq', 'dp'), may hold values from -0.00024414062 to 0.00024414062
- vector_first: float32 [12, 768], P('seq', 'dp'), may hold values from -0.00024414062 to 0.00024414062
- input_second: float32 [768, 2304], P('dp', 'seq'), may hold values from 1.4110135e-10 to 5.644054e-10
- output_second: float32 [768, 768], P('seq', 'dp'), may hold values from 1.4110135e-10 to 5.644054e-10
- expand_second: float32 [768, 3072], P('seq', 'dp'), may hold values from 1.4110135e-10 to 5.644054e-10
- reduce_second: float32 [3072, 768], P('seq', 'dp'), may hold values from 1.4110135e-10 to 5.644054e-10
- vector_second: float32 [12, 768], P('seq', 'dp'), may hold values from 1.4110135e-10 to 5.644054e-10
Outputs:
- layer_output: bfloat16 [12288, 768], P(('dp', 'seq'))
- frames_gradient: float32 [12288, 768], P(('dp', 'seq'))
- gradient_norm: float32 [], replicated
- input_mean: float32 [768, 2304], P('dp', 'seq')
- input_square: float32 [768, 2304], P('dp', 'seq')
- input_new: float32 [768, 2304], P('dp', 'seq')
- input_rounded: bfloat16 [768, 2304], P('dp', 'seq')
- output_mean: float32 [768, 768], P('seq', 'dp')
- output_square: float32 [768, 768], P('seq', 'dp')
- output_new: float32 [768, 768], P('seq', 'dp')
- output_rounded: bfloat16 [768, 768], P('seq', 'dp')
- expand_mean: float32 [768, 3072], P('seq', 'dp')
- expand_square: float32 [768, 3072], P('seq', 'dp')
- expand_new: float32 [768, 3072], P('seq', 'dp')
- expand_rounded: bfloat16 [768, 3072], P('seq', 'dp')
- reduce_mean: float32 [3072, 768], P('seq', 'dp')
- reduce_square: float32 [3072, 768], P('seq', 'dp')
- reduce_new: float32 [3072, 768], P('seq', 'dp')
- reduce_rounded: bfloat16 [3072, 768], P('seq', 'dp')
- vector_mean: float32 [12, 768], P('seq', 'dp')
- vector_square: float32 [12, 768], P('seq', 'dp')
- vector_new: float32 [12, 768], P('seq', 'dp')
- vector_rounded: bfloat16 [12, 768], P('seq', 'dp')
The draws below stay inside these ranges and needn't reach their ends.
Inputs may be any that keep to these rules, and one draw needn't show every extreme that they name: `lengths`: the utterances of a group stand end to end from the group's first frame; the group's frames after the last one are padding.
All inputs are finite; a program needn't handle non-finite values.
Results may differ from the reference program's by a relative error of at most 0.012.
Values may be sent and summed in bfloat16 or wider, within the bound.
No kernel may reach another device: no remote copies, remote signals or barrier semaphores. Data moves between devices by JAX's collectives and lax.ppermute only.
A program may use at most 128 MiB of HBM per device.

```python
import math
import jax
import jax.numpy as jnp
from jax import lax

D = 768
FF = 3072
HD = 64
TOK_DEV = 384
UTT = 3
STEP = 10
SLAB = 1536
GROUPS = 8
TOKENS = 12288


def vector_rows(key, gain_low, gain_high, bias_scale):
    noise_key, bias_key = jax.random.split(key)
    gain_ramp = jnp.linspace(gain_low, gain_high, D, dtype=jnp.float32)
    jitter = jnp.exp(jax.random.uniform(noise_key, (12, D), jnp.float32, -0.22, 0.22))
    biases = bias_scale * jax.random.uniform(bias_key, (12, D), jnp.float32, -1.7, 1.7)
    is_gain = (jnp.arange(12) == 3) | (jnp.arange(12) == 6)
    return jnp.where(is_gain[:, None], gain_ramp[None, :] * jitter, biases)


def draw_vector_copy(key, part):
    key = jax.random.fold_in(key, 21)
    return vector_rows(key, 0.5, 1.5, 0.2).astype(jnp.bfloat16)


def draw_vector_master(key, part):
    key = jax.random.fold_in(key, 22)
    return vector_rows(key, 0.5, 1.5, 0.2)


def draw_lengths(key, part):
    key = jax.random.fold_in(key, 5)
    short_key, pad_key, place_key = jax.random.split(key, 3)
    lowest = max(TOK_DEV // 8, 1)
    highest = TOK_DEV // 4 + 1
    shorts = jax.random.randint(short_key, (GROUPS, UTT - 1), lowest, highest)
    padding = jax.random.randint(pad_key, (GROUPS,), 0, TOK_DEV // 4 + 1)
    shorts = shorts.at[0].set(lowest)
    padding = padding.at[0].set(0)
    longest = SLAB - padding - jnp.sum(shorts, axis=1)
    stacked = jnp.concatenate([longest[:, None], shorts], axis=1)
    position_long = jax.random.randint(place_key, (GROUPS, 1), 0, UTT)
    column = (jnp.arange(UTT)[None, :] - position_long) % UTT
    return jnp.take_along_axis(stacked, column, axis=1).astype(jnp.int32)


def steps_of(key, dims, cuts, low, high):
    gain, own = 1.0, jax.random.fold_in(key, 6)
    for dim, parts in cuts:
        steps = jnp.exp(jax.random.uniform(jax.random.fold_in(own, dim), (parts,), jnp.float32, low / len(cuts), high / len(cuts)))
        gain = gain * jnp.repeat(steps, dims[dim] // parts).reshape([-1 if axis == dim else 1 for axis in range(len(dims))])
    return gain


def normal_values(key, extent, spread, most, cuts=(), kind=jnp.bfloat16):
    drawn = spread * jax.random.normal(key, extent, jnp.float32)
    if cuts:
        drawn = drawn * steps_of(key, extent, cuts, -0.22, 0.18)
    return jnp.clip(drawn, -most, most).astype(kind)


def setup_inputs(seed: int = 0) -> dict:
    arg_keys = jax.random.split(jax.random.key(seed), 24)
    return {
        "frames": normal_values(arg_keys[0], (TOKENS, D), 1.0, 6.0, ((0, 32),)),
        "cotangent": normal_values(arg_keys[1], (TOKENS, D), 1.0, 6.0, ((0, 32),)),
        "lengths": draw_lengths(jax.random.fold_in(arg_keys[23], 71), 0),
        "input_weight": normal_values(arg_keys[3], (D, 3 * D), D ** -0.5, 0.21875),
        "output_weight": normal_values(arg_keys[4], (D, D), D ** -0.5, 0.21875),
        "expand_weight": normal_values(arg_keys[5], (D, FF), D ** -0.5, 0.21875),
        "reduce_weight": normal_values(arg_keys[6], (FF, D), FF ** -0.5, 0.109375),
        "vector_copy": draw_vector_copy(jax.random.fold_in(arg_keys[23], 71), 0),
        "input_master": normal_values(arg_keys[8], (D, 3 * D), D ** -0.5, 0.21875, ((0, 8), (1, 4)), jnp.float32),
        "output_master": normal_values(arg_keys[9], (D, D), D ** -0.5, 0.21875, ((0, 4), (1, 8)), jnp.float32),
        "expand_master": normal_values(arg_keys[10], (D, FF), D ** -0.5, 0.21875, ((0, 4), (1, 8)), jnp.float32),
        "reduce_master": normal_values(arg_keys[11], (FF, D), FF ** -0.5, 0.109375, ((0, 4), (1, 8)), jnp.float32),
        "vector_master": draw_vector_master(jax.random.fold_in(arg_keys[23], 71), 0),
        "input_first": normal_values(arg_keys[13], (D, 3 * D), (0.111 / (4 * D * D + 2 * D * FF + 12 * D) ** 0.5), 0.00024414062, ((0, 8), (1, 4)), jnp.float32),
        "output_first": normal_values(arg_keys[14], (D, D), (0.111 / (4 * D * D + 2 * D * FF + 12 * D) ** 0.5), 0.00024414062, ((0, 4), (1, 8)), jnp.float32),
        "expand_first": normal_values(arg_keys[15], (D, FF), (0.111 / (4 * D * D + 2 * D * FF + 12 * D) ** 0.5), 0.00024414062, ((0, 4), (1, 8)), jnp.float32),
        "reduce_first": normal_values(arg_keys[16], (FF, D), (0.111 / (4 * D * D + 2 * D * FF + 12 * D) ** 0.5), 0.00024414062, ((0, 4), (1, 8)), jnp.float32),
        "vector_first": normal_values(arg_keys[17], (12, D), (0.111 / (4 * D * D + 2 * D * FF + 12 * D) ** 0.5), 0.00024414062, ((0, 4), (1, 8)), jnp.float32),
        "input_second": jnp.clip(jnp.exp(math.log(5.644054112963204e-10) - 1.3862944 * jax.random.uniform(arg_keys[18], (D, 3 * D), jnp.float32) ** steps_of(arg_keys[18], (D, 3 * D), ((0, 8), (1, 4)), -0.2, 0.2)), 1.411013528240801e-10, 5.644054112963204e-10),
        "output_second": jnp.clip(jnp.exp(math.log(5.644054112963204e-10) - 1.3862944 * jax.random.uniform(arg_keys[19], (D, D), jnp.float32) ** steps_of(arg_keys[19], (D, D), ((0, 4), (1, 8)), -0.2, 0.2)), 1.411013528240801e-10, 5.644054112963204e-10),
        "expand_second": jnp.clip(jnp.exp(math.log(5.644054112963204e-10) - 1.3862944 * jax.random.uniform(arg_keys[20], (D, FF), jnp.float32) ** steps_of(arg_keys[20], (D, FF), ((0, 4), (1, 8)), -0.2, 0.2)), 1.411013528240801e-10, 5.644054112963204e-10),
        "reduce_second": jnp.clip(jnp.exp(math.log(5.644054112963204e-10) - 1.3862944 * jax.random.uniform(arg_keys[21], (FF, D), jnp.float32) ** steps_of(arg_keys[21], (FF, D), ((0, 4), (1, 8)), -0.2, 0.2)), 1.411013528240801e-10, 5.644054112963204e-10),
        "vector_second": jnp.clip(jnp.exp(math.log(5.644054112963204e-10) - 1.3862944 * jax.random.uniform(arg_keys[22], (12, D), jnp.float32) ** steps_of(arg_keys[22], (12, D), ((0, 4), (1, 8)), -0.2, 0.2)), 1.411013528240801e-10, 5.644054112963204e-10),
    }


@jax.custom_vjp
def low(v):
    return lax.optimization_barrier(v.astype(jnp.bfloat16)).astype(jnp.float32)

@jax.custom_vjp
def low_back(v):
    return v

def low_keep(v):
    return (low(v), None)

def low_pass(kept, grad):
    return (grad,)

def back_keep(v):
    return (v, None)

def back_low(kept, grad):
    return (low(grad),)
low.defvjp(low_keep, low_pass)
low_back.defvjp(back_keep, back_low)
layer_eps = 1e-05
masked_score = -1000000000.0
highest = lax.Precision.HIGHEST
clip_limit = 1.0

def normalize(values, gain_row, shift_row):
    center = values - lax.optimization_barrier(jnp.mean(values, axis=-1, keepdims=True))
    normed = center * lax.rsqrt(lax.optimization_barrier(jnp.mean(center * center, axis=-1, keepdims=True)) + layer_eps)
    return normed * gain_row + shift_row

def smooth_gate(values):
    return values * 0.5 * (1.0 + jax.scipy.special.erf(values * 0.7071067811865476))

@jax.checkpoint
def attend_block(query_block, segment_block, key_rows, value_rows, segments):
    raw_scores = jnp.einsum('qhd,khd->hqk', query_block, key_rows, precision=highest)
    scores = low_back(raw_scores * HD ** (-0.5))
    allowed = segment_block[:, None] == segments[None, :]
    scores = jnp.where(allowed[None], scores, masked_score)
    row_top = lax.optimization_barrier(jnp.max(scores, axis=-1, keepdims=True))
    row_total = lax.optimization_barrier(jnp.sum(jnp.exp(scores - row_top), axis=-1, keepdims=True))
    weights_low = low(jnp.exp(scores - (row_top + jnp.log(row_total))))
    return jnp.einsum('hqk,khd->qhd', weights_low, value_rows, precision=highest)

def group_forward(frames_group, segments, input_weight, output_weight, expand_weight, reduce_weight, vectors):
    head_count = D // HD
    bias_row = jnp.concatenate([vectors[0], jnp.zeros_like(vectors[0]), vectors[1]])
    projected = jnp.dot(frames_group, input_weight, precision=highest) + bias_row
    projected = low_back(low(projected))
    queries = projected[:, :D].reshape(SLAB, head_count, HD)
    key_rows = projected[:, D:2 * D].reshape(SLAB, head_count, HD)
    value_rows = projected[:, 2 * D:].reshape(SLAB, head_count, HD)
    block_rows = min(512, SLAB)
    block_count = SLAB // block_rows
    query_blocks = queries.reshape(block_count, block_rows, head_count, HD)
    segment_blocks = segments.reshape(block_count, block_rows)
    mixed_heads = lax.map(lambda pieces: attend_block(pieces[0], pieces[1], key_rows, value_rows, segments), (query_blocks, segment_blocks))
    mixed = low_back(low(mixed_heads.reshape(SLAB, D)))
    attended = low_back(jnp.dot(mixed, output_weight, precision=highest) + vectors[2])
    hidden = normalize(frames_group + attended, vectors[3], vectors[4])
    hidden_low = low(hidden)
    expanded = low_back(jnp.dot(hidden_low, expand_weight, precision=highest) + vectors[8:12].reshape(FF))
    activated = low(smooth_gate(expanded))
    branch = low_back(jnp.dot(activated, reduce_weight, precision=highest) + vectors[5])
    result = normalize(hidden + branch, vectors[6], vectors[7])
    return result * (segments < UTT).astype(result.dtype)[:, None]

def adam_step(master, moment_one, moment_two, gradient, step_rate, decay_weight):
    new_one = 0.9 * moment_one + 0.1 * gradient
    new_two = 0.999 * moment_two + 0.001 * gradient * gradient
    corrected_one = new_one / (1.0 - 0.9 ** STEP)
    corrected_two = new_two / (1.0 - 0.999 ** STEP)
    new_master = master - step_rate * (corrected_one / (jnp.sqrt(corrected_two) + 1e-08) + decay_weight * master)
    return (new_one, new_two, new_master, new_master.astype(jnp.bfloat16))

def reference(frames, cotangent, lengths, input_weight, output_weight, expand_weight, reduce_weight, vector_copy, input_master, output_master, expand_master, reduce_master, vector_master, input_first, output_first, expand_first, reduce_first, vector_first, input_second, output_second, expand_second, reduce_second, vector_second):
    utterance_ends = jnp.cumsum(lengths, axis=1).astype(jnp.int32)
    positions = jnp.arange(SLAB, dtype=jnp.int32)
    segments = lax.optimization_barrier(jnp.sum((positions[None, :, None] >= utterance_ends[:, None, :]).astype(jnp.int32), axis=2)).astype(jnp.int32)

    def forward(frames_all, weight_in, weight_out, weight_expand, weight_reduce, vectors):
        outputs = lax.map(lambda pieces: group_forward(pieces[0], pieces[1], weight_in, weight_out, weight_expand, weight_reduce, vectors), (frames_all.reshape(GROUPS, SLAB, D), segments))
        return outputs.reshape(TOKENS, D)
    primal, pullback = jax.vjp(forward, frames.astype(jnp.float32), input_weight.astype(jnp.float32), output_weight.astype(jnp.float32), expand_weight.astype(jnp.float32), reduce_weight.astype(jnp.float32), vector_copy.astype(jnp.float32))
    gradients = pullback(cotangent.astype(jnp.float32))
    layer_output = primal.astype(jnp.bfloat16)
    frames_gradient = gradients[0]
    squares_total = jnp.float32(0.0)
    for gradient in gradients[1:]:
        squares_total = squares_total + jnp.sum(gradient * gradient)
    gradient_norm = jnp.sqrt(squares_total)
    factor = clip_limit / jnp.maximum(gradient_norm, clip_limit)
    input_parts = adam_step(input_master, input_first, input_second, gradients[1] * factor, 2.0 * D ** (-0.5), 0.01)
    output_parts = adam_step(output_master, output_first, output_second, gradients[2] * factor, 2.0 * D ** (-0.5), 0.01)
    expand_parts = adam_step(expand_master, expand_first, expand_second, gradients[3] * factor, 2.0 * D ** (-0.5), 0.01)
    reduce_parts = adam_step(reduce_master, reduce_first, reduce_second, gradients[4] * factor, 2.0 * FF ** (-0.5), 0.01)
    vector_parts = adam_step(vector_master, vector_first, vector_second, gradients[5] * factor, 0.5, 0.0)
    return (layer_output, frames_gradient, gradient_norm, input_parts[0], input_parts[1], input_parts[2], input_parts[3], output_parts[0], output_parts[1], output_parts[2], output_parts[3], expand_parts[0], expand_parts[1], expand_parts[2], expand_parts[3], reduce_parts[0], reduce_parts[1], reduce_parts[2], reduce_parts[3], vector_parts[0], vector_parts[1], vector_parts[2], vector_parts[3])
```

```python
import functools

import jax
import jax.numpy as jnp
from jax import lax
from jax.experimental import pallas as pl
from jax.experimental.pallas import tpu as pltpu
from jax.sharding import PartitionSpec as P

HD = 64
STEP = 10
LANES = 128
NORM_EPS = 1e-05
MASK = -float(2**30)
BF = jnp.bfloat16
F32 = jnp.float32
AXES = ("dp", "seq")

GROUPS = (
    (0, 2, 3, 5),
    (1, 4),
)
PLACES = (
    {
        0: ((0, 0, 0), (1, 1, 1), (2, 2, 2)),
        2: ((0, 0, 1), (1, 1, 2), (2, 3, 0)),
        3: ((0, 0, 2), (1, 2, 0), (2, 3, 1)),
        5: ((0, 1, 0), (1, 2, 1), (2, 3, 2)),
    },
    {
        1: ((0, 0, 0), (1, 1, 1), (2, 2, 1), (2, 3, 0)),
        4: ((0, 0, 1), (0, 1, 0), (1, 2, 0), (2, 3, 1)),
    },
)
WIDTHS = (3 * LANES, 2 * LANES)


def params(**more):
    return pltpu.CompilerParams(vmem_limit_bytes=60 * 2**20, **more)


def dot(a, b):
    return lax.dot_general(a, b, (((1,), (0,)), ((), ())), preferred_element_type=F32)


def dot_t(a, b):
    return lax.dot_general(a, b, (((1,), (1,)), ((), ())), preferred_element_type=F32)


def attend_kernel(
    x_ref, xp_ref, wq_ref, wk_ref, wv_ref, vec_ref, kmask_ref, qhot_ref,
    mixed_ref, e_ref, rinv_ref, q_ref, k_ref, v_ref, xt_ref,
):
    rows = q_ref.shape[0]
    xt_ref[...] = xp_ref[...].T
    wkv = jnp.concatenate([wk_ref[...], wv_ref[...]], axis=1)
    kv = dot(x_ref[...], wkv)
    k = kv[:, :LANES].astype(BF)
    v = (kv[:, LANES:] + vec_ref[1:2, :]).astype(BF)
    q = (dot(x_ref[:rows, :], wq_ref[...]) + vec_ref[0:1, :]).astype(BF)
    q = q * jnp.asarray(HD**-0.5, BF)
    q_ref[...] = q
    k_ref[...] = k
    v_ref[...] = v
    keys = jnp.concatenate([k, kmask_ref[...]], axis=1)
    low = lax.broadcasted_iota(jnp.int32, (rows, LANES), 1) < HD
    outs, inverses = [], []
    for head in range(2):
        own = low if head == 0 else jnp.logical_not(low)
        qh = jnp.where(own, q, jnp.zeros_like(q))
        scores = dot_t(jnp.concatenate([qh, qhot_ref[...]], axis=1), keys)
        top = jnp.max(scores, axis=1, keepdims=True)
        e = jnp.exp(scores - top)
        total = jnp.sum(e, axis=1, keepdims=True)
        e_low = e.astype(BF)
        e_ref[head] = e_low
        outs.append(dot(e_low, v))
        inverses.append(1.0 / total)
    rinv = jnp.where(low, inverses[0], inverses[1])
    rinv_ref[...] = rinv
    mixed_ref[...] = (jnp.where(low, outs[0], outs[1]) * rinv).astype(BF)


def attend(x_all, input_weight, vectors, kmask, qhot):
    slab, width = x_all.shape
    rows = qhot.shape[0]
    pairs = width // LANES
    full = lambda a: pl.BlockSpec(a.shape, lambda p: (0,) * a.ndim)
    cols = lambda r, off=0: pl.BlockSpec((r, LANES), lambda p: (0, p + off))
    return pl.pallas_call(
        attend_kernel,
        grid=(pairs,),
        in_specs=[
            full(x_all), cols(slab), cols(width), cols(width, pairs), cols(width, 2 * pairs),
            cols(vectors.shape[0]), full(kmask), full(qhot),
        ],
        out_specs=[
            cols(rows), pl.BlockSpec((2, rows, slab), lambda p: (p, 0, 0)), cols(rows), cols(rows),
            cols(slab), cols(slab), pl.BlockSpec((LANES, slab), lambda p: (p, 0)),
        ],
        out_shape=[
            jax.ShapeDtypeStruct((rows, width), BF),
            jax.ShapeDtypeStruct((2 * pairs, rows, slab), BF),
            jax.ShapeDtypeStruct((rows, width), F32),
            jax.ShapeDtypeStruct((rows, width), BF),
            jax.ShapeDtypeStruct((slab, width), BF),
            jax.ShapeDtypeStruct((slab, width), BF),
            jax.ShapeDtypeStruct((width, slab), BF),
        ],
        compiler_params=params(),
        name="attend",
    )(x_all, x_all, input_weight, input_weight, input_weight, vectors, kmask, qhot)


def spot(d, own_d):
    rel = d ^ own_d
    return (rel & 1) * 4 + (rel >> 1)


def mid_kernel(
    own_ref, mixed_ref, x_ref, cot_ref, qhot_ref, wo_ref, we_ref, wr_ref, vec_ref,
    layer_ref, gf_ref, gm_ref, rs_ref, rk_ref, es_ref, ek_ref, os_ref, ok_ref, vg_ref,
    act, slope, hid, norm1, inv1, hl, hlt, acc, gb, gbt, tmp,
):
    step = pl.program_id(0)
    own_s, own_d = own_ref[0], own_ref[1]
    rows, width = x_ref.shape
    chunks = act.shape[0]
    j = lax.rem(step, chunks)
    rel = jnp.where(j < 2, 2 * j + 1, 2 * (j - 2))
    shard = rel ^ own_s
    row = lambda i: vec_ref[i : i + 1, :]

    @pl.when(step == 0)
    def _():
        z = x_ref[...].astype(F32) + dot(mixed_ref[...], wo_ref[...]) + row(2)
        center = z - jnp.mean(z, axis=1, keepdims=True)
        inverse = lax.rsqrt(jnp.mean(center * center, axis=1, keepdims=True) + NORM_EPS)
        normed = center * inverse
        hidden = normed * row(3) + row(4)
        hid[...] = hidden
        norm1[...] = normed
        inv1[...] = jnp.broadcast_to(inverse, inv1.shape)
        low = hidden.astype(BF)
        hl[...] = low
        hlt[...] = low.T

    @pl.when(step < chunks)
    def _():
        pre = dot(hl[...], we_ref[...]) + vec_ref[pl.ds(8 + shard, 1), :]
        cdf = 0.5 * (1.0 + lax.erf(pre * 0.7071067811865476))
        density = jnp.exp(-0.5 * pre * pre) * 0.3989422804014327
        low = (pre * cdf).astype(BF)
        act[j] = low
        slope[j] = cdf + pre * density
        part = dot(low, wr_ref[...])

        @pl.when(step == 0)
        def _():
            acc[...] = part

        @pl.when(step > 0)
        def _():
            acc[...] += part

    @pl.when(step == chunks - 1)
    def _():
        z = hid[...] + acc[...] + row(5)
        center = z - jnp.mean(z, axis=1, keepdims=True)
        inverse = lax.rsqrt(jnp.mean(center * center, axis=1, keepdims=True) + NORM_EPS)
        normed = center * inverse
        valid = 1.0 - qhot_ref[:, 3:4].astype(F32)
        layer_ref[...] = ((normed * row(6) + row(7)) * valid).astype(BF)
        gy = cot_ref[...].astype(F32) * valid
        vg_ref[6:7, :] = jnp.sum(gy * normed, axis=0, keepdims=True)
        vg_ref[7:8, :] = jnp.sum(gy, axis=0, keepdims=True)
        e = gy * row(6)
        grad = e - jnp.mean(e, axis=1, keepdims=True)
        grad = (grad - normed * jnp.mean(e * normed, axis=1, keepdims=True)) * inverse
        low = grad.astype(BF)
        vg_ref[5:6, :] = jnp.sum(low.astype(F32), axis=0, keepdims=True)
        gb[...] = low
        gbt[...] = low.T
        acc[...] = grad

    @pl.when(step >= chunks)
    def _():
        grad_act = dot_t(gb[...], wr_ref[...])
        low = (grad_act * slope[j]).astype(BF)
        vg_ref[pl.ds(8 + shard, 1), :] = jnp.sum(low.astype(F32), axis=0, keepdims=True)
        acc[...] += dot_t(low, we_ref[...])
        piece = width // 8
        reduce_t = dot(gbt[...], act[j]).astype(BF)
        for ref, ours in ((rs_ref, j < 2), (rk_ref, j >= 2)):

            @pl.when(ours)
            def _():
                for d in range(8):
                    ref[0, spot(d, own_d)] = reduce_t[d * piece : (d + 1) * piece, :]

        grad_e = dot(hlt[...], low).astype(BF)
        tmp[...] = grad_e.reshape(tmp.shape)
        half = grad_e.shape[1] // 2
        for part, ref in ((1, es_ref), (0, ek_ref)):
            for ry in range(2):
                for t in range(2):
                    ref[t ^ (own_d & 1), ry, 0] = tmp[own_s ^ (2 * ry + part), :, t * half : (t + 1) * half]

    @pl.when(step == 2 * chunks - 1)
    def _():
        gy = acc[...]
        normed = norm1[...]
        vg_ref[3:4, :] = jnp.sum(gy * normed, axis=0, keepdims=True)
        vg_ref[4:5, :] = jnp.sum(gy, axis=0, keepdims=True)
        e = gy * row(3)
        grad = e - jnp.mean(e, axis=1, keepdims=True)
        grad = (grad - normed * jnp.mean(e * normed, axis=1, keepdims=True)) * inv1[:, :1]
        gf_ref[...] = grad
        low = grad.astype(BF)
        vg_ref[2:3, :] = jnp.sum(low.astype(F32), axis=0, keepdims=True)
        vg_ref[0:2, :] = jnp.zeros((2, width), F32)
        vg_ref[12:16, :] = jnp.zeros((4, width), F32)
        gm_ref[...] = dot_t(low, wo_ref[...]).astype(BF)
        gat = low.T
        tmp2 = mixed_ref[...].T
        hlt[...] = tmp2
        piece, fourth = width // 8, width // 4
        for ref, part in ((os_ref, 1), (ok_ref, 0)):
            for ry in range(2):
                start = pl.multiple_of((own_s ^ (2 * ry + part)) * fourth, fourth)
                out = dot_t(gat, hlt[pl.ds(start, fourth), :]).astype(BF)
                for d in range(8):
                    ref[ry, spot(d, own_d)] = out[d * piece : (d + 1) * piece, :]


def middle(own, mixed, frames, cotangent, qhot, output_weight, expand_weight, reduce_weight, vectors):
    rows, width = frames.shape
    hidden = expand_weight.shape[1]
    chunks = 4
    cut = hidden // chunks
    piece, fourth, eighth = width // 8, width // 4, hidden // 8

    def shard_of(step, own):
        j = lax.rem(step, chunks)
        return jnp.where(j < 2, 2 * j + 1, 2 * (j - 2)) ^ own[0]

    def deep(step, own):
        return (0, 0, shard_of(jnp.maximum(step, chunks), own) ^ (own[1] >> 1), 0, 0)

    full = lambda shape: pl.BlockSpec(shape, lambda s, own: (0,) * len(shape))
    spread = pl.BlockSpec((2, 2, 1, fourth, eighth), deep)
    return pl.pallas_call(
        mid_kernel,
        grid_spec=pltpu.PrefetchScalarGridSpec(
            num_scalar_prefetch=1,
            grid=(2 * chunks,),
            in_specs=[
                full(mixed.shape), full(frames.shape), full(cotangent.shape), full(qhot.shape),
                full(output_weight.shape),
                pl.BlockSpec((width, cut), lambda s, own: (0, shard_of(s, own))),
                pl.BlockSpec((cut, width), lambda s, own: (shard_of(s, own), 0)),
                full(vectors.shape),
            ],
            out_specs=[
                full((rows, width)), full((rows, width)), full((rows, width)),
                pl.BlockSpec((1, 8, piece, cut), lambda s, own: (jnp.clip(s - chunks, 0, 1), 0, 0, 0)),
                pl.BlockSpec((1, 8, piece, cut), lambda s, own: (jnp.clip(s - chunks - 2, 0, 1), 0, 0, 0)),
                spread, spread,
                full((2, 8, piece, fourth)), full((2, 8, piece, fourth)), full((16, width)),
            ],
            scratch_shapes=[
                pltpu.VMEM((chunks, rows, cut), BF),
                pltpu.VMEM((chunks, rows, cut), F32),
                pltpu.VMEM((rows, width), F32),
                pltpu.VMEM((rows, width), F32),
                pltpu.VMEM((rows, LANES), F32),
                pltpu.VMEM((rows, width), BF),
                pltpu.VMEM((width, rows), BF),
                pltpu.VMEM((rows, width), F32),
                pltpu.VMEM((rows, width), BF),
                pltpu.VMEM((width, rows), BF),
                pltpu.VMEM((4, fourth, cut), BF),
            ],
        ),
        out_shape=[
            jax.ShapeDtypeStruct((rows, width), BF),
            jax.ShapeDtypeStruct((rows, width), F32),
            jax.ShapeDtypeStruct((rows, width), BF),
            jax.ShapeDtypeStruct((2, 8, piece, cut), BF),
            jax.ShapeDtypeStruct((2, 8, piece, cut), BF),
            jax.ShapeDtypeStruct((2, 2, 4, fourth, eighth), BF),
            jax.ShapeDtypeStruct((2, 2, 4, fourth, eighth), BF),
            jax.ShapeDtypeStruct((2, 8, piece, fourth), BF),
            jax.ShapeDtypeStruct((2, 8, piece, fourth), BF),
            jax.ShapeDtypeStruct((16, width), F32),
        ],
        compiler_params=params(),
        name="middle",
    )(own, mixed, frames, cotangent, qhot, output_weight, expand_weight, reduce_weight, vectors)


def back_kernel(group, own_ref, e_ref, q_ref, k_ref, v_ref, gm_ref, mixed_ref, rinv_ref, wq_ref, wk_ref, wv_ref,
                xt_ref, gx_in_ref, *rest):
    first, last = group == 0, group == len(GROUPS) - 1
    rest = list(rest)
    dx_in_ref = None if first else rest.pop(0)
    gs_ref, gk_ref, gx_ref, vb_ref = rest[:4]
    rest = rest[4:]
    dxs_ref = dxk_ref = None
    if last:
        dxs_ref, dxk_ref, gw, dx = rest
    else:
        dx, gw = rest
    i = pl.program_id(0)
    own_s, own_d = own_ref[0], own_ref[1]
    rows = q_ref.shape[0]
    q, k, v = q_ref[...], k_ref[...], v_ref[...]
    rinv = rinv_ref[...]
    gm = gm_ref[...].astype(F32) * rinv
    both = gm * mixed_ref[...].astype(F32)
    gm_low = gm.astype(BF)
    gm_t = gm_low.T
    q_t = q.T
    low = lax.broadcasted_iota(jnp.int32, (rows, LANES), 1) < HD
    dqs, dks, dvs = [], [], []
    for head in range(2):
        own = low if head == 0 else jnp.logical_not(low)
        span = slice(head * HD, (head + 1) * HD)
        e = e_ref[head]
        inner = jnp.sum(jnp.where(own, both, 0.0), axis=1, keepdims=True)
        grad_e = dot_t(jnp.where(own, gm_low, jnp.zeros_like(gm_low)), v)
        ds = (e.astype(F32) * (grad_e - inner)).astype(BF)
        dqs.append(dot(ds, k))
        dks.append(dot(q_t[span, :], ds))
        dvs.append(dot(gm_t[span, :], e))
    dq = (jnp.where(low, dqs[0], dqs[1]) * HD**-0.5).astype(BF)
    dkv_t = jnp.concatenate([*dks, *dvs], axis=0).astype(BF)
    ones = jnp.ones((8, dkv_t.shape[1]), BF)
    vb_ref[0:1, :] = jnp.sum(dq.astype(F32), axis=0, keepdims=True)
    vb_ref[1:2, :] = dot_t(ones, dkv_t[LANES:, :])[0:1, :]

    @pl.when(i == 0)
    def _():
        gx_ref[...] = gx_in_ref[...]
        dx[...] = jnp.zeros_like(dx) if first else dx_in_ref[...]

    gx_ref[...] += dot_t(dq, wq_ref[...])
    dx[...] += dot(jnp.concatenate([wk_ref[...], wv_ref[...]], axis=1), dkv_t)
    grad_q = dot(xt_ref[:, :rows], dq).astype(BF)
    grad_kv = dot_t(xt_ref[...], dkv_t).astype(BF)
    piece = grad_q.shape[0] // 8
    blocks = [b.reshape(8, piece, LANES) for b in (grad_q, grad_kv[:, :LANES], grad_kv[:, LANES:])]
    for n, pair in enumerate(GROUPS[group]):

        @pl.when(i == n)
        def _():
            for which, shard, place in PLACES[group][pair]:
                gw[shard, :, :, place * LANES : (place + 1) * LANES] = blocks[which]

    @pl.when(i == len(GROUPS[group]) - 1)
    def _():
        for ref, part in ((gs_ref, 1), (gk_ref, 0)):
            for ry in range(2):
                for d in range(8):
                    ref[ry, spot(d, own_d)] = gw[own_s ^ (2 * ry + part), d]
        if last:
            for ry in range(2):
                dxk_ref[ry] = dx[:, ry * rows : (ry + 1) * rows]
                dxs_ref[ry] = dx[:, (2 + ry) * rows : (3 + ry) * rows].astype(BF)


def attend_back(group, own, e, q, k, v, grad_mixed, mixed, rinv, input_weight, x_t, gx, dx):
    pairs = GROUPS[group]
    first, last = group == 0, group == len(GROUPS) - 1
    rows, width = q.shape
    slab = k.shape[0]
    count = width // LANES
    piece = width // 8
    span = WIDTHS[group]
    own = jnp.concatenate([own, jnp.array(pairs, jnp.int32)])
    full = lambda shape: pl.BlockSpec(shape, lambda i, own: (0,) * len(shape))
    cols = lambda r, off=0: pl.BlockSpec((r, LANES), lambda i, own: (0, own[2 + i] + off))
    inputs = [e, q, k, v, grad_mixed, mixed, rinv, input_weight, input_weight, input_weight, x_t, gx]
    in_specs = [
        pl.BlockSpec((2, rows, slab), lambda i, own: (own[2 + i], 0, 0)),
        cols(rows), cols(slab), cols(slab), cols(rows), cols(rows), cols(rows),
        cols(width), cols(width, count), cols(width, 2 * count), full(x_t.shape), full(gx.shape),
    ]
    out_shape = [
        jax.ShapeDtypeStruct((2, 8, piece, span), BF),
        jax.ShapeDtypeStruct((2, 8, piece, span), BF),
        jax.ShapeDtypeStruct((rows, width), F32),
        jax.ShapeDtypeStruct((8, len(pairs) * LANES), F32),
    ]
    out_specs = [
        full((2, 8, piece, span)), full((2, 8, piece, span)), full((rows, width)),
        pl.BlockSpec((8, LANES), lambda i, own: (0, i)),
    ]
    scratch = [pltpu.VMEM((4, 8, piece, span), BF)]
    if not first:
        inputs.append(dx)
        in_specs.append(full((width, slab)))
    if last:
        out_shape += [jax.ShapeDtypeStruct((2, width, rows), BF), jax.ShapeDtypeStruct((2, width, rows), F32)]
        out_specs += [full((2, width, rows)), full((2, width, rows))]
        scratch.append(pltpu.VMEM((width, slab), F32))
    else:
        out_shape.append(jax.ShapeDtypeStruct((width, slab), F32))
        out_specs.append(full((width, slab)))
    return pl.pallas_call(
        functools.partial(back_kernel, group),
        grid_spec=pltpu.PrefetchScalarGridSpec(
            num_scalar_prefetch=1, grid=(len(pairs),), in_specs=in_specs, out_specs=out_specs, scratch_shapes=scratch
        ),
        out_shape=out_shape,
        compiler_params=params(),
        name=f"attend_back_{group}",
    )(own, *inputs)


def split_kernel(count, *refs):
    n = len(refs) // (2 + count)
    for a in range(n):
        keep, came = refs[2 * a], refs[2 * a + 1]
        for part in range(count):
            out = refs[2 * n + a * count + part]
            out[...] = (keep[part].astype(F32) + came[part].astype(F32)).astype(out.dtype)


def split_sum(pairs, count, kinds=None):
    kinds = kinds or (BF,) * count
    inputs, in_specs, out_shape, out_specs = [], [], [], []
    steps = 4 if count == 2 else 2
    for keep, came in pairs:
        rows, cols = keep.size // keep.shape[-1] // count, keep.shape[-1]
        for a in (keep, came):
            inputs.append(a.reshape(count, rows, cols))
            in_specs.append(pl.BlockSpec((count, rows // steps, cols), lambda i: (0, i, 0)))
        for kind in kinds:
            out_shape.append(jax.ShapeDtypeStruct((rows, cols), kind))
            out_specs.append(pl.BlockSpec((rows // steps, cols), lambda i: (i, 0)))
    outs = pl.pallas_call(
        functools.partial(split_kernel, count),
        grid=(steps,), in_specs=in_specs, out_specs=out_specs, out_shape=out_shape,
        compiler_params=params(), name="split_sum",
    )(*inputs)
    return [outs[count * a : count * (a + 1)] for a in range(len(pairs))]


def frames_kernel(gx_ref, keep_ref, came_ref, out_ref):
    out_ref[...] = gx_ref[...] + (keep_ref[...] + came_ref[...].astype(F32)).T


def frames_end(gx, keep, came):
    rows, width = gx.shape
    across = pl.BlockSpec((rows, LANES), lambda p: (0, p))
    down = pl.BlockSpec((LANES, rows), lambda p: (p, 0))
    return pl.pallas_call(
        frames_kernel,
        grid=(width // LANES,), in_specs=[across, down, down], out_specs=across,
        out_shape=jax.ShapeDtypeStruct((rows, width), F32), compiler_params=params(), name="frames_end",
    )(gx, keep, came)


def adam_step(master, moment_one, moment_two, gradient, step_rate, decay_weight):
    new_one = 0.9 * moment_one + 0.1 * gradient
    new_two = 0.999 * moment_two + 0.001 * gradient * gradient
    corrected_one = new_one / (1.0 - 0.9**STEP)
    corrected_two = new_two / (1.0 - 0.999**STEP)
    new_master = master - step_rate * (
        corrected_one / (jnp.sqrt(corrected_two) + 1e-08) + decay_weight * master
    )
    return (new_one, new_two, new_master, new_master.astype(BF))


def adam_kernel(rates, turned, squares_ref, *refs):
    n = len(rates)
    ins, outs = refs[: 4 * n], refs[4 * n :]
    norm = jnp.sqrt(squares_ref[0:1, 0:1])
    outs[0][...] = norm
    factor = 1.0 / jnp.maximum(norm, 1.0)
    for a in range(n):
        master, one, two, grad = (r[...] for r in ins[4 * a : 4 * a + 4])
        if turned[a]:
            grad = grad.T
        made = adam_step(master, one, two, grad * factor, rates[a][0], rates[a][1])
        for b in range(4):
            outs[1 + 4 * a + b][...] = made[b]


def adam_all(squares, states, grads, rates, turned):
    inputs, out_shape = [squares], [jax.ShapeDtypeStruct((1, 1), F32)]
    for state, grad in zip(states, grads):
        inputs += [*state, grad]
        shape = state[0].shape
        out_shape += [jax.ShapeDtypeStruct(shape, F32)] * 3 + [jax.ShapeDtypeStruct(shape, BF)]
    vmem = pl.BlockSpec(memory_space=pltpu.VMEM)
    return pl.pallas_call(
        functools.partial(adam_kernel, rates, turned),
        in_specs=[vmem] * len(inputs), out_specs=[vmem] * len(out_shape), out_shape=out_shape,
        compiler_params=params(), name="adam",
    )(*inputs)


def mover(dp, seq):
    def move(value, bits_d, bits_s):
        pairs = [(d * seq + s, (d ^ bits_d) * seq + (s ^ bits_s)) for d in range(dp) for s in range(seq)]
        return lax.ppermute(value, AXES, pairs)

    return move


def tree_sum(move, value):
    value = value + move(value, 0, 1)
    value = (value + move(value, 0, 2)) + (move(value, 1, 0) + move(value, 1, 2))
    return (value + move(value, 2, 0)) + (move(value, 4, 0) + move(value, 6, 0))


def scatter_fast(move, kept, sent, x_first):
    came = move(sent, 0, 1)
    (keep, send), = split_sum([(kept, came)], 2)
    steps = ((1, 0), (0, 2)) if x_first else ((0, 2), (1, 0))
    came = move(send, *steps[0])
    (keep, send), = split_sum([(keep, came)], 2)
    came = move(send, *steps[1])
    parts, = split_sum([(keep, came)], 4)
    return [parts[0], *(move(parts[b], 2 * b, 0) for b in (1, 2, 3))]


def scatter_plain(kept, sent, x_first):
    if x_first:
        parts = jnp.stack([kept, sent], axis=2).transpose(1, 2, 4, 3, 0, 5)
        parts = parts.reshape(4, parts.shape[2], -1)
    else:
        parts = jnp.stack([kept, sent], axis=1)
        rows, cols = parts.shape[-2:]
        parts = parts.reshape(4, 2, 4, rows, cols).swapaxes(1, 2).reshape(4, 8 * rows, cols)
    part = lax.psum_scatter(parts, "seq", scatter_dimension=0, tiled=True)[0].astype(F32)
    return lax.psum_scatter(part, "dp", scatter_dimension=1 if x_first else 0, tiled=True)


def local(
    frames, cotangent, lengths,
    input_weight, output_weight, expand_weight, reduce_weight, vector_copy,
    *states,
):
    rows, width = frames.shape
    seq, dp = lax.axis_size("seq"), lax.axis_size("dp")
    slab = rows * seq
    move = mover(dp, seq)
    own_s, own_d = lax.axis_index("seq"), lax.axis_index("dp")
    fast = dp == 8
    vectors = vector_copy.astype(F32)

    across = move(frames, 0, 2)
    near = move(frames, 0, 1)
    far = move(across, 0, 1)
    x_all = jnp.concatenate([frames, across, near, far], axis=0)

    first_end = lengths[0, 0]
    second_end = first_end + lengths[0, 1]
    third_end = second_end + lengths[0, 2]
    order = jnp.array([0, 2, 1, 3], jnp.int32) ^ own_s
    positions = (order[:, None] * rows + jnp.arange(rows, dtype=jnp.int32)[None, :]).reshape(slab, 1)
    segments = sum((positions >= end).astype(jnp.int32) for end in (first_end, second_end, third_end))
    lanes = jnp.arange(LANES, dtype=jnp.int32)[None, :]
    kmask = jnp.where((segments == lanes) | (lanes > 3), 0.0, MASK).astype(BF)
    qhot = (segments[:rows] == lanes).astype(BF)

    mixed, e, rinv, q, k, v, x_t = attend(x_all, input_weight, vectors, kmask, qhot)
    if fast:
        own = jnp.stack([own_s, own_d]).astype(jnp.int32)
    else:
        own = jnp.zeros((2,), jnp.int32)
    layer, gf, grad_mixed, red_s, red_k, exp_s, exp_k, out_s, out_k, vec_grad = middle(
        own, mixed, frames, cotangent, qhot, output_weight, expand_weight, reduce_weight, vectors
    )
    in_s1, in_k1, gx, vb1, dx = attend_back(
        0, own, e, q, k, v, grad_mixed, mixed, rinv, input_weight, x_t, gf, None
    )
    in_s2, in_k2, gx, vb2, dx_s, dx_k = attend_back(
        1, own, e, q, k, v, grad_mixed, mixed, rinv, input_weight, x_t, gx, dx
    )
    came = move(dx_s, 0, 1)
    (dx_keep, dx_send), = split_sum([(dx_k, came)], 2, (F32, BF))
    frames_gradient = frames_end(gx, dx_keep, move(dx_send, 0, 2))

    vb = jnp.concatenate([vb1, vb2], axis=1)[:2].reshape(2, -1, LANES)
    where = [(*GROUPS[0], *GROUPS[1]).index(p) for p in range(width // LANES)]
    vb = jnp.stack([vb[:, p] for p in where], axis=1).reshape(2, width)
    vec_grad = jnp.concatenate([vb, vec_grad[2:12]], axis=0)

    scattered = (
        (red_k, red_s, False), (exp_k, exp_s, True), (out_k, out_s, False), (in_k1, in_s1, False), (in_k2, in_s2, False)
    )
    if fast:
        totals = []
        for entry in scattered:
            parts = [p.astype(F32) for p in scatter_fast(move, *entry)]
            totals.append((parts[0] + parts[1]) + (parts[2] + parts[3]))
        vec_all = tree_sum(move, vec_grad)
        shape = (vec_grad.shape[0] // seq, width // dp)
        vec = lax.dynamic_slice(vec_all, (own_s * shape[0], own_d * shape[1]), shape)
    else:
        totals = [scatter_plain(*entry) for entry in scattered]
        vec = lax.psum_scatter(vec_grad, "seq", scatter_dimension=0, tiled=True)
        vec = lax.psum_scatter(vec, "dp", scatter_dimension=1, tiled=True)
    red, exp, out, in1, in2 = totals
    odd = own_s % 2 == 1
    even_cols = jnp.concatenate([in1[:, :128], in2[:, :128], in1[:, 128:], in2[:, 128:192]], axis=1)
    odd_cols = jnp.concatenate([in2[:, 64:128], in1[:, :256], in2[:, 128:], in1[:, 256:]], axis=1)
    inp = jnp.where(odd, odd_cols, even_cols)
    grads = [inp, out, exp, red, vec]
    squares = sum(jnp.sum(g * g) for g in grads)
    squares = jnp.full((8, LANES), squares, F32)
    squares = tree_sum(move, squares) if fast else lax.psum(squares, AXES)
    masters, firsts, seconds = states[:5], states[5:10], states[10:]
    hidden = expand_weight.shape[1]
    wide, narrow = 2.0 * width**-0.5, 2.0 * hidden**-0.5
    made = adam_all(
        squares, list(zip(masters, firsts, seconds)), grads,
        ((wide, 0.01), (wide, 0.01), (wide, 0.01), (narrow, 0.01), (0.5, 0.0)),
        (False, True, False, True, False),
    )
    return (layer, frames_gradient, made[0].reshape(()), *made[1:])


def solution(mesh):
    tokens, whole = P(("dp", "seq"), None), P()
    state = (P("dp", "seq"), *(P("seq", "dp"),) * 4)
    outs = tuple(s for s in state for _ in range(4))
    return jax.shard_map(
        local,
        mesh=mesh,
        in_specs=(tokens, tokens, P("dp", None), *(whole,) * 5, *state * 3),
        out_specs=(tokens, tokens, whole, *outs),
        check_vma=False,
    )
```

```python
import functools

import jax
import jax.numpy as jnp
from jax import lax
from jax.experimental import pallas as pl
from jax.experimental.pallas import tpu as pltpu
from jax.sharding import PartitionSpec as P

HD = 64
STEP = 10
LANES = 128
NORM_EPS = 1e-05
MASK = -float(2**30)
BF = jnp.bfloat16
F32 = jnp.float32
AXES = ("dp", "seq")

PLACES = (
    {
        0: ((0, 0, 0), (1, 1, 1), (2, 2, 2)),
        2: ((0, 0, 1), (1, 1, 2), (2, 3, 0)),
        3: ((0, 0, 2), (1, 2, 0), (2, 3, 1)),
        5: ((0, 1, 0), (1, 2, 1), (2, 3, 2)),
    },
    {
        1: ((0, 0, 0), (1, 1, 1), (2, 2, 1), (2, 3, 0)),
        4: ((0, 0, 1), (0, 1, 0), (1, 2, 0), (2, 3, 1)),
    },
)
WIDTHS = (3 * LANES, 2 * LANES)
CALLS = ((0, 2), (3, 5), (1, 4))


def params(**more):
    return pltpu.CompilerParams(vmem_limit_bytes=60 * 2**20, **more)


def cost(microseconds):
    return pl.CostEstimate(flops=int(microseconds * 4.4e9), bytes_accessed=0, transcendentals=0)


def dot(a, b):
    return lax.dot_general(a, b, (((1,), (0,)), ((), ())), preferred_element_type=F32)


def dot_t(a, b):
    return lax.dot_general(a, b, (((1,), (1,)), ((), ())), preferred_element_type=F32)


def attend_kernel(
    x0_ref, x1_ref, x2_ref, x3_ref, wq_ref, wk_ref, wv_ref, vec_ref, kmask_ref, qhot_ref,
    mixed_ref, e_ref, rinv_ref, q_ref, k_ref, v_ref, xt_ref, x_ref,
):
    rows = q_ref.shape[0]
    step = pl.program_id(0)

    @pl.when(step == 0)
    def _():
        for i, ref in enumerate((x0_ref, x1_ref, x2_ref, x3_ref)):
            x_ref[i * rows : (i + 1) * rows, :] = ref[...]

    xt_ref[...] = x_ref[:, pl.ds(pl.multiple_of(step * LANES, LANES), LANES)].T
    wkv = jnp.concatenate([wk_ref[...], wv_ref[...]], axis=1)
    kv = dot(x_ref[...], wkv)
    k = kv[:, :LANES].astype(BF)
    v = (kv[:, LANES:] + vec_ref[1:2, :]).astype(BF)
    q = (dot(x_ref[:rows, :], wq_ref[...]) + vec_ref[0:1, :]).astype(BF)
    q = q * jnp.asarray(HD**-0.5, BF)
    q_ref[...] = q
    k_ref[...] = k
    v_ref[...] = v
    keys = jnp.concatenate([k, kmask_ref[...]], axis=1)
    low = lax.broadcasted_iota(jnp.int32, (rows, LANES), 1) < HD
    outs, inverses = [], []
    for head in range(2):
        own = low if head == 0 else jnp.logical_not(low)
        qh = jnp.where(own, q, jnp.zeros_like(q))
        scores = dot_t(jnp.concatenate([qh, qhot_ref[...]], axis=1), keys)
        top = jnp.max(scores, axis=1, keepdims=True)
        e = jnp.exp(scores - top)
        total = jnp.sum(e, axis=1, keepdims=True)
        e_low = e.astype(BF)
        e_ref[head] = e_low
        outs.append(dot(e_low, v))
        inverses.append(1.0 / total)
    rinv = jnp.where(low, inverses[0], inverses[1])
    rinv_ref[...] = rinv
    mixed_ref[...] = (jnp.where(low, outs[0], outs[1]) * rinv).astype(BF)


def attend(blocks, input_weight, vectors, kmask, qhot):
    rows, width = blocks[0].shape
    slab = rows * len(blocks)
    pairs = width // LANES
    full = lambda a: pl.BlockSpec(a.shape, lambda p: (0,) * a.ndim)
    cols = lambda r, off=0: pl.BlockSpec((r, LANES), lambda p: (0, p + off))
    return pl.pallas_call(
        attend_kernel,
        grid=(pairs,),
        in_specs=[
            *map(full, blocks), cols(width), cols(width, pairs), cols(width, 2 * pairs),
            cols(vectors.shape[0]), full(kmask), full(qhot),
        ],
        out_specs=[
            cols(rows), pl.BlockSpec((2, rows, slab), lambda p: (p, 0, 0)), cols(rows), cols(rows),
            cols(slab), cols(slab), pl.BlockSpec((LANES, slab), lambda p: (p, 0)),
        ],
        out_shape=[
            jax.ShapeDtypeStruct((rows, width), BF),
            jax.ShapeDtypeStruct((2 * pairs, rows, slab), BF),
            jax.ShapeDtypeStruct((rows, width), F32),
            jax.ShapeDtypeStruct((rows, width), BF),
            jax.ShapeDtypeStruct((slab, width), BF),
            jax.ShapeDtypeStruct((slab, width), BF),
            jax.ShapeDtypeStruct((width, slab), BF),
        ],
        scratch_shapes=[pltpu.VMEM((slab, width), BF)],
        compiler_params=params(), cost_estimate=cost(29),
        name="attend",
    )(*blocks, input_weight, input_weight, input_weight, vectors, kmask, qhot)


def spot(d, own_d):
    rel = d ^ own_d
    return (rel & 1) * 4 + (rel >> 1)


def turn(j):
    return jnp.where(j < 2, 2 * j + 1, 2 * (j - 2))


def store_rows(ref, block, own_d):
    piece = block.shape[0] // 8
    for d in range(8):
        ref[0, spot(d, own_d)] = block[d * piece : (d + 1) * piece, :]


def reduce_kernel(own_ref, gbt_ref, act_ref, rk_ref):
    store_rows(rk_ref, dot(gbt_ref[...], act_ref[0]).astype(BF), own_ref[1])


def reduce_kept(own, gbt, act):
    width, rows = gbt.shape
    chunks, _, cut = act.shape
    return pl.pallas_call(
        reduce_kernel,
        grid_spec=pltpu.PrefetchScalarGridSpec(
            num_scalar_prefetch=1,
            grid=(2,),
            in_specs=[
                pl.BlockSpec((width, rows), lambda j, own: (0, 0)),
                pl.BlockSpec((1, rows, cut), lambda j, own: (j + 2, 0, 0)),
            ],
            out_specs=pl.BlockSpec((1, 8, width // 8, cut), lambda j, own: (j, 0, 0, 0)),
        ),
        out_shape=jax.ShapeDtypeStruct((2, 8, width // 8, cut), BF),
        compiler_params=params(), cost_estimate=cost(5),
        name="reduce_kept",
    )(own, gbt, act)


def ahead_kernel(
    own_ref, mixed_ref, x_ref, cot_ref, qhot_ref, wo_ref, we_ref, wr_ref, vec_ref,
    layer_ref, act_ref, slope_ref, norm1_ref, inv1_ref, hlt_ref, mt_ref, gs_ref, gb_ref, gbt, rs_ref, vg_ref,
    act, hid, hl, acc,
):
    step = pl.program_id(0)
    own_s, own_d = own_ref[0], own_ref[1]
    rows, width = x_ref.shape
    chunks = act.shape[0]
    j = lax.rem(step, chunks)
    shard = turn(j) ^ own_s
    row = lambda i: vec_ref[i : i + 1, :]

    @pl.when(step == 0)
    def _():
        z = x_ref[...].astype(F32) + dot(mixed_ref[...], wo_ref[...]) + row(2)
        center = z - jnp.mean(z, axis=1, keepdims=True)
        inverse = lax.rsqrt(jnp.mean(center * center, axis=1, keepdims=True) + NORM_EPS)
        normed = center * inverse
        hidden = normed * row(3) + row(4)
        hid[...] = hidden
        norm1_ref[...] = normed
        inv1_ref[...] = jnp.broadcast_to(inverse, inv1_ref.shape)
        low = hidden.astype(BF)
        hl[...] = low
        hlt_ref[...] = low.T
        mt_ref[...] = mixed_ref[...].T
        vg_ref[...] = jnp.zeros_like(vg_ref)

    @pl.when(step < chunks)
    def _():
        pre = dot(hl[...], we_ref[...]) + vec_ref[pl.ds(8 + shard, 1), :]
        cdf = 0.5 * (1.0 + lax.erf(pre * 0.7071067811865476))
        density = jnp.exp(-0.5 * pre * pre) * 0.3989422804014327
        low = (pre * cdf).astype(BF)
        act[j] = low
        act_ref[0] = low
        slope_ref[0] = cdf + pre * density
        part = dot(low, wr_ref[...])

        @pl.when(step == 0)
        def _():
            acc[...] = part

        @pl.when(step > 0)
        def _():
            acc[...] += part

    @pl.when(step == chunks - 1)
    def _():
        z = hid[...] + acc[...] + row(5)
        center = z - jnp.mean(z, axis=1, keepdims=True)
        inverse = lax.rsqrt(jnp.mean(center * center, axis=1, keepdims=True) + NORM_EPS)
        normed = center * inverse
        valid = 1.0 - qhot_ref[:, 3:4].astype(F32)
        layer_ref[...] = ((normed * row(6) + row(7)) * valid).astype(BF)
        gy = cot_ref[...].astype(F32) * valid
        vg_ref[6:7, :] = jnp.sum(gy * normed, axis=0, keepdims=True)
        vg_ref[7:8, :] = jnp.sum(gy, axis=0, keepdims=True)
        e = gy * row(6)
        grad = e - jnp.mean(e, axis=1, keepdims=True)
        grad = (grad - normed * jnp.mean(e * normed, axis=1, keepdims=True)) * inverse
        low = grad.astype(BF)
        vg_ref[5:6, :] = jnp.sum(low.astype(F32), axis=0, keepdims=True)
        gb_ref[...] = low
        gbt[...] = low.T
        gs_ref[...] = grad

    @pl.when(step >= chunks)
    def _():
        store_rows(rs_ref, dot(gbt[...], act[j]).astype(BF), own_d)


def ahead(own, mixed, frames, cotangent, qhot, output_weight, expand_weight, reduce_weight, vectors):
    rows, width = frames.shape
    hidden = expand_weight.shape[1]
    chunks = 4
    cut = hidden // chunks
    piece = width // 8
    first = lambda s: jnp.minimum(s, chunks - 1)
    shard_of = lambda s, own: turn(first(s)) ^ own[0]
    full = lambda shape: pl.BlockSpec(shape, lambda s, own: (0,) * len(shape))
    chunk = pl.BlockSpec((1, rows, cut), lambda s, own: (first(s), 0, 0))
    return pl.pallas_call(
        ahead_kernel,
        grid_spec=pltpu.PrefetchScalarGridSpec(
            num_scalar_prefetch=1,
            grid=(chunks + 2,),
            in_specs=[
                full(mixed.shape), full(frames.shape), full(cotangent.shape), full(qhot.shape),
                full(output_weight.shape),
                pl.BlockSpec((width, cut), lambda s, own: (0, shard_of(s, own))),
                pl.BlockSpec((cut, width), lambda s, own: (shard_of(s, own), 0)),
                full(vectors.shape),
            ],
            out_specs=[
                full((rows, width)), chunk, chunk, full((rows, width)), full((rows, LANES)),
                full((width, rows)), full((width, rows)), full((rows, width)), full((rows, width)), full((width, rows)),
                pl.BlockSpec((1, 8, piece, cut), lambda s, own: (jnp.maximum(s - chunks, 0), 0, 0, 0)),
                full((16, width)),
            ],
            scratch_shapes=[
                pltpu.VMEM((chunks, rows, cut), BF),
                pltpu.VMEM((rows, width), F32),
                pltpu.VMEM((rows, width), BF),
                pltpu.VMEM((rows, width), F32),
            ],
        ),
        out_shape=[
            jax.ShapeDtypeStruct((rows, width), BF),
            jax.ShapeDtypeStruct((chunks, rows, cut), BF),
            jax.ShapeDtypeStruct((chunks, rows, cut), F32),
            jax.ShapeDtypeStruct((rows, width), F32),
            jax.ShapeDtypeStruct((rows, LANES), F32),
            jax.ShapeDtypeStruct((width, rows), BF),
            jax.ShapeDtypeStruct((width, rows), BF),
            jax.ShapeDtypeStruct((rows, width), F32),
            jax.ShapeDtypeStruct((rows, width), BF),
            jax.ShapeDtypeStruct((width, rows), BF),
            jax.ShapeDtypeStruct((2, 8, piece, cut), BF),
            jax.ShapeDtypeStruct((16, width), F32),
        ],
        compiler_params=params(), cost_estimate=cost(20),
        name="ahead",
    )(own, mixed, frames, cotangent, qhot, output_weight, expand_weight, reduce_weight, vectors)


def behind_kernel(
    own_ref, slope_ref, gb_ref, gs_ref, norm1_ref, inv1_ref, hlt_ref, mt_ref, wo_ref, we_ref, wr_ref, vec_ref, _,
    gf_ref, gm_ref, es_ref, ek_ref, vg_ref,
    acc, tmp,
):
    j = pl.program_id(0)
    own_s, own_d = own_ref[0], own_ref[1]
    rows, width = gb_ref.shape
    shard = turn(j) ^ own_s
    row = lambda i: vec_ref[i : i + 1, :]
    piece, fourth = width // 8, width // 4

    @pl.when(j == 0)
    def _():
        acc[...] = gs_ref[...]
        vg_ref[...] = jnp.zeros_like(vg_ref)

    grad_act = dot_t(gb_ref[...], wr_ref[...])
    low = (grad_act * slope_ref[0]).astype(BF)
    vg_ref[pl.ds(8 + shard, 1), :] = jnp.sum(low.astype(F32), axis=0, keepdims=True)
    acc[...] += dot_t(low, we_ref[...])
    grad_e = dot(hlt_ref[...], low).astype(BF)
    tmp[...] = grad_e.reshape(tmp.shape)
    half = grad_e.shape[1] // 2
    rz = shard ^ (own_d >> 1)
    for part, ref in ((1, es_ref), (0, ek_ref)):
        for ry in range(2):
            for t in range(2):
                block = tmp[own_s ^ (2 * ry + part), :, t * half : (t + 1) * half]
                ref[ry, t ^ (own_d & 1), rz, :fourth, :] = block

    @pl.when(j == pl.num_programs(0) - 1)
    def _():
        gy = acc[...]
        normed = norm1_ref[...]
        vg_ref[3:4, :] = jnp.sum(gy * normed, axis=0, keepdims=True)
        vg_ref[4:5, :] = jnp.sum(gy, axis=0, keepdims=True)
        e = gy * row(3)
        grad = e - jnp.mean(e, axis=1, keepdims=True)
        grad = (grad - normed * jnp.mean(e * normed, axis=1, keepdims=True)) * inv1_ref[:, :1]
        gf_ref[...] = grad
        low = grad.astype(BF)
        vg_ref[2:3, :] = jnp.sum(low.astype(F32), axis=0, keepdims=True)
        gm_ref[...] = dot_t(low, wo_ref[...]).astype(BF)
        gat = low.T
        for part, ref in ((1, es_ref), (0, ek_ref)):
            for ry in range(2):
                start = pl.multiple_of((own_s ^ (2 * ry + part)) * fourth, fourth)
                out = dot_t(gat, mt_ref[pl.ds(start, fourth), :]).astype(BF)
                for d in range(8):
                    block = out[d * piece : (d + 1) * piece, :]
                    block = jnp.concatenate([block[: piece // 2], block[piece // 2 :]], axis=1)
                    ref[ry, (d & 1) ^ (own_d & 1), (d >> 1) ^ (own_d >> 1), fourth:, :] = block


def behind(own, slope, gb, gs, norm1, inv1, hlt, mt, output_weight, expand_weight, reduce_weight, vectors, after):
    rows, width = gb.shape
    hidden = expand_weight.shape[1]
    chunks = 4
    cut = hidden // chunks
    fourth, eighth = width // 4, hidden // 8
    shard_of = lambda s, own: turn(s) ^ own[0]
    full = lambda shape: pl.BlockSpec(shape, lambda s, own: (0,) * len(shape))
    spread = (2, 2, 4, fourth + width // 16, eighth)
    return pl.pallas_call(
        behind_kernel,
        grid_spec=pltpu.PrefetchScalarGridSpec(
            num_scalar_prefetch=1,
            grid=(chunks,),
            in_specs=[
                pl.BlockSpec((1, rows, cut), lambda s, own: (s, 0, 0)),
                full(gb.shape), full(gs.shape), full(norm1.shape), full(inv1.shape), full(hlt.shape), full(mt.shape),
                full(output_weight.shape),
                pl.BlockSpec((width, cut), lambda s, own: (0, shard_of(s, own))),
                pl.BlockSpec((cut, width), lambda s, own: (shard_of(s, own), 0)),
                full(vectors.shape), pl.BlockSpec(memory_space=pl.ANY),
            ],
            out_specs=[full((rows, width)), full((rows, width)), full(spread), full(spread), full((16, width))],
            scratch_shapes=[pltpu.VMEM((rows, width), F32), pltpu.VMEM((4, fourth, cut), BF)],
        ),
        out_shape=[
            jax.ShapeDtypeStruct((rows, width), F32),
            jax.ShapeDtypeStruct((rows, width), BF),
            jax.ShapeDtypeStruct(spread, BF),
            jax.ShapeDtypeStruct(spread, BF),
            jax.ShapeDtypeStruct((16, width), F32),
        ],
        compiler_params=params(), cost_estimate=cost(18),
        name="behind",
    )(own, slope, gb, gs, norm1, inv1, hlt, mt, output_weight, expand_weight, reduce_weight, vectors, after)


def back_kernel(group, pairs, first, last, own_ref, e_ref, q_ref, k_ref, v_ref, gm_ref, mixed_ref, rinv_ref, xt_ref,
                *rest):
    rest = list(rest[1:])
    gw_in_ref = None if first else rest.pop(0)
    vec_in = [rest.pop(0) for _ in range(4)] if group == 1 else []
    dq_ref, dkv_ref, vb_ref = rest[:3]
    rest = rest[3:]
    if last:
        gs_ref, gk_ref, gw, *vecs = rest
    else:
        (gw,) = rest
    i = pl.program_id(0)
    own_s, own_d = own_ref[0], own_ref[1]
    rows = q_ref.shape[0]
    q, k, v = q_ref[...], k_ref[...], v_ref[...]
    gm = gm_ref[...].astype(F32) * rinv_ref[...]
    both = gm * mixed_ref[...].astype(F32)
    gm_low = gm.astype(BF)
    gm_t = gm_low.T
    q_t = q.T
    low = lax.broadcasted_iota(jnp.int32, (rows, LANES), 1) < HD
    dqs, dks, dvs = [], [], []
    for head in range(2):
        own = low if head == 0 else jnp.logical_not(low)
        span = slice(head * HD, (head + 1) * HD)
        e = e_ref[head]
        inner = jnp.sum(jnp.where(own, both, 0.0), axis=1, keepdims=True)
        grad_e = dot_t(jnp.where(own, gm_low, jnp.zeros_like(gm_low)), v)
        ds = (e.astype(F32) * (grad_e - inner)).astype(BF)
        dqs.append(dot(ds, k))
        dks.append(dot(q_t[span, :], ds))
        dvs.append(dot(gm_t[span, :], e))
    dq = (jnp.where(low, dqs[0], dqs[1]) * HD**-0.5).astype(BF)
    dkv = jnp.concatenate([*dks, *dvs], axis=0).astype(BF)
    dq_ref[...] = dq
    dkv_ref[...] = dkv
    ones = jnp.ones((8, dkv.shape[1]), BF)
    bias = jnp.concatenate(
        [jnp.sum(dq.astype(F32), axis=0, keepdims=True), dot_t(ones, dkv[LANES:, :])[0:1, :]], axis=0
    )
    vb_ref[0:2, :] = bias

    if group == 1:

        @pl.when(i == 0)
        def _():
            vecs[0][...] = vec_in[0][...] + vec_in[1][...]
            for call, ref in zip(CALLS, vec_in[2:]):
                for n, p in enumerate(call):
                    vecs[0][0:2, p * LANES : (p + 1) * LANES] = ref[0:2, n * LANES : (n + 1) * LANES]

    if not first:

        @pl.when(i == 0)
        def _():
            gw[...] = gw_in_ref[...]

    grad_q = dot(xt_ref[:, :rows], dq).astype(BF)
    grad_kv = dot_t(xt_ref[...], dkv).astype(BF)
    piece = grad_q.shape[0] // 8
    blocks = [b.reshape(8, piece, LANES) for b in (grad_q, grad_kv[:, :LANES], grad_kv[:, LANES:])]
    for n, pair in enumerate(pairs):

        @pl.when(i == n)
        def _():
            for which, shard, place in PLACES[group][pair]:
                gw[shard, :, :piece, place * LANES : (place + 1) * LANES] = blocks[which]
            if group == 1:
                vecs[0][0:2, pair * LANES : (pair + 1) * LANES] = bias

    if last:

        @pl.when(i == len(pairs) - 1)
        def _():
            if group == 1:
                vec, tall = vecs[0][...], vecs[0].shape[1]
                for d in range(8):
                    turned = pltpu.roll(vec, (tall - piece * d) % tall, axis=1)[:, : gw.shape[3]]
                    for shard in range(4):
                        block = pltpu.roll(turned, (16 - 3 * shard) % 16, axis=0) if shard else turned
                        gw[shard, d, piece:, :] = block.astype(BF)
            for ref, part in ((gs_ref, 1), (gk_ref, 0)):
                for ry in range(2):
                    for d in range(8):
                        ref[ry, spot(d, own_d)] = gw[own_s ^ (2 * ry + part), d]


def attend_back(group, pairs, own, e, q, k, v, grad_mixed, mixed, rinv, x_t, after, gw=None, last=True, vecs=()):
    first = gw is None
    rows, width = q.shape
    slab = k.shape[0]
    piece = width // 8
    span = WIDTHS[group]
    own = jnp.concatenate([own, jnp.array(pairs, jnp.int32)])
    full = lambda shape: pl.BlockSpec(shape, lambda i, own: (0,) * len(shape))
    cols = lambda r: pl.BlockSpec((r, LANES), lambda i, own: (0, own[2 + i]))
    inputs = [e, q, k, v, grad_mixed, mixed, rinv, x_t, after]
    in_specs = [
        pl.BlockSpec((2, rows, slab), lambda i, own: (own[2 + i], 0, 0)),
        cols(rows), cols(slab), cols(slab), cols(rows), cols(rows), cols(rows), full(x_t.shape),
        pl.BlockSpec(memory_space=pl.ANY),
    ]
    out_shape = [
        jax.ShapeDtypeStruct((rows, len(pairs) * LANES), BF),
        jax.ShapeDtypeStruct((len(pairs) * 2 * LANES, slab), BF),
        jax.ShapeDtypeStruct((8, len(pairs) * LANES), F32),
    ]
    out_specs = [
        pl.BlockSpec((rows, LANES), lambda i, own: (0, i)),
        pl.BlockSpec((2 * LANES, slab), lambda i, own: (i, 0)),
        pl.BlockSpec((8, LANES), lambda i, own: (0, i)),
    ]
    scratch = []
    whole = (4, 8, piece + (16 if vecs else 0), span)
    if not first:
        inputs.append(gw)
        in_specs.append(full(whole))
    inputs += vecs
    in_specs += [full(a.shape) for a in vecs]
    if last:
        out_shape += [jax.ShapeDtypeStruct((2, *whole[1:]), BF)] * 2
        out_specs += [full((2, *whole[1:]))] * 2
        scratch.append(pltpu.VMEM(whole, BF))
        if vecs:
            scratch.append(pltpu.VMEM((16, width), F32))
    else:
        out_shape.append(jax.ShapeDtypeStruct(whole, BF))
        out_specs.append(full(whole))
    return pl.pallas_call(
        functools.partial(back_kernel, group, pairs, first, last),
        grid_spec=pltpu.PrefetchScalarGridSpec(
            num_scalar_prefetch=1, grid=(len(pairs),), in_specs=in_specs, out_specs=out_specs, scratch_shapes=scratch
        ),
        out_shape=out_shape,
        compiler_params=params(), cost_estimate=cost(12),
        name="attend_back",
    )(own, *inputs)


def frames_kernel(pairs, last, w_ref, gx_in_ref, after_ref, *refs):
    n = len(pairs)
    dqs, dkvs = refs[:n], refs[n : 2 * n]
    refs = list(refs[2 * n :])
    dx_ref = refs.pop(0) if last else None
    gx_ref, *outs, wkv = refs
    j = pl.program_id(0)
    width = gx_ref.shape[1]
    flat = [p for call in pairs for p in call]

    @pl.when(j == 0)
    def _():
        for i, p in enumerate(flat):
            for t in range(2):
                start = (1 + t) * width + p * LANES
                wkv[:, (2 * i + t) * LANES : (2 * i + t + 1) * LANES] = w_ref[:, start : start + LANES]
        wq = jnp.concatenate([w_ref[:, p * LANES : (p + 1) * LANES] for p in flat], axis=1)
        dq = jnp.concatenate([r[...] for r in dqs], axis=1)
        gx_ref[...] = gx_in_ref[...] + dot_t(dq, wq)

    made = dot(wkv[...], jnp.concatenate([r[...] for r in dkvs], axis=0))
    if not last:
        outs[0][0] = made
        return
    made = made + dx_ref[0]

    @pl.when(j < 2)
    def _():
        outs[0][0] = made.astype(BF)

    @pl.when(j >= 2)
    def _():
        outs[1][0] = made


def frames_back(input_weight, gx, after, pairs, dqs, dkvs, dx=None):
    rows, width = gx.shape
    last = dx is not None
    count = 2 * sum(map(len, pairs))
    full = lambda a: pl.BlockSpec(a.shape, lambda j: (0,) * a.ndim)
    column = lambda a: pl.BlockSpec((a.shape[0], rows), lambda j: (0, lax.rem(j + 2, 4)))
    block = lambda pick: pl.BlockSpec((1, width, rows), lambda j: (pick(j), 0, 0))
    if last:
        out_specs = [block(lambda j: jnp.minimum(j, 1)), block(lambda j: jnp.maximum(j - 2, 0))]
        out_shape = [jax.ShapeDtypeStruct((2, width, rows), BF), jax.ShapeDtypeStruct((2, width, rows), F32)]
    else:
        out_specs = [block(lambda j: j)]
        out_shape = [jax.ShapeDtypeStruct((4, width, rows), F32)]
    return pl.pallas_call(
        functools.partial(frames_kernel, pairs, last),
        grid=(4,),
        in_specs=[
            full(input_weight), full(gx), pl.BlockSpec(memory_space=pl.ANY), *map(full, dqs), *map(column, dkvs),
            *([block(lambda j: j)] if last else []),
        ],
        out_specs=[full(gx), *out_specs],
        out_shape=[jax.ShapeDtypeStruct((rows, width), F32), *out_shape],
        scratch_shapes=[pltpu.VMEM((width, count * LANES), BF)],
        compiler_params=params(), cost_estimate=cost(4 if last else 8),
        name="frames_back",
    )(input_weight, gx, after, *dqs, *dkvs, *([dx] if last else []))


def frames_end_kernel(gx_ref, keep_ref, came_ref, out_ref):
    out_ref[...] = gx_ref[...] + (keep_ref[0] + came_ref[0].astype(F32)).T


def frames_end(gx, keep, came):
    rows, width = gx.shape
    across = pl.BlockSpec((rows, LANES), lambda p: (0, p))
    down = pl.BlockSpec((1, LANES, rows), lambda p: (0, p, 0))
    return pl.pallas_call(
        frames_end_kernel,
        grid=(width // LANES,), in_specs=[across, down, down], out_specs=across,
        out_shape=jax.ShapeDtypeStruct((rows, width), F32), compiler_params=params(), cost_estimate=cost(5), name="frames_end",
    )(gx, keep, came)


def gather_kernel(plan, *refs):
    start, out = 0, sum(n for n, _ in plan) + 1
    for n, outs in plan:
        ins = refs[start : start + n]
        start += n
        for parts in outs:
            for i, part in enumerate(parts):
                terms = [r[part].astype(F32) for r in ins]
                while len(terms) > 1:
                    terms = [terms[t] + terms[t + 1] for t in range(0, len(terms), 2)]
                refs[out][i] = terms[0].astype(refs[out].dtype)
            out += 1


def gather(sums, after, steps=2):
    inputs, in_specs, out_shape, out_specs, plan = [], [], [], [], []
    for arrays, count, outs in sums:
        cols = arrays[0].shape[-1]
        rows = arrays[0].size // cols // count
        plan.append((len(arrays), tuple(parts for parts, _ in outs)))
        for a in arrays:
            inputs.append(a.reshape(count, rows, cols))
            in_specs.append(pl.BlockSpec((count, rows // steps, cols), lambda i: (0, i, 0)))
        for parts, kind in outs:
            out_shape.append(jax.ShapeDtypeStruct((len(parts), rows, cols), kind))
            out_specs.append(pl.BlockSpec((len(parts), rows // steps, cols), lambda i: (0, i, 0)))
    outs = pl.pallas_call(
        functools.partial(gather_kernel, plan),
        grid=(steps,), in_specs=[*in_specs, pl.BlockSpec(memory_space=pl.ANY)], out_specs=out_specs,
        out_shape=out_shape, compiler_params=params(), cost_estimate=cost(3), name="gather",
    )(*inputs, after)
    made = []
    for _, parts in plan:
        made.append(outs[: len(parts)])
        outs = outs[len(parts) :]
    return made


def finish_kernel(counts, own_ref, *refs):
    sums = []
    for n in counts:
        parts = [r[0].astype(F32) for r in refs[:n]]
        refs = refs[n:]
        while len(parts) > 1:
            parts = [parts[t] + parts[t + 1] for t in range(0, len(parts), 2)]
        sums.append(parts[0])
    inp_ref, out_ref, exp_ref, red_ref, vec_ref, sq_ref = refs
    red, exp, in1, in2 = sums
    rows = in1.shape[0]
    vec = in2[rows : rows + vec_ref.shape[0], : vec_ref.shape[1]]
    vec_ref[...] = vec
    in2 = in2[:rows]
    even = jnp.concatenate([in1[:, :128], in2[:, :128], in1[:, 128:], in2[:, 128:]], axis=1)
    odd = jnp.concatenate([in2[:, :128], in1[:, :256], in2[:, 128:], in1[:, 256:]], axis=1)
    odd = pltpu.roll(odd, odd.shape[1] - HD, axis=1)
    inp = jnp.where((own_ref[0] & 1) == 1, odd, even)[:, : inp_ref.shape[1]]
    tall = exp_ref.shape[0]
    out = exp[tall:, :]
    half = out_ref.shape[1]
    out = jnp.concatenate([out[:, :half], pltpu.roll(out, half, axis=1)[:, :half]], axis=0)
    inp_ref[...] = inp
    out_ref[...] = out
    exp_ref[...] = exp[:tall, :]
    red_ref[...] = red
    squares = jnp.zeros((1, 1), F32)
    for g in (inp, out, exp[:tall, :], red, vec):
        squares = squares + jnp.sum(jnp.sum(g * g, axis=0, keepdims=True), axis=1, keepdims=True)
    sq_ref[...] = jnp.broadcast_to(squares, sq_ref.shape)


def finish(own, red, exp, in1, in2):
    piece = in1[0].shape[1]
    tall = exp[0].shape[1] - piece // 2
    vmem = pl.BlockSpec(memory_space=pltpu.VMEM)
    inputs = [*red, *exp, *in1, *in2]
    return pl.pallas_call(
        functools.partial(finish_kernel, tuple(map(len, (red, exp, in1, in2)))),
        in_specs=[pl.BlockSpec(memory_space=pltpu.SMEM), *[vmem] * len(inputs)],
        out_specs=[vmem] * 6,
        out_shape=[
            jax.ShapeDtypeStruct((piece, 9 * HD), F32),
            jax.ShapeDtypeStruct((piece, 3 * HD), F32),
            jax.ShapeDtypeStruct((tall, exp[0].shape[2]), F32),
            jax.ShapeDtypeStruct(red[0].shape[1:], F32),
            jax.ShapeDtypeStruct((3, piece), F32),
            jax.ShapeDtypeStruct((8, LANES), F32),
        ],
        compiler_params=params(), cost_estimate=cost(3), name="finish",
    )(own, *inputs)


def adam_step(master, moment_one, moment_two, gradient, step_rate, decay_weight):
    new_one = 0.9 * moment_one + 0.1 * gradient
    new_two = 0.999 * moment_two + 0.001 * gradient * gradient
    corrected_one = new_one / (1.0 - 0.9**STEP)
    corrected_two = new_two / (1.0 - 0.999**STEP)
    new_master = master - step_rate * (
        corrected_one / (jnp.sqrt(corrected_two) + 1e-08) + decay_weight * master
    )
    return (new_one, new_two, new_master, new_master.astype(BF))


def adam_kernel(rates, turned, squares_ref, *refs):
    n = len(rates)
    ins, outs = refs[: 4 * n], refs[4 * n :]
    norm = jnp.sqrt(squares_ref[0:1, 0:1])
    outs[0][...] = norm
    factor = 1.0 / jnp.maximum(norm, 1.0)
    for a in range(n):
        master, one, two, grad = (r[...] for r in ins[4 * a : 4 * a + 4])
        if turned[a]:
            grad = grad.T
        made = adam_step(master, one, two, grad * factor, rates[a][0], rates[a][1])
        for b in range(4):
            outs[1 + 4 * a + b][...] = made[b]


def adam_all(squares, states, grads, rates, turned):
    inputs, out_shape = [squares], [jax.ShapeDtypeStruct((1, 1), F32)]
    for state, grad in zip(states, grads):
        inputs += [*state, grad]
        shape = state[0].shape
        out_shape += [jax.ShapeDtypeStruct(shape, F32)] * 3 + [jax.ShapeDtypeStruct(shape, BF)]
    vmem = pl.BlockSpec(memory_space=pltpu.VMEM)
    return pl.pallas_call(
        functools.partial(adam_kernel, rates, turned),
        in_specs=[vmem] * len(inputs), out_specs=[vmem] * len(out_shape), out_shape=out_shape,
        compiler_params=params(), cost_estimate=cost(5), name="adam",
    )(*inputs)


def mover(dp, seq):
    def move(value, bits_d, bits_s):
        pairs = [(d * seq + s, (d ^ bits_d) * seq + (s ^ bits_s)) for d in range(dp) for s in range(seq)]
        return lax.ppermute(value, AXES, pairs)

    return move


def tree_sum(move, value):
    value = value + move(value, 0, 1)
    value = (value + move(value, 0, 2)) + (move(value, 1, 0) + move(value, 1, 2))
    return (value + move(value, 2, 0)) + (move(value, 4, 0) + move(value, 6, 0))


def spread_out(move, parts):
    return [parts[0], *(move(parts[b], 2 * b, 0) for b in (1, 2, 3))]


def plane(move, parts):
    return [parts[0], move(parts[1], 1, 0), move(parts[2], 0, 2), move(parts[3], 1, 2)]


def scatter_plain(parts, dim):
    part = lax.psum_scatter(parts, "seq", scatter_dimension=0, tiled=True)[0].astype(F32)
    return lax.psum_scatter(part, "dp", scatter_dimension=dim, tiled=True)


def in_order(kept, sent):
    parts = jnp.stack([kept, sent], axis=1)
    rows, cols = parts.shape[-2:]
    return parts.reshape(4, 2, 4, rows, cols).swapaxes(1, 2).reshape(4, 8 * rows, cols)


HALVES = tuple((parts, BF) for parts in ((0, 2), (4, 6), (1, 5), (3, 7)))
PAIR = (((0,), BF), ((1,), BF))
QUARTERS = tuple(((part,), BF) for part in range(4))
ONE = (((0,), BF),)
Z_HALVES = (((0, 1), BF), ((2, 3), BF))


def both_ways(move, cut):
    y_keep, y_send, x_keep, x_send = cut
    return (y_keep, move(y_send, 0, 2)), (x_keep, move(x_send, 1, 0))


def turned_ways(move, y_cut, x_cut):
    return (y_cut[0], move(y_cut[1], 1, 0)), (x_cut[0], move(x_cut[1], 0, 2))


def reduce_fast(move, own, back, behind_of, input_weight, gbt, act, red_s, vec1):
    red_c = move(red_s, 0, 1)
    red_k = reduce_kept(own, gbt, act)
    (red,) = gather([((red_k, red_c), 8, HALVES)], red_k)
    red_y, red_x = both_ways(move, red)

    gf, grad_mixed, exp_s, exp_k, vec2 = behind_of(red[0])
    exp_c = move(exp_s, 0, 1)
    red_y, red_x = gather([(red_y, 2, PAIR), (red_x, 2, PAIR)], vec2)
    red_y, red_x = turned_ways(move, red_y, red_x)

    dq0, dkv0, vb0, gw = back(0, CALLS[0], grad_mixed, red_y[0], last=False)
    (red_k,), (red_s,), exp = gather([(red_y, 1, ONE), (red_x, 1, ONE), ((exp_k, exp_c), 8, HALVES)], vb0)
    red = red_k, move(red_s, 4, 0)
    exp_y, exp_x = both_ways(move, exp)

    dq1, dkv1, vb1, in_s1, in_k1 = back(0, CALLS[1], grad_mixed, red_k, gw=gw)
    in_c1 = move(in_s1, 0, 1)
    (red_k, red_s), exp_y, exp_x = gather([(red, 2, PAIR), (exp_y, 2, PAIR), (exp_x, 2, PAIR)], vb1)
    red = red_k, move(red_s, 2, 0)
    exp_y, exp_x = turned_ways(move, exp_y, exp_x)

    gx, dx = frames_back(input_weight, gf, red_k, CALLS[:2], (dq0, dq1), (dkv0, dkv1))
    (exp_k,), (exp_s,), in1 = gather([(exp_y, 1, ONE), (exp_x, 1, ONE), ((in_k1, in_c1), 4, QUARTERS)], gx)
    exp = exp_k, move(exp_s, 4, 0)
    in1 = plane(move, in1)

    dq2, dkv2, vb2, in_s2, in_k2 = back(1, CALLS[2], grad_mixed, exp_k, vecs=(vec1, vec2, vb0, vb1))
    in_c2 = move(in_s2, 0, 1)
    (exp_k, exp_s), (in1_k, in1_s) = gather([(exp, 2, PAIR), (in1, 4, Z_HALVES)], vb2, 1)
    in1 = in1_k, move(in1_s, 4, 0)
    (in2,) = gather([((in_k2, in_c2), 4, QUARTERS)], exp_k, 1)
    in2 = plane(move, in2)

    gx, dx_s, dx_k = frames_back(input_weight, gx, in2[0], CALLS[2:], (dq2,), (dkv2,), dx)
    dx_c = move(dx_s, 0, 1)
    in2, (in1_k, in1_s) = gather([(in2, 4, QUARTERS), (in1, 2, PAIR)], gx, 1)
    in2 = spread_out(move, in2)
    in1 = in1_k, move(in1_s, 2, 0)
    exp = exp_k, move(exp_s, 2, 0)
    ((dx_k, dx_s),) = gather([((dx_k, dx_c), 2, (((0,), F32), ((1,), BF)))], in1_k)
    return red, exp, in1, in2, gx, (dx_k, move(dx_s, 0, 2))


def reduce_plain(move, own, back, behind_of, input_weight, gbt, act, red_s, vec1):
    red_k = reduce_kept(own, gbt, act)
    gf, grad_mixed, exp_s, exp_k, vec2 = behind_of(red_k)
    dq0, dkv0, vb0, gw = back(0, CALLS[0], grad_mixed, vec2, last=False)
    dq1, dkv1, vb1, in_s1, in_k1 = back(0, CALLS[1], grad_mixed, vb0, gw=gw)
    dq2, dkv2, vb2, in_s2, in_k2 = back(1, CALLS[2], grad_mixed, vb1, vecs=(vec1, vec2, vb0, vb1))
    gx, dx = frames_back(input_weight, gf, vb2, CALLS[:2], (dq0, dq1), (dkv0, dkv1))
    gx, dx_s, dx_k = frames_back(input_weight, gx, vb2, CALLS[2:], (dq2,), (dkv2,), dx)
    ((dx_keep, dx_send),) = gather([((dx_k, move(dx_s, 0, 1)), 2, (((0,), F32), ((1,), BF)))], vb2)
    dx = dx_keep, move(dx_send, 0, 2)
    red = scatter_plain(in_order(red_k, red_s), 0)
    in1 = scatter_plain(in_order(in_k1, in_s1), 0)
    both = in_order(in_k2, in_s2)
    both = both.reshape(4, 8, -1, both.shape[-1])
    piece = in_k1.shape[2]
    in2 = scatter_plain(both[:, :, :piece].reshape(4, 8 * piece, -1), 0)
    vec = scatter_plain(both[:, :, piece : piece + 3, :piece].swapaxes(1, 2).reshape(4, 3, -1), 1)
    both = jnp.stack([exp_k, exp_s], axis=1).transpose(0, 1, 3, 2, 4, 5)
    tall, wide = both.shape[-2] - piece // 2, both.shape[-1]
    both = both.reshape(4, 8, -1, wide)
    exp = scatter_plain(both[:, :, :tall].swapaxes(1, 2).reshape(4, tall, 8 * wide), 1)
    out = both[:, :, tall:].reshape(4, 8, piece // 2, 2, wide // 2).swapaxes(2, 3)
    out = scatter_plain(out.reshape(4, 8 * piece, wide // 2), 0)
    even = jnp.concatenate([in1[:, :128], in2[:, :128], in1[:, 128:], in2[:, 128:192]], axis=1)
    odd = jnp.concatenate([in2[:, 64:128], in1[:, :256], in2[:, 128:], in1[:, 256:]], axis=1)
    inp = jnp.where(lax.axis_index("seq") % 2 == 1, odd, even)
    squares = sum(jnp.sum(g * g) for g in (inp, out, exp, red, vec))
    squares = lax.psum(jnp.full((8, LANES), squares, F32), AXES)
    return inp, out, exp, red, vec, squares, gx, dx


def local(
    frames, cotangent, lengths,
    input_weight, output_weight, expand_weight, reduce_weight, vector_copy,
    *states,
):
    rows, width = frames.shape
    seq, dp = lax.axis_size("seq"), lax.axis_size("dp")
    slab = rows * seq
    move = mover(dp, seq)
    own_s, own_d = lax.axis_index("seq"), lax.axis_index("dp")
    fast = dp == 8
    vectors = vector_copy.astype(F32)

    across = move(frames, 0, 2)
    near = move(frames, 0, 1)
    far = move(across, 0, 1)

    first_end = lengths[0, 0]
    second_end = first_end + lengths[0, 1]
    third_end = second_end + lengths[0, 2]
    order = jnp.array([0, 2, 1, 3], jnp.int32) ^ own_s
    positions = (order[:, None] * rows + jnp.arange(rows, dtype=jnp.int32)[None, :]).reshape(slab, 1)
    segments = sum((positions >= end).astype(jnp.int32) for end in (first_end, second_end, third_end))
    lanes = jnp.arange(LANES, dtype=jnp.int32)[None, :]
    kmask = jnp.where((segments == lanes) | (lanes > 3), 0.0, MASK).astype(BF)
    qhot = (segments[:rows] == lanes).astype(BF)
    if fast:
        own = jnp.stack([own_s, own_d]).astype(jnp.int32)
    else:
        own = jnp.zeros((2,), jnp.int32)

    mixed, e, rinv, q, k, v, x_t = attend((frames, across, near, far), input_weight, vectors, kmask, qhot)
    layer, act, slope, norm1, inv1, hlt, mt, gs, gb, gbt, red_s, vec1 = ahead(
        own, mixed, frames, cotangent, qhot, output_weight, expand_weight, reduce_weight, vectors
    )

    def behind_of(after):
        return behind(
            own, slope, gb, gs, norm1, inv1, hlt, mt, output_weight, expand_weight, reduce_weight, vectors, after
        )

    def back(group, pairs, grad_mixed, after, **more):
        return attend_back(group, pairs, own, e, q, k, v, grad_mixed, mixed, rinv, x_t, after, **more)

    if fast:
        red, exp, in1, in2, gx, dx = reduce_fast(move, own, back, behind_of, input_weight, gbt, act, red_s, vec1)
        inp, out, exp, red, vec, squares = finish(own, red, exp, in1, in2)
        squares = tree_sum(move, squares)
    else:
        inp, out, exp, red, vec, squares, gx, dx = reduce_plain(
            move, own, back, behind_of, input_weight, gbt, act, red_s, vec1
        )
    frames_gradient = frames_end(gx, *dx)

    grads = [inp, out, exp, red, vec]
    masters, firsts, seconds = (list(states[i : i + 5]) for i in (0, 5, 10))
    for group in (masters, firsts, seconds):
        group[3] = group[3].T
    hidden = expand_weight.shape[1]
    wide, narrow = 2.0 * width**-0.5, 2.0 * hidden**-0.5
    norm, *made = adam_all(
        squares, list(zip(masters, firsts, seconds)), grads,
        ((wide, 0.01), (wide, 0.01), (wide, 0.01), (narrow, 0.01), (0.5, 0.0)),
        (False, True, False, False, False),
    )
    made[12:16] = [m.T for m in made[12:16]]
    return (layer, frames_gradient, norm.reshape(()), *made)


def solution(mesh):
    tokens, whole = P(("dp", "seq"), None), P()
    state = (P("dp", "seq"), *(P("seq", "dp"),) * 4)
    outs = tuple(s for s in state for _ in range(4))
    return jax.shard_map(
        local,
        mesh=mesh,
        in_specs=(tokens, tokens, P("dp", None), *(whole,) * 5, *state * 3),
        out_specs=(tokens, tokens, whole, *outs),
        check_vma=False,
    )
```

```python
import functools

import jax
import jax.numpy as jnp
from jax import lax
from jax.experimental import pallas as pl
from jax.experimental.pallas import tpu as pltpu
from jax.sharding import PartitionSpec as P

HD = 64
STEP = 10
LANES = 128
NORM_EPS = 1e-05
MASK = -float(2**30)
BF = jnp.bfloat16
F32 = jnp.float32
AXES = ("dp", "seq")

PLACES = (
    {
        0: ((0, 0, 0), (1, 1, 1), (2, 2, 2)),
        2: ((0, 0, 1), (1, 1, 2), (2, 3, 0)),
        3: ((0, 0, 2), (1, 2, 0), (2, 3, 1)),
        5: ((0, 1, 0), (1, 2, 1), (2, 3, 2)),
    },
    {
        1: ((0, 0, 0), (1, 1, 1), (2, 2, 1), (2, 3, 0)),
        4: ((0, 0, 1), (0, 1, 0), (1, 2, 0), (2, 3, 1)),
    },
)
WIDTHS = (3 * LANES, 2 * LANES)
CALLS = ((0, 2), (3, 5), (1, 4))


def params(**more):
    return pltpu.CompilerParams(vmem_limit_bytes=34 * 2**20, **more)


def cost(microseconds):
    return pl.CostEstimate(flops=int(microseconds * 4.4e9), bytes_accessed=0, transcendentals=0)


def dot(a, b):
    return lax.dot_general(a, b, (((1,), (0,)), ((), ())), preferred_element_type=F32)


def dot_t(a, b):
    return lax.dot_general(a, b, (((1,), (1,)), ((), ())), preferred_element_type=F32)


def attend_kernel(
    x0_ref, x1_ref, x2_ref, x3_ref, wq_ref, wk_ref, wv_ref, vec_ref, kmask_ref, qhot_ref,
    mixed_ref, e_ref, rinv_ref, q_ref, k_ref, v_ref, xt_ref, x_ref,
):
    rows = q_ref.shape[0]
    step = pl.program_id(0)
    wide = wq_ref.shape[1]
    pairs = wide // LANES

    @pl.when(step == 0)
    def _():
        for i, ref in enumerate((x0_ref, x1_ref, x2_ref, x3_ref)):
            x_ref[i * rows : (i + 1) * rows, :] = ref[...]

    xt_ref[...] = x_ref[:, pl.ds(pl.multiple_of(step * wide, LANES), wide)].T
    k = dot(x_ref[...], wk_ref[...]).astype(BF)
    v = (dot(x_ref[...], wv_ref[...]) + vec_ref[1:2, :]).astype(BF)
    q = (dot(x_ref[:rows, :], wq_ref[...]) + vec_ref[0:1, :]).astype(BF)
    q = q * jnp.asarray(HD**-0.5, BF)
    q_ref[...] = q
    k_ref[...] = k
    v_ref[...] = v
    low = lax.broadcasted_iota(jnp.int32, (rows, LANES), 1) < HD
    part = lambda a, p: a[:, p * LANES : (p + 1) * LANES]
    keys = [jnp.concatenate([part(k, p), kmask_ref[...]], axis=1) for p in range(pairs)]
    values = [jnp.concatenate([part(v, p), jnp.ones((v.shape[0], LANES), BF)], axis=1) for p in range(pairs)]

    def score(head):
        qh = part(q, head // 2)
        qh = jnp.where(low if head % 2 == 0 else jnp.logical_not(low), qh, jnp.zeros_like(qh))
        return dot_t(jnp.concatenate([qh, qhot_ref[...]], axis=1), keys[head // 2])

    following = score(0)
    done = []
    for head in range(2 * pairs):
        scores = following
        if head + 1 < 2 * pairs:
            following = score(head + 1)
        e = jnp.exp(scores - jnp.max(scores, axis=1, keepdims=True)).astype(BF)
        e_ref[head] = e
        both = dot(e, values[head // 2])
        done.append((both[:, :LANES], 1.0 / both[:, LANES:]))
        if head % 2 == 1:
            (out0, rinv0), (out1, rinv1) = done[-2:]
            span = slice(head // 2 * LANES, (head // 2 + 1) * LANES)
            rinv = jnp.where(low, rinv0, rinv1)
            rinv_ref[:, span] = rinv
            mixed_ref[:, span] = (jnp.where(low, out0, out1) * rinv).astype(BF)


def attend(blocks, input_weight, vectors, kmask, qhot):
    rows, width = blocks[0].shape
    slab = rows * len(blocks)
    wide = 2 * LANES
    steps = width // wide
    full = lambda a: pl.BlockSpec(a.shape, lambda p: (0,) * a.ndim)
    cols = lambda r, off=0: pl.BlockSpec((r, wide), lambda p: (0, p + off))
    return pl.pallas_call(
        attend_kernel,
        grid=(steps,),
        in_specs=[
            *map(full, blocks), cols(width), cols(width, steps), cols(width, 2 * steps),
            cols(vectors.shape[0]), full(kmask), full(qhot),
        ],
        out_specs=[
            cols(rows), pl.BlockSpec((wide // HD, rows, slab), lambda p: (p, 0, 0)), cols(rows), cols(rows),
            cols(slab), cols(slab), pl.BlockSpec((wide, slab), lambda p: (p, 0)),
        ],
        out_shape=[
            jax.ShapeDtypeStruct((rows, width), BF),
            jax.ShapeDtypeStruct((width // HD, rows, slab), BF),
            jax.ShapeDtypeStruct((rows, width), F32),
            jax.ShapeDtypeStruct((rows, width), BF),
            jax.ShapeDtypeStruct((slab, width), BF),
            jax.ShapeDtypeStruct((slab, width), BF),
            jax.ShapeDtypeStruct((width, slab), BF),
        ],
        scratch_shapes=[pltpu.VMEM((slab, width), BF)],
        compiler_params=params(), cost_estimate=cost(20),
        name="attend",
    )(*blocks, input_weight, input_weight, input_weight, vectors, kmask, qhot)


def spot(d, own_d):
    rel = d ^ own_d
    return (rel & 1) * 4 + (rel >> 1)


def turn(j):
    return jnp.where(j < 2, 2 * j + 1, 2 * (j - 2))


def store_rows(ref, block, own_d):
    piece = block.shape[0] // 8
    for d in range(8):
        ref[0, spot(d, own_d)] = block[d * piece : (d + 1) * piece, :]


def reduce_kernel(own_ref, gbt_ref, act_ref, rk_ref):
    store_rows(rk_ref, dot(gbt_ref[...], act_ref[0]).astype(BF), own_ref[1])


def reduce_kept(own, gbt, act):
    width, rows = gbt.shape
    chunks, _, cut = act.shape
    return pl.pallas_call(
        reduce_kernel,
        grid_spec=pltpu.PrefetchScalarGridSpec(
            num_scalar_prefetch=1,
            grid=(2,),
            in_specs=[
                pl.BlockSpec((width, rows), lambda j, own: (0, 0)),
                pl.BlockSpec((1, rows, cut), lambda j, own: (j + 2, 0, 0)),
            ],
            out_specs=pl.BlockSpec((1, 8, width // 8, cut), lambda j, own: (j, 0, 0, 0)),
        ),
        out_shape=jax.ShapeDtypeStruct((2, 8, width // 8, cut), BF),
        compiler_params=params(), cost_estimate=cost(5),
        name="reduce_kept",
    )(own, gbt, act)


def ahead_kernel(
    own_ref, mixed_ref, x_ref, cot_ref, qhot_ref, wo_ref, we_ref, wr_ref, vec_ref,
    layer_ref, act_ref, slope_ref, norm1_ref, inv1_ref, hlt_ref, mt_ref, gs_ref, gb_ref, gbt, rs_ref, vg_ref,
    act, hid, hl, acc,
):
    step = pl.program_id(0)
    own_s, own_d = own_ref[0], own_ref[1]
    rows, width = x_ref.shape
    chunks = act.shape[0]
    j = lax.rem(step, chunks)
    shard = turn(j) ^ own_s
    row = lambda i: vec_ref[i : i + 1, :]

    @pl.when(step == 0)
    def _():
        z = x_ref[...].astype(F32) + dot(mixed_ref[...], wo_ref[...]) + row(2)
        center = z - jnp.mean(z, axis=1, keepdims=True)
        inverse = lax.rsqrt(jnp.mean(center * center, axis=1, keepdims=True) + NORM_EPS)
        normed = center * inverse
        hidden = normed * row(3) + row(4)
        hid[...] = hidden
        norm1_ref[...] = normed
        inv1_ref[...] = jnp.broadcast_to(inverse, inv1_ref.shape)
        low = hidden.astype(BF)
        hl[...] = low
        hlt_ref[...] = low.T
        mt_ref[...] = mixed_ref[...].T
        vg_ref[...] = jnp.zeros_like(vg_ref)

    @pl.when(step < chunks)
    def _():
        pre = dot(hl[...], we_ref[...]) + vec_ref[pl.ds(8 + shard, 1), :]
        cdf = 0.5 * (1.0 + lax.erf(pre * 0.7071067811865476))
        density = jnp.exp(-0.5 * pre * pre) * 0.3989422804014327
        low = (pre * cdf).astype(BF)
        act[j] = low
        act_ref[0] = low
        slope_ref[0] = cdf + pre * density
        part = dot(low, wr_ref[...])

        @pl.when(step == 0)
        def _():
            acc[...] = part

        @pl.when(step > 0)
        def _():
            acc[...] += part

    @pl.when(step == chunks - 1)
    def _():
        z = hid[...] + acc[...] + row(5)
        center = z - jnp.mean(z, axis=1, keepdims=True)
        inverse = lax.rsqrt(jnp.mean(center * center, axis=1, keepdims=True) + NORM_EPS)
        normed = center * inverse
        valid = 1.0 - qhot_ref[:, 3:4].astype(F32)
        layer_ref[...] = ((normed * row(6) + row(7)) * valid).astype(BF)
        gy = cot_ref[...].astype(F32) * valid
        vg_ref[6:7, :] = jnp.sum(gy * normed, axis=0, keepdims=True)
        vg_ref[7:8, :] = jnp.sum(gy, axis=0, keepdims=True)
        e = gy * row(6)
        grad = e - jnp.mean(e, axis=1, keepdims=True)
        grad = (grad - normed * jnp.mean(e * normed, axis=1, keepdims=True)) * inverse
        low = grad.astype(BF)
        vg_ref[5:6, :] = jnp.sum(low.astype(F32), axis=0, keepdims=True)
        gb_ref[...] = low
        gbt[...] = low.T
        gs_ref[...] = grad

    @pl.when(step >= chunks)
    def _():
        store_rows(rs_ref, dot(gbt[...], act[j]).astype(BF), own_d)


def ahead(own, mixed, frames, cotangent, qhot, output_weight, expand_weight, reduce_weight, vectors):
    rows, width = frames.shape
    hidden = expand_weight.shape[1]
    chunks = 4
    cut = hidden // chunks
    piece = width // 8
    first = lambda s: jnp.minimum(s, chunks - 1)
    shard_of = lambda s, own: turn(first(s)) ^ own[0]
    full = lambda shape: pl.BlockSpec(shape, lambda s, own: (0,) * len(shape))
    chunk = pl.BlockSpec((1, rows, cut), lambda s, own: (first(s), 0, 0))
    return pl.pallas_call(
        ahead_kernel,
        grid_spec=pltpu.PrefetchScalarGridSpec(
            num_scalar_prefetch=1,
            grid=(chunks + 2,),
            in_specs=[
                full(mixed.shape), full(frames.shape), full(cotangent.shape), full(qhot.shape),
                full(output_weight.shape),
                pl.BlockSpec((width, cut), lambda s, own: (0, shard_of(s, own))),
                pl.BlockSpec((cut, width), lambda s, own: (shard_of(s, own), 0)),
                full(vectors.shape),
            ],
            out_specs=[
                full((rows, width)), chunk, chunk, full((rows, width)), full((rows, LANES)),
                full((width, rows)), full((width, rows)), full((rows, width)), full((rows, width)), full((width, rows)),
                pl.BlockSpec((1, 8, piece, cut), lambda s, own: (jnp.maximum(s - chunks, 0), 0, 0, 0)),
                full((16, width)),
            ],
            scratch_shapes=[
                pltpu.VMEM((chunks, rows, cut), BF),
                pltpu.VMEM((rows, width), F32),
                pltpu.VMEM((rows, width), BF),
                pltpu.VMEM((rows, width), F32),
            ],
        ),
        out_shape=[
            jax.ShapeDtypeStruct((rows, width), BF),
            jax.ShapeDtypeStruct((chunks, rows, cut), BF),
            jax.ShapeDtypeStruct((chunks, rows, cut), F32),
            jax.ShapeDtypeStruct((rows, width), F32),
            jax.ShapeDtypeStruct((rows, LANES), F32),
            jax.ShapeDtypeStruct((width, rows), BF),
            jax.ShapeDtypeStruct((width, rows), BF),
            jax.ShapeDtypeStruct((rows, width), F32),
            jax.ShapeDtypeStruct((rows, width), BF),
            jax.ShapeDtypeStruct((width, rows), BF),
            jax.ShapeDtypeStruct((2, 8, piece, cut), BF),
            jax.ShapeDtypeStruct((16, width), F32),
        ],
        compiler_params=params(), cost_estimate=cost(20),
        name="ahead",
    )(own, mixed, frames, cotangent, qhot, output_weight, expand_weight, reduce_weight, vectors)


def behind_kernel(
    own_ref, slope_ref, gb_ref, gs_ref, norm1_ref, inv1_ref, hlt_ref, mt_ref, wo_ref, we_ref, wr_ref, vec_ref, _,
    gf_ref, gm_ref, es_ref, ek_ref, vg_ref,
    acc, tmp,
):
    j = pl.program_id(0)
    own_s, own_d = own_ref[0], own_ref[1]
    rows, width = gb_ref.shape
    shard = turn(j) ^ own_s
    row = lambda i: vec_ref[i : i + 1, :]
    piece, fourth = width // 8, width // 4

    @pl.when(j == 0)
    def _():
        acc[...] = gs_ref[...]
        vg_ref[...] = jnp.zeros_like(vg_ref)

    grad_act = dot_t(gb_ref[...], wr_ref[...])
    low = (grad_act * slope_ref[0]).astype(BF)
    vg_ref[pl.ds(8 + shard, 1), :] = jnp.sum(low.astype(F32), axis=0, keepdims=True)
    acc[...] += dot_t(low, we_ref[...])
    grad_e = dot(hlt_ref[...], low).astype(BF)
    tmp[...] = grad_e.reshape(tmp.shape)
    half = grad_e.shape[1] // 2
    rz = shard ^ (own_d >> 1)
    for part, ref in ((1, es_ref), (0, ek_ref)):
        for ry in range(2):
            for t in range(2):
                block = tmp[own_s ^ (2 * ry + part), :, t * half : (t + 1) * half]
                ref[ry, t ^ (own_d & 1), rz, :fourth, :] = block

    @pl.when(j == pl.num_programs(0) - 1)
    def _():
        gy = acc[...]
        normed = norm1_ref[...]
        vg_ref[3:4, :] = jnp.sum(gy * normed, axis=0, keepdims=True)
        vg_ref[4:5, :] = jnp.sum(gy, axis=0, keepdims=True)
        e = gy * row(3)
        grad = e - jnp.mean(e, axis=1, keepdims=True)
        grad = (grad - normed * jnp.mean(e * normed, axis=1, keepdims=True)) * inv1_ref[:, :1]
        gf_ref[...] = grad
        low = grad.astype(BF)
        vg_ref[2:3, :] = jnp.sum(low.astype(F32), axis=0, keepdims=True)
        gm_ref[...] = dot_t(low, wo_ref[...]).astype(BF)
        gat = low.T
        for part, ref in ((1, es_ref), (0, ek_ref)):
            for ry in range(2):
                start = pl.multiple_of((own_s ^ (2 * ry + part)) * fourth, fourth)
                out = dot_t(gat, mt_ref[pl.ds(start, fourth), :]).astype(BF)
                for d in range(8):
                    block = out[d * piece : (d + 1) * piece, :]
                    block = jnp.concatenate([block[: piece // 2], block[piece // 2 :]], axis=1)
                    ref[ry, (d & 1) ^ (own_d & 1), (d >> 1) ^ (own_d >> 1), fourth:, :] = block


def behind(own, slope, gb, gs, norm1, inv1, hlt, mt, output_weight, expand_weight, reduce_weight, vectors, after):
    rows, width = gb.shape
    hidden = expand_weight.shape[1]
    chunks = 4
    cut = hidden // chunks
    fourth, eighth = width // 4, hidden // 8
    shard_of = lambda s, own: turn(s) ^ own[0]
    full = lambda shape: pl.BlockSpec(shape, lambda s, own: (0,) * len(shape))
    spread = (2, 2, 4, fourth + width // 16, eighth)
    return pl.pallas_call(
        behind_kernel,
        grid_spec=pltpu.PrefetchScalarGridSpec(
            num_scalar_prefetch=1,
            grid=(chunks,),
            in_specs=[
                pl.BlockSpec((1, rows, cut), lambda s, own: (s, 0, 0)),
                full(gb.shape), full(gs.shape), full(norm1.shape), full(inv1.shape), full(hlt.shape), full(mt.shape),
                full(output_weight.shape),
                pl.BlockSpec((width, cut), lambda s, own: (0, shard_of(s, own))),
                pl.BlockSpec((cut, width), lambda s, own: (shard_of(s, own), 0)),
                full(vectors.shape), pl.BlockSpec(memory_space=pl.ANY),
            ],
            out_specs=[full((rows, width)), full((rows, width)), full(spread), full(spread), full((16, width))],
            scratch_shapes=[pltpu.VMEM((rows, width), F32), pltpu.VMEM((4, fourth, cut), BF)],
        ),
        out_shape=[
            jax.ShapeDtypeStruct((rows, width), F32),
            jax.ShapeDtypeStruct((rows, width), BF),
            jax.ShapeDtypeStruct(spread, BF),
            jax.ShapeDtypeStruct(spread, BF),
            jax.ShapeDtypeStruct((16, width), F32),
        ],
        compiler_params=params(), cost_estimate=cost(18),
        name="behind",
    )(own, slope, gb, gs, norm1, inv1, hlt, mt, output_weight, expand_weight, reduce_weight, vectors, after)


def back_kernel(group, pairs, first, last, own_ref, e_hbm, *rest):
    n = len(pairs)
    ins = [rest[6 * i : 6 * i + 6] for i in range(n)]
    rest = list(rest[6 * n :])
    xt_hbm, _ = rest[:2]
    rest = rest[2:]
    gw_in_ref = None if first else rest.pop(0)
    vec_in = [rest.pop(0) for _ in range(4)] if group == 1 else []
    dq_ref, dkv_ref, vb_ref = rest[:3]
    rest = rest[3:]
    if last:
        gs_ref, gk_ref, gw, e_ref, xt_ref, sems, *vecs = rest
    else:
        gw, e_ref, xt_ref, sems = rest
    copies = [
        pltpu.make_async_copy(e_hbm.at[2 * p + h], e_ref.at[2 * i + h], sems.at[2 * i + h])
        for i, p in enumerate(pairs) for h in range(2)
    ]
    copies.append(pltpu.make_async_copy(xt_hbm, xt_ref, sems.at[2 * n]))
    for copy in copies:
        copy.start()
    own_s, own_d = own_ref[0], own_ref[1]
    rows = ins[0][0].shape[0]
    low = lax.broadcasted_iota(jnp.int32, (rows, LANES), 1) < HD
    if not first:
        gw[...] = gw_in_ref[...]

    def prepare(i):
        q_ref, k_ref, v_ref, gm_ref, mixed_ref, rinv_ref = ins[i]
        gm = gm_ref[...].astype(F32) * rinv_ref[...]
        both = gm * mixed_ref[...].astype(F32)
        gm_low = gm.astype(BF)
        return q_ref[...].T, k_ref[...], v_ref[...], gm_low, gm_low.T, both

    ready = [prepare(i) for i in range(n)]

    def start(i, head):
        _, _, v, gm_low, _, both = ready[i]
        own = low if head == 0 else jnp.logical_not(low)
        inner = jnp.sum(jnp.where(own, both, 0.0), axis=1, keepdims=True)
        return dot_t(jnp.where(own, gm_low, jnp.zeros_like(gm_low)), v), inner

    tasks = [(i, head) for i in range(n) for head in range(2)]
    ahead = start(*tasks[0])
    made = []
    for t, (i, head) in enumerate(tasks):
        grad_e, inner = ahead
        if t + 1 < len(tasks):
            ahead = start(*tasks[t + 1])
        copies[t].wait()
        e = e_ref[t]
        ds = (e.astype(F32) * (grad_e - inner)).astype(BF)
        q_t, k, v, _, gm_t, _ = ready[i]
        span = slice(head * HD, (head + 1) * HD)
        made.append((dot(ds, k), dot(q_t[span, :], ds), dot(gm_t[span, :], e)))
    copies[-1].wait()
    blocks = []
    for i in range(n):
        (dq0, dk0, dv0), (dq1, dk1, dv1) = made[2 * i : 2 * i + 2]
        dq = (jnp.where(low, dq0, dq1) * HD**-0.5).astype(BF)
        dkv = jnp.concatenate([dk0, dk1, dv0, dv1], axis=0).astype(BF)
        dq_ref[:, i * LANES : (i + 1) * LANES] = dq
        dkv_ref[2 * i * LANES : 2 * (i + 1) * LANES, :] = dkv
    grad_q = dot(xt_ref[:, :rows], dq_ref[...]).astype(BF)
    grad_kv = dot_t(xt_ref[...], dkv_ref[...]).astype(BF)
    ones = jnp.ones((8, dkv_ref.shape[1]), BF)
    sums = dot_t(ones, dkv_ref[...])
    vb_ref[0:1, :] = jnp.sum(dq_ref[...].astype(F32), axis=0, keepdims=True)
    for i in range(n):
        vb_ref[1:2, i * LANES : (i + 1) * LANES] = sums[0:1, (2 * i + 1) * LANES : (2 * i + 2) * LANES]
    piece = grad_q.shape[0] // 8
    for i, pair in enumerate(pairs):
        blocks = [
            b.reshape(8, piece, LANES)
            for b in (
                grad_q[:, i * LANES : (i + 1) * LANES],
                grad_kv[:, 2 * i * LANES : (2 * i + 1) * LANES],
                grad_kv[:, (2 * i + 1) * LANES : (2 * i + 2) * LANES],
            )
        ]
        for which, shard, place in PLACES[group][pair]:
            gw[shard, :, :piece, place * LANES : (place + 1) * LANES] = blocks[which]
    if group == 1:
        vecs[0][...] = vec_in[0][...] + vec_in[1][...]
        for call, ref in zip(CALLS, (*vec_in[2:], vb_ref)):
            for i, p in enumerate(call):
                vecs[0][0:2, p * LANES : (p + 1) * LANES] = ref[0:2, i * LANES : (i + 1) * LANES]
        vec, tall = vecs[0][...], vecs[0].shape[1]
        for d in range(8):
            turned = pltpu.roll(vec, (tall - piece * d) % tall, axis=1)[:, : gw.shape[3]]
            for shard in range(4):
                block = pltpu.roll(turned, (16 - 3 * shard) % 16, axis=0) if shard else turned
                gw[shard, d, piece:, :] = block.astype(BF)
    if last:
        for ref, part in ((gs_ref, 1), (gk_ref, 0)):
            for ry in range(2):
                for d in range(8):
                    ref[ry, spot(d, own_d)] = gw[own_s ^ (2 * ry + part), d]


def attend_back(group, pairs, own, e, q, k, v, grad_mixed, mixed, rinv, x_t, after, gw=None, last=True, vecs=()):
    first = gw is None
    rows, width = q.shape
    slab = k.shape[0]
    piece = width // 8
    n = len(pairs)
    span = WIDTHS[group]
    full = lambda shape: pl.BlockSpec(shape, lambda i: (0,) * len(shape))
    cols = lambda r, p: pl.BlockSpec((r, LANES), lambda i: (0, p))
    anywhere = pl.BlockSpec(memory_space=pl.ANY)
    inputs, in_specs = [own, e], [pl.BlockSpec(memory_space=pltpu.SMEM), anywhere]
    for p in pairs:
        inputs += [q, k, v, grad_mixed, mixed, rinv]
        in_specs += [cols(rows, p), cols(slab, p), cols(slab, p), cols(rows, p), cols(rows, p), cols(rows, p)]
    inputs += [x_t, after]
    in_specs += [anywhere, anywhere]
    out_shape = [
        jax.ShapeDtypeStruct((rows, n * LANES), BF),
        jax.ShapeDtypeStruct((n * 2 * LANES, slab), BF),
        jax.ShapeDtypeStruct((8, n * LANES), F32),
    ]
    whole = (4, 8, piece + (16 if vecs else 0), span)
    scratch = [pltpu.VMEM((2 * n, rows, slab), BF), pltpu.VMEM(x_t.shape, BF), pltpu.SemaphoreType.DMA((2 * n + 1,))]
    if not first:
        inputs.append(gw)
        in_specs.append(full(whole))
    inputs += vecs
    in_specs += [full(a.shape) for a in vecs]
    if last:
        out_shape += [jax.ShapeDtypeStruct((2, *whole[1:]), BF)] * 2
        scratch.insert(0, pltpu.VMEM(whole, BF))
        if vecs:
            scratch.append(pltpu.VMEM((16, width), F32))
    else:
        out_shape.append(jax.ShapeDtypeStruct(whole, BF))
    return pl.pallas_call(
        functools.partial(back_kernel, group, pairs, first, last),
        grid=(1,), in_specs=in_specs, out_specs=[full(a.shape) for a in out_shape], scratch_shapes=scratch,
        out_shape=out_shape,
        compiler_params=params(), cost_estimate=cost(12),
        name="attend_back",
    )(*inputs)


def frames_kernel(pairs, last, w_ref, gx_in_ref, after_ref, *refs):
    n = len(pairs)
    dqs, dkvs = refs[:n], refs[n : 2 * n]
    refs = list(refs[2 * n :])
    dx_ref = refs.pop(0) if last else None
    gx_ref, *outs, wkv = refs
    j = pl.program_id(0)
    width = gx_ref.shape[1]
    flat = [p for call in pairs for p in call]

    @pl.when(j == 0)
    def _():
        for i, p in enumerate(flat):
            for t in range(2):
                start = (1 + t) * width + p * LANES
                wkv[:, (2 * i + t) * LANES : (2 * i + t + 1) * LANES] = w_ref[:, start : start + LANES]
        wq = jnp.concatenate([w_ref[:, p * LANES : (p + 1) * LANES] for p in flat], axis=1)
        dq = jnp.concatenate([r[...] for r in dqs], axis=1)
        gx_ref[...] = gx_in_ref[...] + dot_t(dq, wq)

    made = dot(wkv[...], jnp.concatenate([r[...] for r in dkvs], axis=0))
    if not last:
        outs[0][0] = made
        return
    made = made + dx_ref[0]

    @pl.when(j < 2)
    def _():
        outs[0][0] = made.astype(BF)

    @pl.when(j >= 2)
    def _():
        outs[1][0] = made


def frames_back(input_weight, gx, after, pairs, dqs, dkvs, dx=None):
    rows, width = gx.shape
    last = dx is not None
    count = 2 * sum(map(len, pairs))
    full = lambda a: pl.BlockSpec(a.shape, lambda j: (0,) * a.ndim)
    column = lambda a: pl.BlockSpec((a.shape[0], rows), lambda j: (0, lax.rem(j + 2, 4)))
    block = lambda pick: pl.BlockSpec((1, width, rows), lambda j: (pick(j), 0, 0))
    if last:
        out_specs = [block(lambda j: jnp.minimum(j, 1)), block(lambda j: jnp.maximum(j - 2, 0))]
        out_shape = [jax.ShapeDtypeStruct((2, width, rows), BF), jax.ShapeDtypeStruct((2, width, rows), F32)]
    else:
        out_specs = [block(lambda j: j)]
        out_shape = [jax.ShapeDtypeStruct((4, width, rows), F32)]
    return pl.pallas_call(
        functools.partial(frames_kernel, pairs, last),
        grid=(4,),
        in_specs=[
            full(input_weight), full(gx), pl.BlockSpec(memory_space=pl.ANY), *map(full, dqs), *map(column, dkvs),
            *([block(lambda j: j)] if last else []),
        ],
        out_specs=[full(gx), *out_specs],
        out_shape=[jax.ShapeDtypeStruct((rows, width), F32), *out_shape],
        scratch_shapes=[pltpu.VMEM((width, count * LANES), BF)],
        compiler_params=params(), cost_estimate=cost(4 if last else 8),
        name="frames_back",
    )(input_weight, gx, after, *dqs, *dkvs, *([dx] if last else []))


def frames_end_kernel(gx_ref, keep_ref, came_ref, out_ref):
    out_ref[...] = gx_ref[...] + (keep_ref[0] + came_ref[0].astype(F32)).T


def frames_end(gx, keep, came):
    rows, width = gx.shape
    across = pl.BlockSpec((rows, LANES), lambda p: (0, p))
    down = pl.BlockSpec((1, LANES, rows), lambda p: (0, p, 0))
    return pl.pallas_call(
        frames_end_kernel,
        grid=(width // LANES,), in_specs=[across, down, down], out_specs=across,
        out_shape=jax.ShapeDtypeStruct((rows, width), F32), compiler_params=params(), cost_estimate=cost(5), name="frames_end",
    )(gx, keep, came)


def gather_kernel(plan, *refs):
    start, out = 0, sum(n for n, _ in plan) + 1
    for n, outs in plan:
        ins = refs[start : start + n]
        start += n
        for parts in outs:
            for i, part in enumerate(parts):
                terms = [r[part].astype(F32) for r in ins]
                while len(terms) > 1:
                    terms = [terms[t] + terms[t + 1] for t in range(0, len(terms), 2)]
                refs[out][i] = terms[0].astype(refs[out].dtype)
            out += 1


def gather(sums, after, steps=2):
    inputs, in_specs, out_shape, out_specs, plan = [], [], [], [], []
    for arrays, count, outs in sums:
        cols = arrays[0].shape[-1]
        rows = arrays[0].size // cols // count
        plan.append((len(arrays), tuple(parts for parts, _ in outs)))
        for a in arrays:
            inputs.append(a.reshape(count, rows, cols))
            in_specs.append(pl.BlockSpec((count, rows // steps, cols), lambda i: (0, i, 0)))
        for parts, kind in outs:
            out_shape.append(jax.ShapeDtypeStruct((len(parts), rows, cols), kind))
            out_specs.append(pl.BlockSpec((len(parts), rows // steps, cols), lambda i: (0, i, 0)))
    outs = pl.pallas_call(
        functools.partial(gather_kernel, plan),
        grid=(steps,), in_specs=[*in_specs, pl.BlockSpec(memory_space=pl.ANY)], out_specs=out_specs,
        out_shape=out_shape, compiler_params=params(), cost_estimate=cost(3), name="gather",
    )(*inputs, after)
    made = []
    for _, parts in plan:
        made.append(outs[: len(parts)])
        outs = outs[len(parts) :]
    return made


def finish_kernel(counts, own_ref, *refs):
    sums = []
    for n in counts:
        parts = [r[0].astype(F32) for r in refs[:n]]
        refs = refs[n:]
        while len(parts) > 1:
            parts = [parts[t] + parts[t + 1] for t in range(0, len(parts), 2)]
        sums.append(parts[0])
    inp_ref, out_ref, exp_ref, red_ref, vec_ref, sq_ref = refs[1:]
    red, exp, in1, in2 = sums
    rows = in1.shape[0]
    vec = in2[rows : rows + vec_ref.shape[0], : vec_ref.shape[1]]
    vec_ref[...] = vec
    in2 = in2[:rows]
    even = jnp.concatenate([in1[:, :128], in2[:, :128], in1[:, 128:], in2[:, 128:]], axis=1)
    odd = jnp.concatenate([in2[:, :128], in1[:, :256], in2[:, 128:], in1[:, 256:]], axis=1)
    odd = pltpu.roll(odd, odd.shape[1] - HD, axis=1)
    inp = jnp.where((own_ref[0] & 1) == 1, odd, even)[:, : inp_ref.shape[1]]
    tall = exp_ref.shape[0]
    out = exp[tall:, :]
    half = out_ref.shape[1]
    out = jnp.concatenate([out[:, :half], pltpu.roll(out, half, axis=1)[:, :half]], axis=0)
    inp_ref[...] = inp
    out_ref[...] = out
    exp_ref[...] = exp[:tall, :]
    red_ref[...] = red
    squares = jnp.zeros((1, 1), F32)
    for g in (inp, out, exp[:tall, :], red, vec):
        squares = squares + jnp.sum(jnp.sum(g * g, axis=0, keepdims=True), axis=1, keepdims=True)
    sq_ref[...] = jnp.broadcast_to(squares, sq_ref.shape)


def finish(own, red, exp, in1, in2, after):
    piece = in1[0].shape[1]
    tall = exp[0].shape[1] - piece // 2
    vmem = pl.BlockSpec(memory_space=pltpu.VMEM)
    inputs = [*red, *exp, *in1, *in2]
    return pl.pallas_call(
        functools.partial(finish_kernel, tuple(map(len, (red, exp, in1, in2)))),
        in_specs=[
            pl.BlockSpec(memory_space=pltpu.SMEM), *[vmem] * len(inputs), pl.BlockSpec(memory_space=pl.ANY)
        ],
        out_specs=[vmem] * 6,
        out_shape=[
            jax.ShapeDtypeStruct((piece, 9 * HD), F32),
            jax.ShapeDtypeStruct((piece, 3 * HD), F32),
            jax.ShapeDtypeStruct((tall, exp[0].shape[2]), F32),
            jax.ShapeDtypeStruct(red[0].shape[1:], F32),
            jax.ShapeDtypeStruct((3, piece), F32),
            jax.ShapeDtypeStruct((8, LANES), F32),
        ],
        compiler_params=params(), cost_estimate=cost(3), name="finish",
    )(own, *inputs, after)


def adam_step(master, moment_one, moment_two, gradient, step_rate, decay_weight):
    new_one = 0.9 * moment_one + 0.1 * gradient
    new_two = 0.999 * moment_two + 0.001 * gradient * gradient
    corrected_one = new_one / (1.0 - 0.9**STEP)
    corrected_two = new_two / (1.0 - 0.999**STEP)
    new_master = master - step_rate * (
        corrected_one / (jnp.sqrt(corrected_two) + 1e-08) + decay_weight * master
    )
    return (new_one, new_two, new_master, new_master.astype(BF))


def adam_kernel(rates, turned, squares_ref, _, *refs):
    n = len(rates)
    ins, outs = refs[: 4 * n], refs[4 * n :]
    norm = jnp.sqrt(squares_ref[0:1, 0:1])
    outs[0][...] = norm
    factor = 1.0 / jnp.maximum(norm, 1.0)
    for a in range(n):
        master, one, two, grad = (r[...] for r in ins[4 * a : 4 * a + 4])
        if turned[a]:
            grad = grad.T
        made = adam_step(master, one, two, grad * factor, rates[a][0], rates[a][1])
        for b in range(4):
            outs[1 + 4 * a + b][...] = made[b]


def adam_all(squares, after, states, grads, rates, turned):
    inputs, out_shape = [squares, after], [jax.ShapeDtypeStruct((1, 1), F32)]
    for state, grad in zip(states, grads):
        inputs += [*state, grad]
        shape = state[0].shape
        out_shape += [jax.ShapeDtypeStruct(shape, F32)] * 3 + [jax.ShapeDtypeStruct(shape, BF)]
    vmem = pl.BlockSpec(memory_space=pltpu.VMEM)
    return pl.pallas_call(
        functools.partial(adam_kernel, rates, turned),
        in_specs=[vmem, pl.BlockSpec(memory_space=pl.ANY), *[vmem] * (len(inputs) - 2)], out_specs=[vmem] * len(out_shape), out_shape=out_shape,
        compiler_params=params(), cost_estimate=cost(5), name="adam",
    )(*inputs)


def mover(dp, seq):
    def move(value, bits_d, bits_s):
        pairs = [(d * seq + s, (d ^ bits_d) * seq + (s ^ bits_s)) for d in range(dp) for s in range(seq)]
        return lax.ppermute(value, AXES, pairs)

    return move


def tree_sum(move, value):
    value = value + move(value, 0, 1)
    value = (value + move(value, 0, 2)) + (move(value, 1, 0) + move(value, 1, 2))
    return (value + move(value, 2, 0)) + (move(value, 4, 0) + move(value, 6, 0))


def spread_out(move, parts):
    return [parts[0], *(move(parts[b], 2 * b, 0) for b in (1, 2, 3))]


def plane(move, parts):
    return [parts[0], move(parts[1], 1, 0), move(parts[2], 0, 2), move(parts[3], 1, 2)]


def scatter_plain(parts, dim):
    part = lax.psum_scatter(parts, "seq", scatter_dimension=0, tiled=True)[0].astype(F32)
    return lax.psum_scatter(part, "dp", scatter_dimension=dim, tiled=True)


def in_order(kept, sent):
    parts = jnp.stack([kept, sent], axis=1)
    rows, cols = parts.shape[-2:]
    return parts.reshape(4, 2, 4, rows, cols).swapaxes(1, 2).reshape(4, 8 * rows, cols)


HALVES = tuple((parts, BF) for parts in ((0, 2), (4, 6), (1, 5), (3, 7)))
PAIR = (((0,), BF), ((1,), BF))
QUARTERS = tuple(((part,), BF) for part in range(4))
ONE = (((0,), BF),)
Z_HALVES = (((0, 1), BF), ((2, 3), BF))


def both_ways(move, cut):
    y_keep, y_send, x_keep, x_send = cut
    return (y_keep, move(y_send, 0, 2)), (x_keep, move(x_send, 1, 0))


def turned_ways(move, y_cut, x_cut):
    return (y_cut[0], move(y_cut[1], 1, 0)), (x_cut[0], move(x_cut[1], 0, 2))


def reduce_fast(move, own, back, behind_of, input_weight, gbt, act, red_s, vec1):
    red_c = move(red_s, 0, 1)
    red_k = reduce_kept(own, gbt, act)
    (red,) = gather([((red_k, red_c), 8, HALVES)], red_k)
    red_y, red_x = both_ways(move, red)

    gf, grad_mixed, exp_s, exp_k, vec2 = behind_of(red[0])
    exp_c = move(exp_s, 0, 1)
    red_y, red_x = gather([(red_y, 2, PAIR), (red_x, 2, PAIR)], vec2)
    red_y, red_x = turned_ways(move, red_y, red_x)

    dq0, dkv0, vb0, gw = back(0, CALLS[0], grad_mixed, red_y[0], last=False)
    (red_k,), (red_s,), exp = gather([(red_y, 1, ONE), (red_x, 1, ONE), ((exp_k, exp_c), 8, HALVES)], vb0)
    red = red_k, move(red_s, 4, 0)
    exp_y, exp_x = both_ways(move, exp)

    dq1, dkv1, vb1, in_s1, in_k1 = back(0, CALLS[1], grad_mixed, red_k, gw=gw)
    in_c1 = move(in_s1, 0, 1)
    (red_k, red_s), exp_y, exp_x = gather([(red, 2, PAIR), (exp_y, 2, PAIR), (exp_x, 2, PAIR)], vb1)
    red = red_k, move(red_s, 2, 0)
    exp_y, exp_x = turned_ways(move, exp_y, exp_x)

    gx, dx = frames_back(input_weight, gf, red_k, CALLS[:2], (dq0, dq1), (dkv0, dkv1))
    (exp_k,), (exp_s,), in1 = gather([(exp_y, 1, ONE), (exp_x, 1, ONE), ((in_k1, in_c1), 4, QUARTERS)], gx)
    exp = exp_k, move(exp_s, 4, 0)
    in1 = plane(move, in1)

    dq2, dkv2, vb2, in_s2, in_k2 = back(1, CALLS[2], grad_mixed, exp_k, vecs=(vec1, vec2, vb0, vb1))
    in_c2 = move(in_s2, 0, 1)
    (exp_k, exp_s), (in1_k, in1_s) = gather([(exp, 2, PAIR), (in1, 4, Z_HALVES)], vb2, 1)
    in1 = in1_k, move(in1_s, 4, 0)
    (in2,) = gather([((in_k2, in_c2), 4, QUARTERS)], exp_k, 1)
    in2 = plane(move, in2)

    gx, dx_s, dx_k = frames_back(input_weight, gx, in2[0], CALLS[2:], (dq2,), (dkv2,), dx)
    dx_c = move(dx_s, 0, 1)
    in2, (in1_k, in1_s) = gather([(in2, 4, QUARTERS), (in1, 2, PAIR)], gx, 1)
    in2 = spread_out(move, in2)
    in1 = in1_k, move(in1_s, 2, 0)
    exp = exp_k, move(exp_s, 2, 0)
    ((dx_k, dx_s),) = gather([((dx_k, dx_c), 2, (((0,), F32), ((1,), BF)))], in1_k)
    return red, exp, in1, in2, gx, (dx_k, move(dx_s, 0, 2))


def reduce_plain(move, own, back, behind_of, input_weight, gbt, act, red_s, vec1):
    red_k = reduce_kept(own, gbt, act)
    gf, grad_mixed, exp_s, exp_k, vec2 = behind_of(red_k)
    dq0, dkv0, vb0, gw = back(0, CALLS[0], grad_mixed, vec2, last=False)
    dq1, dkv1, vb1, in_s1, in_k1 = back(0, CALLS[1], grad_mixed, vb0, gw=gw)
    dq2, dkv2, vb2, in_s2, in_k2 = back(1, CALLS[2], grad_mixed, vb1, vecs=(vec1, vec2, vb0, vb1))
    gx, dx = frames_back(input_weight, gf, vb2, CALLS[:2], (dq0, dq1), (dkv0, dkv1))
    gx, dx_s, dx_k = frames_back(input_weight, gx, vb2, CALLS[2:], (dq2,), (dkv2,), dx)
    ((dx_keep, dx_send),) = gather([((dx_k, move(dx_s, 0, 1)), 2, (((0,), F32), ((1,), BF)))], vb2)
    dx = dx_keep, move(dx_send, 0, 2)
    red = scatter_plain(in_order(red_k, red_s), 0)
    in1 = scatter_plain(in_order(in_k1, in_s1), 0)
    both = in_order(in_k2, in_s2)
    both = both.reshape(4, 8, -1, both.shape[-1])
    piece = in_k1.shape[2]
    in2 = scatter_plain(both[:, :, :piece].reshape(4, 8 * piece, -1), 0)
    vec = scatter_plain(both[:, :, piece : piece + 3, :piece].swapaxes(1, 2).reshape(4, 3, -1), 1)
    both = jnp.stack([exp_k, exp_s], axis=1).transpose(0, 1, 3, 2, 4, 5)
    tall, wide = both.shape[-2] - piece // 2, both.shape[-1]
    both = both.reshape(4, 8, -1, wide)
    exp = scatter_plain(both[:, :, :tall].swapaxes(1, 2).reshape(4, tall, 8 * wide), 1)
    out = both[:, :, tall:].reshape(4, 8, piece // 2, 2, wide // 2).swapaxes(2, 3)
    out = scatter_plain(out.reshape(4, 8 * piece, wide // 2), 0)
    even = jnp.concatenate([in1[:, :128], in2[:, :128], in1[:, 128:], in2[:, 128:192]], axis=1)
    odd = jnp.concatenate([in2[:, 64:128], in1[:, :256], in2[:, 128:], in1[:, 256:]], axis=1)
    inp = jnp.where(lax.axis_index("seq") % 2 == 1, odd, even)
    squares = sum(jnp.sum(g * g) for g in (inp, out, exp, red, vec))
    squares = lax.psum(jnp.full((8, LANES), squares, F32), AXES)
    return inp, out, exp, red, vec, squares, gx, dx


def local(
    frames, cotangent, lengths,
    input_weight, output_weight, expand_weight, reduce_weight, vector_copy,
    *states,
):
    rows, width = frames.shape
    seq, dp = lax.axis_size("seq"), lax.axis_size("dp")
    slab = rows * seq
    move = mover(dp, seq)
    own_s, own_d = lax.axis_index("seq"), lax.axis_index("dp")
    fast = dp == 8
    vectors = vector_copy.astype(F32)

    across = move(frames, 0, 2)
    near = move(frames, 0, 1)
    far = move(across, 0, 1)

    first_end = lengths[0, 0]
    second_end = first_end + lengths[0, 1]
    third_end = second_end + lengths[0, 2]
    order = jnp.array([0, 2, 1, 3], jnp.int32) ^ own_s
    positions = (order[:, None] * rows + jnp.arange(rows, dtype=jnp.int32)[None, :]).reshape(slab, 1)
    segments = sum((positions >= end).astype(jnp.int32) for end in (first_end, second_end, third_end))
    lanes = jnp.arange(LANES, dtype=jnp.int32)[None, :]
    kmask = jnp.where((segments == lanes) | (lanes > 3), 0.0, MASK).astype(BF)
    qhot = (segments[:rows] == lanes).astype(BF)
    if fast:
        own = jnp.stack([own_s, own_d]).astype(jnp.int32)
    else:
        own = jnp.zeros((2,), jnp.int32)

    mixed, e, rinv, q, k, v, x_t = attend((frames, across, near, far), input_weight, vectors, kmask, qhot)
    layer, act, slope, norm1, inv1, hlt, mt, gs, gb, gbt, red_s, vec1 = ahead(
        own, mixed, frames, cotangent, qhot, output_weight, expand_weight, reduce_weight, vectors
    )

    def behind_of(after):
        return behind(
            own, slope, gb, gs, norm1, inv1, hlt, mt, output_weight, expand_weight, reduce_weight, vectors, after
        )

    def back(group, pairs, grad_mixed, after, **more):
        return attend_back(group, pairs, own, e, q, k, v, grad_mixed, mixed, rinv, x_t, after, **more)

    if fast:
        red, exp, in1, in2, gx, dx = reduce_fast(move, own, back, behind_of, input_weight, gbt, act, red_s, vec1)
        inp, out, exp, red, vec, squares = finish(own, red, exp, in1, in2, dx[0])
        squares = tree_sum(move, squares)
    else:
        inp, out, exp, red, vec, squares, gx, dx = reduce_plain(
            move, own, back, behind_of, input_weight, gbt, act, red_s, vec1
        )
    frames_gradient = frames_end(gx, *dx)

    grads = [inp, out, exp, red, vec]
    masters, firsts, seconds = (list(states[i : i + 5]) for i in (0, 5, 10))
    for group in (masters, firsts, seconds):
        group[3] = group[3].T
    hidden = expand_weight.shape[1]
    wide, narrow = 2.0 * width**-0.5, 2.0 * hidden**-0.5
    norm, *made = adam_all(
        squares, frames_gradient, list(zip(masters, firsts, seconds)), grads,
        ((wide, 0.01), (wide, 0.01), (wide, 0.01), (narrow, 0.01), (0.5, 0.0)),
        (False, True, False, False, False),
    )
    made[12:16] = [m.T for m in made[12:16]]
    return (layer, frames_gradient, norm.reshape(()), *made)


def solution(mesh):
    tokens, whole = P(("dp", "seq"), None), P()
    state = (P("dp", "seq"), *(P("seq", "dp"),) * 4)
    outs = tuple(s for s in state for _ in range(4))
    return jax.shard_map(
        local,
        mesh=mesh,
        in_specs=(tokens, tokens, P("dp", None), *(whole,) * 5, *state * 3),
        out_specs=(tokens, tokens, whole, *outs),
        check_vma=False,
    )
```

```python
import functools

import jax
import jax.numpy as jnp
from jax import lax
from jax.experimental import pallas as pl
from jax.experimental.pallas import tpu as pltpu
from jax.sharding import PartitionSpec as P

HD = 64
STEP = 10
LANES = 128
NORM_EPS = 1e-05
MASK = -float(2**30)
BF = jnp.bfloat16
F32 = jnp.float32
AXES = ("dp", "seq")

PLACES = (
    {
        0: ((0, 0, 0), (1, 1, 1), (2, 2, 2)),
        2: ((0, 0, 1), (1, 1, 2), (2, 3, 0)),
        3: ((0, 0, 2), (1, 2, 0), (2, 3, 1)),
        5: ((0, 1, 0), (1, 2, 1), (2, 3, 2)),
    },
    {
        1: ((0, 0, 0), (1, 1, 1), (2, 2, 1), (2, 3, 0)),
        4: ((0, 0, 1), (0, 1, 0), (1, 2, 0), (2, 3, 1)),
    },
)
WIDTHS = (3 * LANES, 2 * LANES)
CALLS = ((0, 2), (3, 5), (1, 4))


def params(mebibytes):
    return pltpu.CompilerParams(vmem_limit_bytes=mebibytes * 2**20)


def cost(microseconds):
    return pl.CostEstimate(flops=int(microseconds * 4.4e9), bytes_accessed=0, transcendentals=0)


def in_hbm(array):
    return pltpu.with_memory_space_constraint(array, pltpu.HBM)


def dot(a, b):
    return lax.dot_general(a, b, (((1,), (0,)), ((), ())), preferred_element_type=F32)


def dot_t(a, b):
    return lax.dot_general(a, b, (((1,), (1,)), ((), ())), preferred_element_type=F32)


def attend_kernel(
    x0_ref, x1_ref, x2_ref, x3_ref, wq_ref, wk_ref, wv_ref, vec_ref, kmask_ref, qhot_ref,
    mixed_ref, e_ref, rinv_ref, q_ref, k_ref, v_ref, xt_ref, x_ref,
):
    rows = q_ref.shape[0]
    step = pl.program_id(0)
    wide = wq_ref.shape[1]
    pairs = wide // LANES

    @pl.when(step == 0)
    def _():
        for i, ref in enumerate((x0_ref, x1_ref, x2_ref, x3_ref)):
            x_ref[i * rows : (i + 1) * rows, :] = ref[...]

    xt_ref[...] = x_ref[:, pl.ds(pl.multiple_of(step * wide, LANES), wide)].T
    k = dot(x_ref[...], wk_ref[...]).astype(BF)
    v = (dot(x_ref[...], wv_ref[...]) + vec_ref[1:2, :]).astype(BF)
    q = (dot(x_ref[:rows, :], wq_ref[...]) + vec_ref[0:1, :]).astype(BF)
    q = q * jnp.asarray(HD**-0.5, BF)
    q_ref[...] = q
    k_ref[...] = k
    v_ref[...] = v
    low = lax.broadcasted_iota(jnp.int32, (rows, LANES), 1) < HD
    part = lambda a, p: a[:, p * LANES : (p + 1) * LANES]
    keys = [jnp.concatenate([part(k, p), kmask_ref[...]], axis=1) for p in range(pairs)]
    values = [jnp.concatenate([part(v, p), jnp.ones((v.shape[0], LANES), BF)], axis=1) for p in range(pairs)]

    def score(head):
        qh = part(q, head // 2)
        qh = jnp.where(low if head % 2 == 0 else jnp.logical_not(low), qh, jnp.zeros_like(qh))
        return dot_t(jnp.concatenate([qh, qhot_ref[...]], axis=1), keys[head // 2])

    following = score(0)
    done = []
    for head in range(2 * pairs):
        scores = following
        if head + 1 < 2 * pairs:
            following = score(head + 1)
        e = jnp.exp(scores - jnp.max(scores, axis=1, keepdims=True)).astype(BF)
        e_ref[head] = e
        both = dot(e, values[head // 2])
        done.append((both[:, :LANES], 1.0 / both[:, LANES:]))
        if head % 2 == 1:
            (out0, rinv0), (out1, rinv1) = done[-2:]
            span = slice(head // 2 * LANES, (head // 2 + 1) * LANES)
            rinv = jnp.where(low, rinv0, rinv1)
            rinv_ref[:, span] = rinv
            mixed_ref[:, span] = (jnp.where(low, out0, out1) * rinv).astype(BF)


def attend(blocks, input_weight, vectors, kmask, qhot):
    rows, width = blocks[0].shape
    slab = rows * len(blocks)
    wide = 2 * LANES
    steps = width // wide
    weight = in_hbm(input_weight)
    full = lambda a: pl.BlockSpec(a.shape, lambda p: (0,) * a.ndim)
    cols = lambda r, off=0: pl.BlockSpec((r, wide), lambda p: (0, p + off))
    return pl.pallas_call(
        attend_kernel,
        grid=(steps,),
        in_specs=[
            *map(full, blocks), cols(width), cols(width, steps), cols(width, 2 * steps),
            cols(vectors.shape[0]), full(kmask), full(qhot),
        ],
        out_specs=[
            cols(rows), pl.BlockSpec((wide // HD, rows, slab), lambda p: (p, 0, 0)), cols(rows), cols(rows),
            cols(slab), cols(slab), pl.BlockSpec((wide, slab), lambda p: (p, 0)),
        ],
        out_shape=[
            jax.ShapeDtypeStruct((rows, width), BF),
            pltpu.HBM((width // HD, rows, slab), BF),
            pltpu.HBM((rows, width), F32),
            pltpu.HBM((rows, width), BF),
            pltpu.HBM((slab, width), BF),
            pltpu.HBM((slab, width), BF),
            pltpu.HBM((width, slab), BF),
        ],
        scratch_shapes=[pltpu.VMEM((slab, width), BF)],
        compiler_params=params(40), cost_estimate=cost(20),
        name="attend",
    )(in_hbm(blocks[0]), *blocks[1:], weight, weight, weight, vectors, kmask, qhot)


def spot(d, own_d):
    rel = d ^ own_d
    return (rel & 1) * 4 + (rel >> 1)


def turn(j):
    return jnp.where(j < 2, 2 * j + 1, 2 * (j - 2))


def store_rows(ref, block, own_d):
    piece = block.shape[0] // 8
    for d in range(8):
        ref[0, spot(d, own_d)] = block[d * piece : (d + 1) * piece, :]


def reduce_kernel(own_ref, gbt_ref, act_ref, rk_ref):
    store_rows(rk_ref, dot(gbt_ref[...], act_ref[0]).astype(BF), own_ref[1])


def reduce_kept(own, gbt, act):
    width, rows = gbt.shape
    chunks, _, cut = act.shape
    return pl.pallas_call(
        reduce_kernel,
        grid_spec=pltpu.PrefetchScalarGridSpec(
            num_scalar_prefetch=1,
            grid=(2,),
            in_specs=[
                pl.BlockSpec((width, rows), lambda j, own: (0, 0)),
                pl.BlockSpec((1, rows, cut), lambda j, own: (j + 2, 0, 0)),
            ],
            out_specs=pl.BlockSpec((1, 8, width // 8, cut), lambda j, own: (j, 0, 0, 0)),
        ),
        out_shape=jax.ShapeDtypeStruct((2, 8, width // 8, cut), BF),
        compiler_params=params(12), cost_estimate=cost(5),
        name="reduce_kept",
    )(own, gbt, act)


def ahead_kernel(
    own_ref, mixed_ref, x_ref, cot_ref, qhot_ref, wo_ref, we_ref, wr_ref, vec_ref,
    layer_ref, act_ref, slope_ref, norm1_ref, inv1_ref, hlt_ref, mt_ref, gs_ref, gb_ref, gbt, rs_ref, vg_ref,
    act, hid, hl, acc,
):
    step = pl.program_id(0)
    own_s, own_d = own_ref[0], own_ref[1]
    rows, width = x_ref.shape
    chunks = act.shape[0]
    j = lax.rem(step, chunks)
    shard = turn(j) ^ own_s
    row = lambda i: vec_ref[i : i + 1, :]

    @pl.when(step == 0)
    def _():
        z = x_ref[...].astype(F32) + dot(mixed_ref[...], wo_ref[...]) + row(2)
        center = z - jnp.mean(z, axis=1, keepdims=True)
        inverse = lax.rsqrt(jnp.mean(center * center, axis=1, keepdims=True) + NORM_EPS)
        normed = center * inverse
        hidden = normed * row(3) + row(4)
        hid[...] = hidden
        norm1_ref[...] = normed
        inv1_ref[...] = jnp.broadcast_to(inverse, inv1_ref.shape)
        low = hidden.astype(BF)
        hl[...] = low
        hlt_ref[...] = low.T
        mt_ref[...] = mixed_ref[...].T
        vg_ref[...] = jnp.zeros_like(vg_ref)

    @pl.when(step < chunks)
    def _():
        pre = dot(hl[...], we_ref[...]) + vec_ref[pl.ds(8 + shard, 1), :]
        cdf = 0.5 * (1.0 + lax.erf(pre * 0.7071067811865476))
        density = jnp.exp(-0.5 * pre * pre) * 0.3989422804014327
        low = (pre * cdf).astype(BF)
        act[j] = low
        act_ref[0] = low
        slope_ref[0] = cdf + pre * density
        part = dot(low, wr_ref[...])

        @pl.when(step == 0)
        def _():
            acc[...] = part

        @pl.when(step > 0)
        def _():
            acc[...] += part

    @pl.when(step == chunks - 1)
    def _():
        z = hid[...] + acc[...] + row(5)
        center = z - jnp.mean(z, axis=1, keepdims=True)
        inverse = lax.rsqrt(jnp.mean(center * center, axis=1, keepdims=True) + NORM_EPS)
        normed = center * inverse
        valid = 1.0 - qhot_ref[:, 3:4].astype(F32)
        layer_ref[...] = ((normed * row(6) + row(7)) * valid).astype(BF)
        gy = cot_ref[...].astype(F32) * valid
        vg_ref[6:7, :] = jnp.sum(gy * normed, axis=0, keepdims=True)
        vg_ref[7:8, :] = jnp.sum(gy, axis=0, keepdims=True)
        e = gy * row(6)
        grad = e - jnp.mean(e, axis=1, keepdims=True)
        grad = (grad - normed * jnp.mean(e * normed, axis=1, keepdims=True)) * inverse
        low = grad.astype(BF)
        vg_ref[5:6, :] = jnp.sum(low.astype(F32), axis=0, keepdims=True)
        gb_ref[...] = low
        gbt[...] = low.T
        gs_ref[...] = grad

    @pl.when(step >= chunks)
    def _():
        store_rows(rs_ref, dot(gbt[...], act[j]).astype(BF), own_d)


def ahead(own, mixed, frames, cotangent, qhot, output_weight, expand_weight, reduce_weight, vectors):
    rows, width = frames.shape
    hidden = expand_weight.shape[1]
    chunks = 4
    cut = hidden // chunks
    piece = width // 8
    first = lambda s: jnp.minimum(s, chunks - 1)
    shard_of = lambda s, own: turn(first(s)) ^ own[0]
    full = lambda shape: pl.BlockSpec(shape, lambda s, own: (0,) * len(shape))
    chunk = pl.BlockSpec((1, rows, cut), lambda s, own: (first(s), 0, 0))
    return pl.pallas_call(
        ahead_kernel,
        grid_spec=pltpu.PrefetchScalarGridSpec(
            num_scalar_prefetch=1,
            grid=(chunks + 2,),
            in_specs=[
                full(mixed.shape), full(frames.shape), full(cotangent.shape), full(qhot.shape),
                full(output_weight.shape),
                pl.BlockSpec((width, cut), lambda s, own: (0, shard_of(s, own))),
                pl.BlockSpec((cut, width), lambda s, own: (shard_of(s, own), 0)),
                full(vectors.shape),
            ],
            out_specs=[
                full((rows, width)), chunk, chunk, full((rows, width)), full((rows, LANES)),
                full((width, rows)), full((width, rows)), full((rows, width)), full((rows, width)), full((width, rows)),
                pl.BlockSpec((1, 8, piece, cut), lambda s, own: (jnp.maximum(s - chunks, 0), 0, 0, 0)),
                full((16, width)),
            ],
            scratch_shapes=[
                pltpu.VMEM((chunks, rows, cut), BF),
                pltpu.VMEM((rows, width), F32),
                pltpu.VMEM((rows, width), BF),
                pltpu.VMEM((rows, width), F32),
            ],
        ),
        out_shape=[
            jax.ShapeDtypeStruct((rows, width), BF),
            jax.ShapeDtypeStruct((chunks, rows, cut), BF),
            jax.ShapeDtypeStruct((chunks, rows, cut), F32),
            jax.ShapeDtypeStruct((rows, width), F32),
            jax.ShapeDtypeStruct((rows, LANES), F32),
            jax.ShapeDtypeStruct((width, rows), BF),
            jax.ShapeDtypeStruct((width, rows), BF),
            jax.ShapeDtypeStruct((rows, width), F32),
            jax.ShapeDtypeStruct((rows, width), BF),
            jax.ShapeDtypeStruct((width, rows), BF),
            jax.ShapeDtypeStruct((2, 8, piece, cut), BF),
            jax.ShapeDtypeStruct((16, width), F32),
        ],
        compiler_params=params(22), cost_estimate=cost(20),
        name="ahead",
    )(own, mixed, frames, cotangent, qhot, output_weight, expand_weight, reduce_weight, vectors)


def behind_kernel(
    own_ref, slope_ref, gb_ref, gs_ref, norm1_ref, inv1_ref, hlt_ref, mt_ref, wo_ref, we_ref, wr_ref, vec_ref, _,
    gf_ref, gm_ref, es_ref, ek_ref, vg_ref,
    acc, tmp,
):
    j = pl.program_id(0)
    own_s, own_d = own_ref[0], own_ref[1]
    rows, width = gb_ref.shape
    shard = turn(j) ^ own_s
    row = lambda i: vec_ref[i : i + 1, :]
    piece, fourth = width // 8, width // 4

    @pl.when(j == 0)
    def _():
        acc[...] = gs_ref[...]
        vg_ref[...] = jnp.zeros_like(vg_ref)

    grad_act = dot_t(gb_ref[...], wr_ref[...])
    low = (grad_act * slope_ref[0]).astype(BF)
    vg_ref[pl.ds(8 + shard, 1), :] = jnp.sum(low.astype(F32), axis=0, keepdims=True)
    acc[...] += dot_t(low, we_ref[...])
    grad_e = dot(hlt_ref[...], low).astype(BF)
    tmp[...] = grad_e.reshape(tmp.shape)
    half = grad_e.shape[1] // 2
    rz = shard ^ (own_d >> 1)
    for part, ref in ((1, es_ref), (0, ek_ref)):
        for ry in range(2):
            for t in range(2):
                block = tmp[own_s ^ (2 * ry + part), :, t * half : (t + 1) * half]
                ref[ry, t ^ (own_d & 1), rz, :fourth, :] = block

    @pl.when(j == pl.num_programs(0) - 1)
    def _():
        gy = acc[...]
        normed = norm1_ref[...]
        vg_ref[3:4, :] = jnp.sum(gy * normed, axis=0, keepdims=True)
        vg_ref[4:5, :] = jnp.sum(gy, axis=0, keepdims=True)
        e = gy * row(3)
        grad = e - jnp.mean(e, axis=1, keepdims=True)
        grad = (grad - normed * jnp.mean(e * normed, axis=1, keepdims=True)) * inv1_ref[:, :1]
        gf_ref[...] = grad
        low = grad.astype(BF)
        vg_ref[2:3, :] = jnp.sum(low.astype(F32), axis=0, keepdims=True)
        gm_ref[...] = dot_t(low, wo_ref[...]).astype(BF)
        gat = low.T
        for part, ref in ((1, es_ref), (0, ek_ref)):
            for ry in range(2):
                start = pl.multiple_of((own_s ^ (2 * ry + part)) * fourth, fourth)
                out = dot_t(gat, mt_ref[pl.ds(start, fourth), :]).astype(BF)
                for d in range(8):
                    block = out[d * piece : (d + 1) * piece, :]
                    block = jnp.concatenate([block[: piece // 2], block[piece // 2 :]], axis=1)
                    ref[ry, (d & 1) ^ (own_d & 1), (d >> 1) ^ (own_d >> 1), fourth:, :] = block


def behind(own, slope, gb, gs, norm1, inv1, hlt, mt, output_weight, expand_weight, reduce_weight, vectors, after):
    rows, width = gb.shape
    hidden = expand_weight.shape[1]
    chunks = 4
    cut = hidden // chunks
    fourth, eighth = width // 4, hidden // 8
    shard_of = lambda s, own: turn(s) ^ own[0]
    full = lambda shape: pl.BlockSpec(shape, lambda s, own: (0,) * len(shape))
    spread = (2, 2, 4, fourth + width // 16, eighth)
    return pl.pallas_call(
        behind_kernel,
        grid_spec=pltpu.PrefetchScalarGridSpec(
            num_scalar_prefetch=1,
            grid=(chunks,),
            in_specs=[
                pl.BlockSpec((1, rows, cut), lambda s, own: (s, 0, 0)),
                full(gb.shape), full(gs.shape), full(norm1.shape), full(inv1.shape), full(hlt.shape), full(mt.shape),
                full(output_weight.shape),
                pl.BlockSpec((width, cut), lambda s, own: (0, shard_of(s, own))),
                pl.BlockSpec((cut, width), lambda s, own: (shard_of(s, own), 0)),
                full(vectors.shape), pl.BlockSpec(memory_space=pl.ANY),
            ],
            out_specs=[full((rows, width)), full((rows, width)), full(spread), full(spread), full((16, width))],
            scratch_shapes=[pltpu.VMEM((rows, width), F32), pltpu.VMEM((4, fourth, cut), BF)],
        ),
        out_shape=[
            jax.ShapeDtypeStruct((rows, width), F32),
            jax.ShapeDtypeStruct((rows, width), BF),
            jax.ShapeDtypeStruct(spread, BF),
            jax.ShapeDtypeStruct(spread, BF),
            jax.ShapeDtypeStruct((16, width), F32),
        ],
        compiler_params=params(20), cost_estimate=cost(18),
        name="behind",
    )(own, slope, gb, gs, norm1, inv1, hlt, mt, output_weight, expand_weight, reduce_weight, vectors, after)


def back_kernel(group, pairs, first, last, own_ref, e_ref, q_ref, k_ref, v_ref, gm_ref, mixed_ref, rinv_ref, xt_ref,
                *rest):
    rest = list(rest[1:])
    gw_in_ref = None if first else rest.pop(0)
    vec_in = [rest.pop(0) for _ in range(4)] if group == 1 else []
    dq_ref, dkv_ref, vb_ref = rest[:3]
    rest = rest[3:]
    if last:
        gs_ref, gk_ref, gw, *vecs = rest
    else:
        (gw,) = rest
    i = pl.program_id(0)
    own_s, own_d = own_ref[0], own_ref[1]
    rows = q_ref.shape[0]
    q, k, v = q_ref[...], k_ref[...], v_ref[...]
    gm = gm_ref[...].astype(F32) * rinv_ref[...]
    both = gm * mixed_ref[...].astype(F32)
    gm_low = gm.astype(BF)
    gm_t = gm_low.T
    q_t = q.T
    low = lax.broadcasted_iota(jnp.int32, (rows, LANES), 1) < HD
    dqs, dks, dvs = [], [], []
    for head in range(2):
        own = low if head == 0 else jnp.logical_not(low)
        span = slice(head * HD, (head + 1) * HD)
        e = e_ref[head]
        inner = jnp.sum(jnp.where(own, both, 0.0), axis=1, keepdims=True)
        grad_e = dot_t(jnp.where(own, gm_low, jnp.zeros_like(gm_low)), v)
        ds = (e.astype(F32) * (grad_e - inner)).astype(BF)
        dqs.append(dot(ds, k))
        dks.append(dot(q_t[span, :], ds))
        dvs.append(dot(gm_t[span, :], e))
    dq = (jnp.where(low, dqs[0], dqs[1]) * HD**-0.5).astype(BF)
    dkv = jnp.concatenate([*dks, *dvs], axis=0).astype(BF)
    dq_ref[...] = dq
    dkv_ref[...] = dkv
    ones = jnp.ones((8, dkv.shape[1]), BF)
    bias = jnp.concatenate(
        [jnp.sum(dq.astype(F32), axis=0, keepdims=True), dot_t(ones, dkv[LANES:, :])[0:1, :]], axis=0
    )
    vb_ref[0:2, :] = bias

    if group == 1:

        @pl.when(i == 0)
        def _():
            vecs[0][...] = vec_in[0][...] + vec_in[1][...]
            for call, ref in zip(CALLS, vec_in[2:]):
                for n, p in enumerate(call):
                    vecs[0][0:2, p * LANES : (p + 1) * LANES] = ref[0:2, n * LANES : (n + 1) * LANES]

    if not first:

        @pl.when(i == 0)
        def _():
            gw[...] = gw_in_ref[...]

    grad_q = dot(xt_ref[:, :rows], dq).astype(BF)
    grad_kv = dot_t(xt_ref[...], dkv).astype(BF)
    piece = grad_q.shape[0] // 8
    blocks = [b.reshape(8, piece, LANES) for b in (grad_q, grad_kv[:, :LANES], grad_kv[:, LANES:])]
    for n, pair in enumerate(pairs):

        @pl.when(i == n)
        def _():
            for which, shard, place in PLACES[group][pair]:
                gw[shard, :, :piece, place * LANES : (place + 1) * LANES] = blocks[which]
            if group == 1:
                vecs[0][0:2, pair * LANES : (pair + 1) * LANES] = bias

    if last:

        @pl.when(i == len(pairs) - 1)
        def _():
            if group == 1:
                vec, tall = vecs[0][...], vecs[0].shape[1]
                for d in range(8):
                    turned = pltpu.roll(vec, (tall - piece * d) % tall, axis=1)[:, : gw.shape[3]]
                    for shard in range(4):
                        block = pltpu.roll(turned, (16 - 3 * shard) % 16, axis=0) if shard else turned
                        gw[shard, d, piece:, :] = block.astype(BF)
            for ref, part in ((gs_ref, 1), (gk_ref, 0)):
                for ry in range(2):
                    for d in range(8):
                        ref[ry, spot(d, own_d)] = gw[own_s ^ (2 * ry + part), d]


def attend_back(group, pairs, own, e, q, k, v, grad_mixed, mixed, rinv, x_t, after, gw=None, last=True, vecs=()):
    first = gw is None
    rows, width = q.shape
    slab = k.shape[0]
    piece = width // 8
    span = WIDTHS[group]
    own = jnp.concatenate([own, jnp.array(pairs, jnp.int32)])
    full = lambda shape: pl.BlockSpec(shape, lambda i, own: (0,) * len(shape))
    cols = lambda r: pl.BlockSpec((r, LANES), lambda i, own: (0, own[2 + i]))
    inputs = [in_hbm(e), q, k, v, grad_mixed, mixed, rinv, x_t, after]
    in_specs = [
        pl.BlockSpec((2, rows, slab), lambda i, own: (own[2 + i], 0, 0)),
        cols(rows), cols(slab), cols(slab), cols(rows), cols(rows), cols(rows), full(x_t.shape),
        pl.BlockSpec(memory_space=pl.ANY),
    ]
    out_shape = [
        jax.ShapeDtypeStruct((rows, len(pairs) * LANES), BF),
        jax.ShapeDtypeStruct((len(pairs) * 2 * LANES, slab), BF),
        jax.ShapeDtypeStruct((8, len(pairs) * LANES), F32),
    ]
    out_specs = [
        pl.BlockSpec((rows, LANES), lambda i, own: (0, i)),
        pl.BlockSpec((2 * LANES, slab), lambda i, own: (i, 0)),
        pl.BlockSpec((8, LANES), lambda i, own: (0, i)),
    ]
    scratch = []
    whole = (4, 8, piece + (16 if vecs else 0), span)
    if not first:
        inputs.append(gw)
        in_specs.append(full(whole))
    inputs += vecs
    in_specs += [full(a.shape) for a in vecs]
    if last:
        out_shape += [jax.ShapeDtypeStruct((2, *whole[1:]), BF)] * 2
        out_specs += [full((2, *whole[1:]))] * 2
        scratch.append(pltpu.VMEM(whole, BF))
        if vecs:
            scratch.append(pltpu.VMEM((16, width), F32))
    else:
        out_shape.append(jax.ShapeDtypeStruct(whole, BF))
        out_specs.append(full(whole))
    return pl.pallas_call(
        functools.partial(back_kernel, group, pairs, first, last),
        grid_spec=pltpu.PrefetchScalarGridSpec(
            num_scalar_prefetch=1, grid=(len(pairs),), in_specs=in_specs, out_specs=out_specs, scratch_shapes=scratch
        ),
        out_shape=out_shape,
        compiler_params=params(20), cost_estimate=cost(12),
        name="attend_back",
    )(own, *inputs)


def frames_kernel(pairs, last, w_ref, gx_in_ref, after_ref, *refs):
    n = len(pairs)
    dqs, dkvs = refs[:n], refs[n : 2 * n]
    refs = list(refs[2 * n :])
    dx_ref = refs.pop(0) if last else None
    gx_ref, *outs, wkv = refs
    j = pl.program_id(0)
    width = gx_ref.shape[1]
    flat = [p for call in pairs for p in call]

    @pl.when(j == 0)
    def _():
        for i, p in enumerate(flat):
            for t in range(2):
                start = (1 + t) * width + p * LANES
                wkv[:, (2 * i + t) * LANES : (2 * i + t + 1) * LANES] = w_ref[:, start : start + LANES]
        wq = jnp.concatenate([w_ref[:, p * LANES : (p + 1) * LANES] for p in flat], axis=1)
        dq = jnp.concatenate([r[...] for r in dqs], axis=1)
        gx_ref[...] = gx_in_ref[...] + dot_t(dq, wq)

    made = dot(wkv[...], jnp.concatenate([r[...] for r in dkvs], axis=0))
    if not last:
        outs[0][0] = made
        return
    made = made + dx_ref[0]

    @pl.when(j < 2)
    def _():
        outs[0][0] = made.astype(BF)

    @pl.when(j >= 2)
    def _():
        outs[1][0] = made


def frames_back(input_weight, gx, after, pairs, dqs, dkvs, dx=None):
    rows, width = gx.shape
    last = dx is not None
    count = 2 * sum(map(len, pairs))
    full = lambda a: pl.BlockSpec(a.shape, lambda j: (0,) * a.ndim)
    column = lambda a: pl.BlockSpec((a.shape[0], rows), lambda j: (0, lax.rem(j + 2, 4)))
    block = lambda pick: pl.BlockSpec((1, width, rows), lambda j: (pick(j), 0, 0))
    if last:
        out_specs = [block(lambda j: jnp.minimum(j, 1)), block(lambda j: jnp.maximum(j - 2, 0))]
        out_shape = [jax.ShapeDtypeStruct((2, width, rows), BF), jax.ShapeDtypeStruct((2, width, rows), F32)]
    else:
        out_specs = [block(lambda j: j)]
        out_shape = [jax.ShapeDtypeStruct((4, width, rows), F32)]
    return pl.pallas_call(
        functools.partial(frames_kernel, pairs, last),
        grid=(4,),
        in_specs=[
            full(input_weight), full(gx), pl.BlockSpec(memory_space=pl.ANY), *map(full, dqs), *map(column, dkvs),
            *([block(lambda j: j)] if last else []),
        ],
        out_specs=[full(gx), *out_specs],
        out_shape=[jax.ShapeDtypeStruct((rows, width), F32), *out_shape],
        scratch_shapes=[pltpu.VMEM((width, count * LANES), BF)],
        compiler_params=params(16), cost_estimate=cost(4 if last else 8),
        name="frames_back",
    )(input_weight, gx, after, *dqs, *dkvs, *([dx] if last else []))


def frames_end_kernel(gx_ref, keep_ref, came_ref, out_ref, token_ref):
    token_ref[...] = jnp.zeros_like(token_ref)
    out_ref[...] = gx_ref[...] + (keep_ref[0] + came_ref[0].astype(F32)).T


def frames_end(gx, keep, came):
    rows, width = gx.shape
    across = pl.BlockSpec((rows, LANES), lambda p: (0, p))
    down = pl.BlockSpec((1, LANES, rows), lambda p: (0, p, 0))
    return pl.pallas_call(
        frames_end_kernel,
        grid=(width // LANES,), in_specs=[across, down, down],
        out_specs=[across, pl.BlockSpec((8, LANES), lambda p: (0, 0))],
        out_shape=[jax.ShapeDtypeStruct((rows, width), F32), jax.ShapeDtypeStruct((8, LANES), F32)], compiler_params=params(8), cost_estimate=cost(5), name="frames_end",
    )(gx, keep, came)


def gather_kernel(plan, *refs):
    start, out = 0, sum(n for n, _ in plan) + 1
    for n, outs in plan:
        ins = refs[start : start + n]
        start += n
        for parts in outs:
            for i, part in enumerate(parts):
                terms = [r[part].astype(F32) for r in ins]
                while len(terms) > 1:
                    terms = [terms[t] + terms[t + 1] for t in range(0, len(terms), 2)]
                refs[out][i] = terms[0].astype(refs[out].dtype)
            out += 1


def gather(sums, after, steps=2):
    inputs, in_specs, out_shape, out_specs, plan = [], [], [], [], []
    for arrays, count, outs in sums:
        cols = arrays[0].shape[-1]
        rows = arrays[0].size // cols // count
        plan.append((len(arrays), tuple(parts for parts, _ in outs)))
        for a in arrays:
            inputs.append(a.reshape(count, rows, cols))
            in_specs.append(pl.BlockSpec((count, rows // steps, cols), lambda i: (0, i, 0)))
        for parts, kind in outs:
            out_shape.append(jax.ShapeDtypeStruct((len(parts), rows, cols), kind))
            out_specs.append(pl.BlockSpec((len(parts), rows // steps, cols), lambda i: (0, i, 0)))
    outs = pl.pallas_call(
        functools.partial(gather_kernel, plan),
        grid=(steps,), in_specs=[*in_specs, pl.BlockSpec(memory_space=pl.ANY)], out_specs=out_specs,
        out_shape=out_shape, compiler_params=params(14), cost_estimate=cost(3), name="gather",
    )(*inputs, after)
    made = []
    for _, parts in plan:
        made.append(outs[: len(parts)])
        outs = outs[len(parts) :]
    return made


def finish_kernel(counts, own_ref, *refs):
    sums = []
    for n in counts:
        parts = [r[0].astype(F32) for r in refs[:n]]
        refs = refs[n:]
        while len(parts) > 1:
            parts = [parts[t] + parts[t + 1] for t in range(0, len(parts), 2)]
        sums.append(parts[0])
    inp_ref, out_ref, exp_ref, red_ref, vec_ref, sq_ref = refs[1:]
    red, exp, in1, in2 = sums
    rows = in1.shape[0]
    vec = in2[rows : rows + vec_ref.shape[0], : vec_ref.shape[1]]
    vec_ref[...] = vec
    in2 = in2[:rows]
    even = jnp.concatenate([in1[:, :128], in2[:, :128], in1[:, 128:], in2[:, 128:]], axis=1)
    odd = jnp.concatenate([in2[:, :128], in1[:, :256], in2[:, 128:], in1[:, 256:]], axis=1)
    odd = pltpu.roll(odd, odd.shape[1] - HD, axis=1)
    inp = jnp.where((own_ref[0] & 1) == 1, odd, even)[:, : inp_ref.shape[1]]
    tall = exp_ref.shape[0]
    out = exp[tall:, :]
    half = out_ref.shape[1]
    out = jnp.concatenate([out[:, :half], pltpu.roll(out, half, axis=1)[:, :half]], axis=0)
    inp_ref[...] = inp
    out_ref[...] = out
    exp_ref[...] = exp[:tall, :]
    red_ref[...] = red
    squares = jnp.zeros((1, 1), F32)
    for g in (inp, out, exp[:tall, :], red, vec):
        squares = squares + jnp.sum(jnp.sum(g * g, axis=0, keepdims=True), axis=1, keepdims=True)
    sq_ref[...] = jnp.broadcast_to(squares, sq_ref.shape)


def finish(own, red, exp, in1, in2, after):
    piece = in1[0].shape[1]
    tall = exp[0].shape[1] - piece // 2
    vmem = pl.BlockSpec(memory_space=pltpu.VMEM)
    inputs = [*red, *exp, *in1, *in2]
    return pl.pallas_call(
        functools.partial(finish_kernel, tuple(map(len, (red, exp, in1, in2)))),
        in_specs=[
            pl.BlockSpec(memory_space=pltpu.SMEM), *[vmem] * len(inputs), pl.BlockSpec(memory_space=pl.ANY)
        ],
        out_specs=[vmem] * 6,
        out_shape=[
            jax.ShapeDtypeStruct((piece, 9 * HD), F32),
            jax.ShapeDtypeStruct((piece, 3 * HD), F32),
            jax.ShapeDtypeStruct((tall, exp[0].shape[2]), F32),
            jax.ShapeDtypeStruct(red[0].shape[1:], F32),
            jax.ShapeDtypeStruct((3, piece), F32),
            jax.ShapeDtypeStruct((8, LANES), F32),
        ],
        compiler_params=params(8), cost_estimate=cost(3), name="finish",
    )(own, *inputs, after)


def adam_step(master, moment_one, moment_two, gradient, step_rate, decay_weight):
    new_one = 0.9 * moment_one + 0.1 * gradient
    new_two = 0.999 * moment_two + 0.001 * gradient * gradient
    corrected_one = new_one / (1.0 - 0.9**STEP)
    corrected_two = new_two / (1.0 - 0.999**STEP)
    new_master = master - step_rate * (
        corrected_one / (jnp.sqrt(corrected_two) + 1e-08) + decay_weight * master
    )
    return (new_one, new_two, new_master, new_master.astype(BF))


def adam_kernel(rates, turned, squares_ref, _, *refs):
    n = len(rates)
    ins, outs = refs[: 4 * n], refs[4 * n :]
    norm = jnp.sqrt(squares_ref[0:1, 0:1])
    outs[0][...] = norm
    factor = 1.0 / jnp.maximum(norm, 1.0)
    for a in range(n):
        master, one, two, grad = (r[...] for r in ins[4 * a : 4 * a + 4])
        if turned[a]:
            grad = grad.T
        made = adam_step(master, one, two, grad * factor, rates[a][0], rates[a][1])
        for b in range(4):
            outs[1 + 4 * a + b][...] = made[b]


def adam_all(squares, after, states, grads, rates, turned):
    inputs, out_shape = [squares, after], [jax.ShapeDtypeStruct((1, 1), F32)]
    for state, grad in zip(states, grads):
        inputs += [*state, grad]
        shape = state[0].shape
        out_shape += [jax.ShapeDtypeStruct(shape, F32)] * 3 + [jax.ShapeDtypeStruct(shape, BF)]
    vmem = pl.BlockSpec(memory_space=pltpu.VMEM)
    return pl.pallas_call(
        functools.partial(adam_kernel, rates, turned),
        in_specs=[vmem, pl.BlockSpec(memory_space=pl.ANY), *[vmem] * (len(inputs) - 2)], out_specs=[vmem] * len(out_shape), out_shape=out_shape,
        compiler_params=params(16), cost_estimate=cost(5), name="adam",
    )(*inputs)


def mover(dp, seq):
    def move(value, bits_d, bits_s):
        pairs = [(d * seq + s, (d ^ bits_d) * seq + (s ^ bits_s)) for d in range(dp) for s in range(seq)]
        return lax.ppermute(value, AXES, pairs)

    return move


def tree_sum(move, value):
    value = value + move(value, 0, 1)
    value = (value + move(value, 0, 2)) + (move(value, 1, 0) + move(value, 1, 2))
    return (value + move(value, 2, 0)) + (move(value, 4, 0) + move(value, 6, 0))


def spread_out(move, parts):
    return [parts[0], *(move(parts[b], 2 * b, 0) for b in (1, 2, 3))]


def plane(move, parts):
    return [parts[0], move(parts[1], 1, 0), move(parts[2], 0, 2), move(parts[3], 1, 2)]


def scatter_plain(parts, dim):
    part = lax.psum_scatter(parts, "seq", scatter_dimension=0, tiled=True)[0].astype(F32)
    return lax.psum_scatter(part, "dp", scatter_dimension=dim, tiled=True)


def in_order(kept, sent):
    parts = jnp.stack([kept, sent], axis=1)
    rows, cols = parts.shape[-2:]
    return parts.reshape(4, 2, 4, rows, cols).swapaxes(1, 2).reshape(4, 8 * rows, cols)


HALVES = tuple((parts, BF) for parts in ((0, 2), (4, 6), (1, 5), (3, 7)))
PAIR = (((0,), BF), ((1,), BF))
QUARTERS = tuple(((part,), BF) for part in range(4))
ONE = (((0,), BF),)
Z_HALVES = (((0, 1), BF), ((2, 3), BF))


def both_ways(move, cut):
    y_keep, y_send, x_keep, x_send = cut
    return (y_keep, move(y_send, 0, 2)), (x_keep, move(x_send, 1, 0))


def turned_ways(move, y_cut, x_cut):
    return (y_cut[0], move(y_cut[1], 1, 0)), (x_cut[0], move(x_cut[1], 0, 2))


def reduce_fast(move, own, back, behind_of, input_weight, gbt, act, red_s, vec1):
    red_c = move(red_s, 0, 1)
    red_k = reduce_kept(own, gbt, act)
    (red,) = gather([((red_k, red_c), 8, HALVES)], red_k)
    red_y, red_x = both_ways(move, red)

    gf, grad_mixed, exp_s, exp_k, vec2 = behind_of(red[0])
    exp_c = move(exp_s, 0, 1)
    red_y, red_x = gather([(red_y, 2, PAIR), (red_x, 2, PAIR)], vec2)
    red_y, red_x = turned_ways(move, red_y, red_x)

    dq0, dkv0, vb0, gw = back(0, CALLS[0], grad_mixed, red_y[0], last=False)
    (red_k,), (red_s,), exp = gather([(red_y, 1, ONE), (red_x, 1, ONE), ((exp_k, exp_c), 8, HALVES)], vb0)
    red = red_k, move(red_s, 4, 0)
    exp_y, exp_x = both_ways(move, exp)

    dq1, dkv1, vb1, in_s1, in_k1 = back(0, CALLS[1], grad_mixed, red_k, gw=gw)
    in_c1 = move(in_s1, 0, 1)
    (red_k, red_s), exp_y, exp_x = gather([(red, 2, PAIR), (exp_y, 2, PAIR), (exp_x, 2, PAIR)], vb1)
    red = red_k, move(red_s, 2, 0)
    exp_y, exp_x = turned_ways(move, exp_y, exp_x)

    gx, dx = frames_back(input_weight, gf, red_k, CALLS[:2], (dq0, dq1), (dkv0, dkv1))
    (exp_k,), (exp_s,), in1 = gather([(exp_y, 1, ONE), (exp_x, 1, ONE), ((in_k1, in_c1), 4, QUARTERS)], gx)
    exp = exp_k, move(exp_s, 4, 0)
    in1 = plane(move, in1)

    dq2, dkv2, vb2, in_s2, in_k2 = back(1, CALLS[2], grad_mixed, exp_k, vecs=(vec1, vec2, vb0, vb1))
    in_c2 = move(in_s2, 0, 1)
    (exp_k, exp_s), (in1_k, in1_s) = gather([(exp, 2, PAIR), (in1, 4, Z_HALVES)], vb2, 1)
    in1 = in1_k, move(in1_s, 4, 0)
    (in2,) = gather([((in_k2, in_c2), 4, QUARTERS)], exp_k, 1)
    in2 = plane(move, in2)

    gx, dx_s, dx_k = frames_back(input_weight, gx, in2[0], CALLS[2:], (dq2,), (dkv2,), dx)
    dx_c = move(dx_s, 0, 1)
    in2, (in1_k, in1_s) = gather([(in2, 4, QUARTERS), (in1, 2, PAIR)], gx, 1)
    in2 = spread_out(move, in2)
    in1 = in1_k, move(in1_s, 2, 0)
    exp = exp_k, move(exp_s, 2, 0)
    ((dx_k, dx_s),) = gather([((dx_k, dx_c), 2, (((0,), F32), ((1,), BF)))], in1_k)
    return red, exp, in1, in2, gx, (dx_k, move(dx_s, 0, 2))


def reduce_plain(move, own, back, behind_of, input_weight, gbt, act, red_s, vec1):
    red_k = reduce_kept(own, gbt, act)
    gf, grad_mixed, exp_s, exp_k, vec2 = behind_of(red_k)
    dq0, dkv0, vb0, gw = back(0, CALLS[0], grad_mixed, vec2, last=False)
    dq1, dkv1, vb1, in_s1, in_k1 = back(0, CALLS[1], grad_mixed, vb0, gw=gw)
    dq2, dkv2, vb2, in_s2, in_k2 = back(1, CALLS[2], grad_mixed, vb1, vecs=(vec1, vec2, vb0, vb1))
    gx, dx = frames_back(input_weight, gf, vb2, CALLS[:2], (dq0, dq1), (dkv0, dkv1))
    gx, dx_s, dx_k = frames_back(input_weight, gx, vb2, CALLS[2:], (dq2,), (dkv2,), dx)
    ((dx_keep, dx_send),) = gather([((dx_k, move(dx_s, 0, 1)), 2, (((0,), F32), ((1,), BF)))], vb2)
    dx = dx_keep, move(dx_send, 0, 2)
    red = scatter_plain(in_order(red_k, red_s), 0)
    in1 = scatter_plain(in_order(in_k1, in_s1), 0)
    both = in_order(in_k2, in_s2)
    both = both.reshape(4, 8, -1, both.shape[-1])
    piece = in_k1.shape[2]
    in2 = scatter_plain(both[:, :, :piece].reshape(4, 8 * piece, -1), 0)
    vec = scatter_plain(both[:, :, piece : piece + 3, :piece].swapaxes(1, 2).reshape(4, 3, -1), 1)
    both = jnp.stack([exp_k, exp_s], axis=1).transpose(0, 1, 3, 2, 4, 5)
    tall, wide = both.shape[-2] - piece // 2, both.shape[-1]
    both = both.reshape(4, 8, -1, wide)
    exp = scatter_plain(both[:, :, :tall].swapaxes(1, 2).reshape(4, tall, 8 * wide), 1)
    out = both[:, :, tall:].reshape(4, 8, piece // 2, 2, wide // 2).swapaxes(2, 3)
    out = scatter_plain(out.reshape(4, 8 * piece, wide // 2), 0)
    even = jnp.concatenate([in1[:, :128], in2[:, :128], in1[:, 128:], in2[:, 128:192]], axis=1)
    odd = jnp.concatenate([in2[:, 64:128], in1[:, :256], in2[:, 128:], in1[:, 256:]], axis=1)
    inp = jnp.where(lax.axis_index("seq") % 2 == 1, odd, even)
    squares = sum(jnp.sum(g * g) for g in (inp, out, exp, red, vec))
    squares = lax.psum(jnp.full((8, LANES), squares, F32), AXES)
    return inp, out, exp, red, vec, squares, gx, dx


def local(
    frames, cotangent, lengths,
    input_weight, output_weight, expand_weight, reduce_weight, vector_copy,
    *states,
):
    rows, width = frames.shape
    seq, dp = lax.axis_size("seq"), lax.axis_size("dp")
    slab = rows * seq
    move = mover(dp, seq)
    own_s, own_d = lax.axis_index("seq"), lax.axis_index("dp")
    fast = dp == 8
    vectors = vector_copy.astype(F32)

    across = move(frames, 0, 2)
    near = move(frames, 0, 1)
    far = move(across, 0, 1)

    first_end = lengths[0, 0]
    second_end = first_end + lengths[0, 1]
    third_end = second_end + lengths[0, 2]
    order = jnp.array([0, 2, 1, 3], jnp.int32) ^ own_s
    positions = (order[:, None] * rows + jnp.arange(rows, dtype=jnp.int32)[None, :]).reshape(slab, 1)
    segments = sum((positions >= end).astype(jnp.int32) for end in (first_end, second_end, third_end))
    lanes = jnp.arange(LANES, dtype=jnp.int32)[None, :]
    kmask = jnp.where((segments == lanes) | (lanes > 3), 0.0, MASK).astype(BF)
    qhot = (segments[:rows] == lanes).astype(BF)
    if fast:
        own = jnp.stack([own_s, own_d]).astype(jnp.int32)
    else:
        own = jnp.zeros((2,), jnp.int32)

    mixed, e, rinv, q, k, v, x_t = attend((frames, across, near, far), input_weight, vectors, kmask, qhot)
    layer, act, slope, norm1, inv1, hlt, mt, gs, gb, gbt, red_s, vec1 = ahead(
        own, mixed, frames, cotangent, qhot, output_weight, expand_weight, reduce_weight, vectors
    )

    def behind_of(after):
        return behind(
            own, slope, gb, gs, norm1, inv1, hlt, mt, output_weight, expand_weight, reduce_weight, vectors, after
        )

    def back(group, pairs, grad_mixed, after, **more):
        return attend_back(group, pairs, own, e, q, k, v, grad_mixed, mixed, rinv, x_t, after, **more)

    if fast:
        red, exp, in1, in2, gx, dx = reduce_fast(move, own, back, behind_of, input_weight, gbt, act, red_s, vec1)
        inp, out, exp, red, vec, squares = finish(own, red, exp, in1, in2, dx[0])
        squares = tree_sum(move, squares)
    else:
        inp, out, exp, red, vec, squares, gx, dx = reduce_plain(
            move, own, back, behind_of, input_weight, gbt, act, red_s, vec1
        )
    frames_gradient, token = frames_end(gx, *dx)

    grads = [inp, out, exp, red, vec]
    masters, firsts, seconds = (list(states[i : i + 5]) for i in (0, 5, 10))
    for group in (masters, firsts, seconds):
        group[3] = group[3].T
    hidden = expand_weight.shape[1]
    wide, narrow = 2.0 * width**-0.5, 2.0 * hidden**-0.5
    norm, *made = adam_all(
        squares, token, list(zip(masters, firsts, seconds)), grads,
        ((wide, 0.01), (wide, 0.01), (wide, 0.01), (narrow, 0.01), (0.5, 0.0)),
        (False, True, False, False, False),
    )
    made[12:16] = [m.T for m in made[12:16]]
    return (layer, frames_gradient, norm.reshape(()), *made)


def solution(mesh):
    tokens, whole = P(("dp", "seq"), None), P()
    state = (P("dp", "seq"), *(P("seq", "dp"),) * 4)
    outs = tuple(s for s in state for _ in range(4))
    return jax.shard_map(
        local,
        mesh=mesh,
        in_specs=(tokens, tokens, P("dp", None), *(whole,) * 5, *state * 3),
        out_specs=(tokens, tokens, whole, *outs),
        check_vma=False,
    )
```

```python
import functools

import jax
import jax.numpy as jnp
from jax import lax
from jax.experimental import pallas as pl
from jax.experimental.pallas import tpu as pltpu
from jax.sharding import PartitionSpec as P

HD = 64
STEP = 10
LANES = 128
NORM_EPS = 1e-05
MASK = -float(2**30)
BF = jnp.bfloat16
F32 = jnp.float32
AXES = ("dp", "seq")

PLACES = (
    {
        0: ((0, 0, 0), (1, 1, 1), (2, 2, 2)),
        2: ((0, 0, 1), (1, 1, 2), (2, 3, 0)),
        3: ((0, 0, 2), (1, 2, 0), (2, 3, 1)),
        5: ((0, 1, 0), (1, 2, 1), (2, 3, 2)),
    },
    {
        1: ((0, 0, 0), (1, 1, 1), (2, 2, 1), (2, 3, 0)),
        4: ((0, 0, 1), (0, 1, 0), (1, 2, 0), (2, 3, 1)),
    },
)
WIDTHS = (3 * LANES, 2 * LANES)
CALLS = ((0, 2), (3, 5), (1, 4))


def params(mebibytes):
    return pltpu.CompilerParams(vmem_limit_bytes=mebibytes * 2**20)


def cost(microseconds):
    return pl.CostEstimate(flops=int(microseconds * 4.4e9), bytes_accessed=0, transcendentals=0)


def in_hbm(array):
    return pltpu.with_memory_space_constraint(array, pltpu.HBM)


def dot(a, b):
    return lax.dot_general(a, b, (((1,), (0,)), ((), ())), preferred_element_type=F32)


def dot_t(a, b):
    return lax.dot_general(a, b, (((1,), (1,)), ((), ())), preferred_element_type=F32)


def softmax_half(q, k, v, kmask, qhot, e_ref):
    rows, wide = q.shape
    pairs = wide // LANES
    low = lax.broadcasted_iota(jnp.int32, (rows, LANES), 1) < HD
    part = lambda a, p: a[:, p * LANES : (p + 1) * LANES]
    keys = [jnp.concatenate([part(k, p), kmask], axis=1) for p in range(pairs)]
    values = [jnp.concatenate([part(v, p), jnp.ones((v.shape[0], LANES), BF)], axis=1) for p in range(pairs)]

    def score(head):
        qh = part(q, head // 2)
        qh = jnp.where(low if head % 2 == 0 else jnp.logical_not(low), qh, jnp.zeros_like(qh))
        return dot_t(jnp.concatenate([qh, qhot], axis=1), keys[head // 2])

    following = score(0)
    done, results = [], []
    for head in range(2 * pairs):
        scores = following
        if head + 1 < 2 * pairs:
            following = score(head + 1)
        top = jnp.max(scores, axis=1, keepdims=True)
        e = jnp.exp(scores - top).astype(BF)
        e_ref[head] = e
        both = dot(e, values[head // 2])
        done.append((top, both[:, LANES:], both[:, :LANES]))
        if head % 2 == 1:
            results.append([jnp.where(low, a, b) for a, b in zip(*done[-2:])])
    return results


def segment_of(lengths_ref, rows, first):
    own = lax.axis_index("seq")
    at = lax.broadcasted_iota(jnp.int32, (rows, LANES), 0)
    half = rows // 2
    place = jnp.where(at < half, (first ^ own) * half + at, ((first + 1) ^ own) * half + at - half)
    segments, end = jnp.zeros((rows, LANES), jnp.int32), 0
    for n in range(lengths_ref.shape[1]):
        end = end + lengths_ref[0, n]
        segments = segments + (place >= end).astype(jnp.int32)
    return segments


def key_mask(lengths_ref, rows, first):
    lanes = lax.broadcasted_iota(jnp.int32, (rows, LANES), 1)
    segments = segment_of(lengths_ref, rows, first)
    return jnp.where((segments == lanes) | (lanes > 3), 0.0, MASK).astype(BF)


def project_half(x_ref, blocks, wk_ref, wv_ref, vec_ref, k_ref, v_ref, xt_ref):
    step = pl.program_id(0)
    wide = wk_ref.shape[1]
    rows = blocks[0].shape[0]

    @pl.when(step == 0)
    def _():
        for i, ref in enumerate(blocks):
            x_ref[i * rows : (i + 1) * rows, :] = ref[...]

    xt_ref[...] = x_ref[:, pl.ds(pl.multiple_of(step * wide, LANES), wide)].T
    k = dot(x_ref[...], wk_ref[...]).astype(BF)
    v = (dot(x_ref[...], wv_ref[...]) + vec_ref[1:2, :].astype(F32)).astype(BF)
    k_ref[...] = k
    v_ref[...] = v
    return k, v


def attend_near_kernel(
    lengths_ref, x0_ref, x1_ref, wk_ref, wv_ref, vec_ref, wq_ref,
    e_ref, k_ref, v_ref, xt_ref, q_ref, top_ref, sum_ref, out_ref, qhot_ref, wide_ref, x_ref, kmask,
):
    rows, slab = q_ref.shape[0], x_ref.shape[0]

    @pl.when(pl.program_id(0) == 0)
    def _():
        kmask[...] = key_mask(lengths_ref, slab, 0)
        lanes = lax.broadcasted_iota(jnp.int32, (rows, LANES), 1)
        qhot_ref[...] = (segment_of(lengths_ref, slab, 0)[:rows] == lanes).astype(F32).astype(BF)

    wide_ref[...] = vec_ref[...].astype(F32)
    k, v = project_half(x_ref, (x0_ref, x1_ref), wk_ref, wv_ref, vec_ref, k_ref, v_ref, xt_ref)
    q = (dot(x_ref[:rows, :], wq_ref[...]) + vec_ref[0:1, :].astype(F32)).astype(BF)
    q = q * jnp.asarray(HD**-0.5, BF)
    q_ref[...] = q
    for p, made in enumerate(softmax_half(q, k, v, kmask[...], qhot_ref[...], e_ref)):
        for ref, value in zip((top_ref, sum_ref, out_ref), made):
            ref[:, p * LANES : (p + 1) * LANES] = value


def pass_kernel(x_ref, _, out_ref):
    out_ref[...] = x_ref[...]


def pass_on(x, after):
    whole = pl.BlockSpec(x.shape, lambda i: (0, 0))
    return pl.pallas_call(
        pass_kernel,
        grid=(1,), in_specs=[whole, pl.BlockSpec(memory_space=pl.ANY)], out_specs=whole,
        out_shape=jax.ShapeDtypeStruct(x.shape, x.dtype),
        compiler_params=params(6), cost_estimate=cost(1), name="pass_on",
    )(x, after)


def project_kernel(x_ref, xp_ref, wk_ref, wv_ref, vec_ref, _, k_ref, v_ref, xt_ref):
    xt_ref[...] = xp_ref[...].T
    k_ref[...] = dot(x_ref[...], wk_ref[...]).astype(BF)
    v_ref[...] = (dot(x_ref[...], wv_ref[...]) + vec_ref[1:2, :]).astype(BF)


def project(x, input_weight, vectors, after):
    rows, width = x.shape
    wide = 3 * LANES
    steps = width // wide
    weight = in_hbm(input_weight)
    cols = lambda r, off=0: pl.BlockSpec((r, wide), lambda p: (0, p + off))
    down = pl.BlockSpec((wide, rows), lambda p: (p, 0))
    return pl.pallas_call(
        project_kernel,
        grid=(steps,),
        in_specs=[
            pl.BlockSpec((rows, width), lambda p: (0, 0)), cols(rows), cols(width, steps), cols(width, 2 * steps),
            cols(vectors.shape[0]), pl.BlockSpec(memory_space=pl.ANY),
        ],
        out_specs=[cols(rows), cols(rows), down],
        out_shape=[jax.ShapeDtypeStruct((rows, width), BF)] * 2 + [jax.ShapeDtypeStruct((width, rows), BF)],
        compiler_params=params(12), cost_estimate=cost(5),
        name="project",
    )(x, x, weight, weight, vectors, after)


def attend_far_kernel(
    lengths_ref, x0_ref, wk_ref, wv_ref, vec_ref, qhot_ref, q_ref, top_ref, sum_ref, out_ref, k0_ref, v0_ref, xt0_ref,
    e_ref, k_ref, v_ref, xt_ref, mixed_ref, near_ref, far_ref, x_ref, kmask,
):
    rows = x0_ref.shape[0]

    @pl.when(pl.program_id(0) == 0)
    def _():
        kmask[...] = key_mask(lengths_ref, 2 * rows, 2)

    project_half(
        x_ref, (x0_ref,), wk_ref, wv_ref, vec_ref, k_ref.at[rows:, :], v_ref.at[rows:, :], xt_ref.at[:, rows:]
    )
    k_ref[:rows, :] = k0_ref[...]
    v_ref[:rows, :] = v0_ref[...]
    xt_ref[:, :rows] = xt0_ref[...]
    k, v = k_ref[...], v_ref[...]
    for p, (top, total, out) in enumerate(softmax_half(q_ref[...], k, v, kmask[...], qhot_ref[...], e_ref)):
        span = slice(p * LANES, (p + 1) * LANES)
        both = jnp.maximum(top, top_ref[:, span])
        near, far = jnp.exp(top_ref[:, span] - both), jnp.exp(top - both)
        rinv = 1.0 / (near * sum_ref[:, span] + far * total)
        near, far = near * rinv, far * rinv
        near_ref[:, span] = near
        far_ref[:, span] = far
        mixed_ref[:, span] = (out_ref[:, span] * near + out * far).astype(BF)


def attend(lengths, blocks, input_weight, vectors, near=()):
    rows, width = blocks[0].shape
    slab = 2 * rows
    wide = 2 * LANES
    steps = width // wide
    weight = in_hbm(input_weight)
    full = lambda shape: pl.BlockSpec(shape, lambda p: (0,) * len(shape))
    cols = lambda r, off=0: pl.BlockSpec((r, wide), lambda p: (0, p + off))
    down = lambda c: pl.BlockSpec((wide, c), lambda p: (p, 0))
    inputs = [lengths, *blocks, weight, weight, vectors]
    in_specs = [
        pl.BlockSpec(memory_space=pltpu.SMEM), *(full(b.shape) for b in blocks), cols(width, steps), cols(width, 2 * steps), cols(vectors.shape[0]),
    ]
    out_specs = [
        pl.BlockSpec((wide // HD, rows, slab), lambda p: (p, 0, 0)), cols(slab), cols(slab), down(slab),
    ]
    out_shape = [
        pltpu.HBM((width // HD, rows, slab), BF), pltpu.HBM((slab, width), BF), pltpu.HBM((slab, width), BF),
        pltpu.HBM((width, slab), BF),
    ]
    if near:
        inputs += near
        in_specs += [full((rows, LANES)), *[cols(rows)] * 6, down(rows)]
        out_specs += [cols(rows)] * 3
        out_shape += [jax.ShapeDtypeStruct((rows, width), BF), *[pltpu.HBM((rows, width), F32)] * 2]
    else:
        inputs[1] = in_hbm(inputs[1])
        inputs.append(weight)
        in_specs.append(cols(width))
        out_specs += [*[cols(rows)] * 4, full((rows, LANES)), cols(vectors.shape[0])]
        out_shape += [
            jax.ShapeDtypeStruct((rows, width), BF), *[jax.ShapeDtypeStruct((rows, width), F32)] * 3,
            jax.ShapeDtypeStruct((rows, LANES), BF), jax.ShapeDtypeStruct(vectors.shape, F32),
        ]
    return pl.pallas_call(
        attend_far_kernel if near else attend_near_kernel,
        grid=(steps,), in_specs=in_specs, out_specs=out_specs,
        scratch_shapes=[pltpu.VMEM((rows * len(blocks), width), BF), pltpu.VMEM((slab, LANES), BF)],
        out_shape=out_shape,
        compiler_params=params(28), cost_estimate=cost(11),
        name="attend",
    )(*inputs)


def spot(d, own_d):
    rel = d ^ own_d
    return (rel & 1) * 4 + (rel >> 1)


def turn(j):
    return jnp.where(j < 2, 2 * j + 1, 2 * (j - 2))


def by_rows(rows, body):
    block = rows // 4

    def step(i, carry):
        body(pl.ds(pl.multiple_of(i * block, block), block))
        return carry

    lax.fori_loop(0, 4, step, 0)


def store_rows(ref, block, own_d):
    piece = block.shape[0] // 8
    for d in range(8):
        ref[0, spot(d, own_d)] = block[d * piece : (d + 1) * piece, :]


def reduce_kernel(own_ref, gbt_ref, act_ref, rk_ref):
    store_rows(rk_ref, dot(gbt_ref[...], act_ref[0]).astype(BF), own_ref[1])


def reduce_kept(own, gbt, act):
    width, rows = gbt.shape
    chunks, _, cut = act.shape
    return pl.pallas_call(
        reduce_kernel,
        grid_spec=pltpu.PrefetchScalarGridSpec(
            num_scalar_prefetch=1,
            grid=(2,),
            in_specs=[
                pl.BlockSpec((width, rows), lambda j, own: (0, 0)),
                pl.BlockSpec((1, rows, cut), lambda j, own: (j + 2, 0, 0)),
            ],
            out_specs=pl.BlockSpec((1, 8, width // 8, cut), lambda j, own: (j, 0, 0, 0)),
        ),
        out_shape=jax.ShapeDtypeStruct((2, 8, width // 8, cut), BF),
        compiler_params=params(12), cost_estimate=cost(5),
        name="reduce_kept",
    )(own, gbt, act)


def ahead_kernel(
    own_ref, mixed_ref, x_ref, cot_ref, qhot_ref, wo_ref, we_ref, wr_ref, vec_ref,
    layer_ref, act_ref, slope_ref, norm1_ref, inv1_ref, hlt_ref, mt_ref, gs_ref, gb_ref, gbt, rs_ref, vg_ref,
    act, hid, hl, acc,
):
    step = pl.program_id(0)
    own_s, own_d = own_ref[0], own_ref[1]
    rows, width = x_ref.shape
    chunks = act.shape[0]
    j = lax.rem(step, chunks)
    shard = turn(j) ^ own_s
    row = lambda i: vec_ref[i : i + 1, :]

    @pl.when(step == 0)
    def _():
        acc[...] = dot(mixed_ref[...], wo_ref[...])

        def first_norm(at):
            z = x_ref[at, :].astype(F32) + acc[at, :] + row(2)
            center = z - jnp.mean(z, axis=1, keepdims=True)
            inverse = lax.rsqrt(jnp.mean(center * center, axis=1, keepdims=True) + NORM_EPS)
            normed = center * inverse
            hidden = normed * row(3) + row(4)
            hid[at, :] = hidden
            norm1_ref[at, :] = normed
            inv1_ref[at, :] = jnp.broadcast_to(inverse, (z.shape[0], LANES))
            hl[at, :] = hidden.astype(BF)

        by_rows(rows, first_norm)
        hlt_ref[...] = hl[...].T
        mt_ref[...] = mixed_ref[...].T
        vg_ref[...] = jnp.zeros_like(vg_ref)

    @pl.when(step < chunks)
    def _():
        pre = dot(hl[...], we_ref[...]) + vec_ref[pl.ds(8 + shard, 1), :]
        cdf = 0.5 * (1.0 + lax.erf(pre * 0.7071067811865476))
        density = jnp.exp(-0.5 * pre * pre) * 0.3989422804014327
        low = (pre * cdf).astype(BF)
        act[j] = low
        act_ref[0] = low
        slope_ref[0] = cdf + pre * density
        part = dot(low, wr_ref[...])

        @pl.when(step == 0)
        def _():
            acc[...] = part

        @pl.when(step > 0)
        def _():
            acc[...] += part

    @pl.when(step == chunks - 1)
    def _():
        def second_norm(at):
            z = hid[at, :] + acc[at, :] + row(5)
            center = z - jnp.mean(z, axis=1, keepdims=True)
            inverse = lax.rsqrt(jnp.mean(center * center, axis=1, keepdims=True) + NORM_EPS)
            normed = center * inverse
            valid = 1.0 - qhot_ref[at, :][:, 3:4].astype(F32)
            layer_ref[at, :] = ((normed * row(6) + row(7)) * valid).astype(BF)
            gy = cot_ref[at, :].astype(F32) * valid
            e = gy * row(6)
            grad = e - jnp.mean(e, axis=1, keepdims=True)
            grad = (grad - normed * jnp.mean(e * normed, axis=1, keepdims=True)) * inverse
            low = grad.astype(BF)
            vg_ref[5:6, :] += jnp.sum(low.astype(F32), axis=0, keepdims=True)
            vg_ref[6:7, :] += jnp.sum(gy * normed, axis=0, keepdims=True)
            vg_ref[7:8, :] += jnp.sum(gy, axis=0, keepdims=True)
            gb_ref[at, :] = low
            gs_ref[at, :] = grad

        by_rows(rows, second_norm)
        gbt[...] = gb_ref[...].T

    @pl.when(step >= chunks)
    def _():
        store_rows(rs_ref, dot(gbt[...], act[j]).astype(BF), own_d)


def ahead(own, mixed, frames, cotangent, qhot, output_weight, expand_weight, reduce_weight, vectors):
    rows, width = frames.shape
    hidden = expand_weight.shape[1]
    chunks = 4
    cut = hidden // chunks
    piece = width // 8
    first = lambda s: jnp.minimum(s, chunks - 1)
    shard_of = lambda s, own: turn(first(s)) ^ own[0]
    full = lambda shape: pl.BlockSpec(shape, lambda s, own: (0,) * len(shape))
    chunk = pl.BlockSpec((1, rows, cut), lambda s, own: (first(s), 0, 0))
    return pl.pallas_call(
        ahead_kernel,
        grid_spec=pltpu.PrefetchScalarGridSpec(
            num_scalar_prefetch=1,
            grid=(chunks + 2,),
            in_specs=[
                full(mixed.shape), full(frames.shape), full(cotangent.shape), full(qhot.shape),
                full(output_weight.shape),
                pl.BlockSpec((width, cut), lambda s, own: (0, shard_of(s, own))),
                pl.BlockSpec((cut, width), lambda s, own: (shard_of(s, own), 0)),
                full(vectors.shape),
            ],
            out_specs=[
                full((rows, width)), chunk, chunk, full((rows, width)), full((rows, LANES)),
                full((width, rows)), full((width, rows)), full((rows, width)), full((rows, width)), full((width, rows)),
                pl.BlockSpec((1, 8, piece, cut), lambda s, own: (jnp.maximum(s - chunks, 0), 0, 0, 0)),
                full((16, width)),
            ],
            scratch_shapes=[
                pltpu.VMEM((chunks, rows, cut), BF),
                pltpu.VMEM((rows, width), F32),
                pltpu.VMEM((rows, width), BF),
                pltpu.VMEM((rows, width), F32),
            ],
        ),
        out_shape=[
            jax.ShapeDtypeStruct((rows, width), BF),
            jax.ShapeDtypeStruct((chunks, rows, cut), BF),
            jax.ShapeDtypeStruct((chunks, rows, cut), F32),
            jax.ShapeDtypeStruct((rows, width), F32),
            jax.ShapeDtypeStruct((rows, LANES), F32),
            jax.ShapeDtypeStruct((width, rows), BF),
            jax.ShapeDtypeStruct((width, rows), BF),
            jax.ShapeDtypeStruct((rows, width), F32),
            jax.ShapeDtypeStruct((rows, width), BF),
            jax.ShapeDtypeStruct((width, rows), BF),
            jax.ShapeDtypeStruct((2, 8, piece, cut), BF),
            jax.ShapeDtypeStruct((16, width), F32),
        ],
        compiler_params=params(22), cost_estimate=cost(20),
        name="ahead",
    )(own, mixed, frames, cotangent, qhot, output_weight, expand_weight, reduce_weight, vectors)


def behind_kernel(
    own_ref, slope_ref, gb_ref, gs_ref, norm1_ref, inv1_ref, hlt_ref, mt_ref, wo_ref, we_ref, wr_ref, vec_ref, _,
    gf_ref, gm_ref, es_ref, ek_ref, vg_ref,
    acc, tmp, ga,
):
    j = pl.program_id(0)
    own_s, own_d = own_ref[0], own_ref[1]
    rows, width = gb_ref.shape
    shard = turn(j) ^ own_s
    row = lambda i: vec_ref[i : i + 1, :]
    piece, fourth = width // 8, width // 4

    @pl.when(j == 0)
    def _():
        acc[...] = gs_ref[...]
        vg_ref[...] = jnp.zeros_like(vg_ref)

    grad_act = dot_t(gb_ref[...], wr_ref[...])
    low = (grad_act * slope_ref[0]).astype(BF)
    vg_ref[pl.ds(8 + shard, 1), :] = jnp.sum(low.astype(F32), axis=0, keepdims=True)
    acc[...] += dot_t(low, we_ref[...])
    grad_e = dot(hlt_ref[...], low).astype(BF)
    tmp[...] = grad_e.reshape(tmp.shape)
    half = grad_e.shape[1] // 2
    rz = shard ^ (own_d >> 1)
    for part, ref in ((1, es_ref), (0, ek_ref)):
        for ry in range(2):
            for t in range(2):
                block = tmp[own_s ^ (2 * ry + part), :, t * half : (t + 1) * half]
                ref[ry, t ^ (own_d & 1), rz, :fourth, :] = block

    @pl.when(j == pl.num_programs(0) - 1)
    def _():
        def first_back(at):
            gy = acc[at, :]
            normed = norm1_ref[at, :]
            e = gy * row(3)
            grad = e - jnp.mean(e, axis=1, keepdims=True)
            grad = (grad - normed * jnp.mean(e * normed, axis=1, keepdims=True)) * inv1_ref[at, :][:, :1]
            gf_ref[at, :] = grad
            rounded = grad.astype(BF)
            vg_ref[2:3, :] += jnp.sum(rounded.astype(F32), axis=0, keepdims=True)
            vg_ref[3:4, :] += jnp.sum(gy * normed, axis=0, keepdims=True)
            vg_ref[4:5, :] += jnp.sum(gy, axis=0, keepdims=True)
            ga[at, :] = rounded

        by_rows(rows, first_back)
        gm_ref[...] = dot_t(ga[...], wo_ref[...]).astype(BF)
        gat = ga[...].T
        for part, ref in ((1, es_ref), (0, ek_ref)):
            for ry in range(2):
                start = pl.multiple_of((own_s ^ (2 * ry + part)) * fourth, fourth)
                out = dot_t(gat, mt_ref[pl.ds(start, fourth), :]).astype(BF)
                for d in range(8):
                    block = out[d * piece : (d + 1) * piece, :]
                    block = jnp.concatenate([block[: piece // 2], block[piece // 2 :]], axis=1)
                    ref[ry, (d & 1) ^ (own_d & 1), (d >> 1) ^ (own_d >> 1), fourth:, :] = block


def behind(own, slope, gb, gs, norm1, inv1, hlt, mt, output_weight, expand_weight, reduce_weight, vectors, after):
    rows, width = gb.shape
    hidden = expand_weight.shape[1]
    chunks = 4
    cut = hidden // chunks
    fourth, eighth = width // 4, hidden // 8
    shard_of = lambda s, own: turn(s) ^ own[0]
    full = lambda shape: pl.BlockSpec(shape, lambda s, own: (0,) * len(shape))
    spread = (2, 2, 4, fourth + width // 16, eighth)
    return pl.pallas_call(
        behind_kernel,
        grid_spec=pltpu.PrefetchScalarGridSpec(
            num_scalar_prefetch=1,
            grid=(chunks,),
            in_specs=[
                pl.BlockSpec((1, rows, cut), lambda s, own: (s, 0, 0)),
                full(gb.shape), full(gs.shape), full(norm1.shape), full(inv1.shape), full(hlt.shape), full(mt.shape),
                full(output_weight.shape),
                pl.BlockSpec((width, cut), lambda s, own: (0, shard_of(s, own))),
                pl.BlockSpec((cut, width), lambda s, own: (shard_of(s, own), 0)),
                full(vectors.shape), pl.BlockSpec(memory_space=pl.ANY),
            ],
            out_specs=[full((rows, width)), full((rows, width)), full(spread), full(spread), full((16, width))],
            scratch_shapes=[
                pltpu.VMEM((rows, width), F32), pltpu.VMEM((4, fourth, cut), BF), pltpu.VMEM((rows, width), BF),
            ],
        ),
        out_shape=[
            jax.ShapeDtypeStruct((rows, width), F32),
            jax.ShapeDtypeStruct((rows, width), BF),
            jax.ShapeDtypeStruct(spread, BF),
            jax.ShapeDtypeStruct(spread, BF),
            jax.ShapeDtypeStruct((16, width), F32),
        ],
        compiler_params=params(20), cost_estimate=cost(18),
        name="behind",
    )(own, slope, gb, gs, norm1, inv1, hlt, mt, output_weight, expand_weight, reduce_weight, vectors, after)


def back_kernel(group, pairs, first, last, own_ref, q_ref, gm_ref, mixed_ref, *rest):
    halves, rest = (rest[:5], rest[5:10]), list(rest[11:])
    gw_in_ref = None if first else rest.pop(0)
    vec_in = [rest.pop(0) for _ in range(4)] if group == 1 else []
    dq_ref, dkv_ref, vb_ref = rest[:3]
    rest = rest[3:]
    if last:
        gs_ref, gk_ref, gw, *vecs = rest
    else:
        (gw,) = rest
    i = pl.program_id(0)
    own_s, own_d = own_ref[0], own_ref[1]
    rows = q_ref.shape[0]
    q_t = q_ref[...].T
    low = lax.broadcasted_iota(jnp.int32, (rows, LANES), 1) < HD
    dqs, dkvs = [0.0, 0.0], []
    for e_ref, k_ref, v_ref, rinv_ref, _ in halves:
        k, v = k_ref[...], v_ref[...]
        gm = gm_ref[...].astype(F32) * rinv_ref[...]
        both = gm * mixed_ref[...].astype(F32)
        gm_low = gm.astype(BF)
        gm_t = gm_low.T
        dks, dvs = [], []
        for head in range(2):
            own = low if head == 0 else jnp.logical_not(low)
            span = slice(head * HD, (head + 1) * HD)
            e = e_ref[head]
            inner = jnp.sum(jnp.where(own, both, 0.0), axis=1, keepdims=True)
            grad_e = dot_t(jnp.where(own, gm_low, jnp.zeros_like(gm_low)), v)
            ds = (e.astype(F32) * (grad_e - inner)).astype(BF)
            dqs[head] = dqs[head] + dot(ds, k)
            dks.append(dot(q_t[span, :], ds))
            dvs.append(dot(gm_t[span, :], e))
        dkvs.append(jnp.concatenate([*dks, *dvs], axis=0).astype(BF))
    dq = (jnp.where(low, dqs[0], dqs[1]) * HD**-0.5).astype(BF)
    dkv = jnp.concatenate(dkvs, axis=1)
    dq_ref[...] = dq
    dkv_ref[...] = dkv
    ones = jnp.ones((8, dkv.shape[1]), BF)
    bias = jnp.concatenate(
        [jnp.sum(dq.astype(F32), axis=0, keepdims=True), dot_t(ones, dkv[LANES:, :])[0:1, :]], axis=0
    )
    vb_ref[0:2, :] = bias

    if group == 1:

        @pl.when(i == 0)
        def _():
            vecs[0][...] = vec_in[0][...] + vec_in[1][...]
            for call, ref in zip(CALLS, vec_in[2:]):
                for n, p in enumerate(call):
                    vecs[0][0:2, p * LANES : (p + 1) * LANES] = ref[0:2, n * LANES : (n + 1) * LANES]

    if not first:

        @pl.when(i == 0)
        def _():
            gw[...] = gw_in_ref[...]

    grad_q = dot(halves[0][4][:, :rows], dq).astype(BF)
    grad_kv = sum(dot_t(half[4][...], part) for half, part in zip(halves, dkvs)).astype(BF)
    piece = grad_q.shape[0] // 8
    blocks = [b.reshape(8, piece, LANES) for b in (grad_q, grad_kv[:, :LANES], grad_kv[:, LANES:])]
    for n, pair in enumerate(pairs):

        @pl.when(i == n)
        def _():
            for which, shard, place in PLACES[group][pair]:
                gw[shard, :, :piece, place * LANES : (place + 1) * LANES] = blocks[which]
            if group == 1:
                vecs[0][0:2, pair * LANES : (pair + 1) * LANES] = bias

    if last:

        @pl.when(i == len(pairs) - 1)
        def _():
            if group == 1:
                vec, tall = vecs[0][...], vecs[0].shape[1]
                for d in range(8):
                    turned = pltpu.roll(vec, (tall - piece * d) % tall, axis=1)[:, : gw.shape[3]]
                    for shard in range(4):
                        block = pltpu.roll(turned, (16 - 3 * shard) % 16, axis=0) if shard else turned
                        gw[shard, d, piece:, :] = block.astype(BF)
            for ref, part in ((gs_ref, 1), (gk_ref, 0)):
                for ry in range(2):
                    for d in range(8):
                        ref[ry, spot(d, own_d)] = gw[own_s ^ (2 * ry + part), d]


def attend_back(group, pairs, own, q, grad_mixed, mixed, halves, after, gw=None, last=True, vecs=()):
    first = gw is None
    rows, width = q.shape
    half = halves[0][1].shape[0]
    slab = 2 * half
    piece = width // 8
    span = WIDTHS[group]
    pair_of = lambda i: jnp.where(i == 0, pairs[0], pairs[1])
    full = lambda shape: pl.BlockSpec(shape, lambda i, own: (0,) * len(shape))
    cols = lambda r: pl.BlockSpec((r, LANES), lambda i, own: (0, pair_of(i)))
    inputs = [q, grad_mixed, mixed]
    in_specs = [cols(rows)] * 3
    for e, k, v, rinv, x_t in halves:
        inputs += [in_hbm(e), k, v, rinv, x_t]
        in_specs += [
            pl.BlockSpec((2, rows, half), lambda i, own: (pair_of(i), 0, 0)),
            cols(half), cols(half), cols(rows), full(x_t.shape),
        ]
    inputs.append(after)
    in_specs.append(pl.BlockSpec(memory_space=pl.ANY))
    out_shape = [
        jax.ShapeDtypeStruct((rows, len(pairs) * LANES), BF),
        jax.ShapeDtypeStruct((len(pairs) * 2 * LANES, slab), BF),
        jax.ShapeDtypeStruct((8, len(pairs) * LANES), F32),
    ]
    out_specs = [
        pl.BlockSpec((rows, LANES), lambda i, own: (0, i)),
        pl.BlockSpec((2 * LANES, slab), lambda i, own: (i, 0)),
        pl.BlockSpec((8, LANES), lambda i, own: (0, i)),
    ]
    scratch = []
    whole = (4, 8, piece + (16 if vecs else 0), span)
    if not first:
        inputs.append(gw)
        in_specs.append(full(whole))
    inputs += vecs
    in_specs += [full(a.shape) for a in vecs]
    if last:
        out_shape += [jax.ShapeDtypeStruct((2, *whole[1:]), BF)] * 2
        out_specs += [full((2, *whole[1:]))] * 2
        scratch.append(pltpu.VMEM(whole, BF))
        if vecs:
            scratch.append(pltpu.VMEM((16, width), F32))
    else:
        out_shape.append(jax.ShapeDtypeStruct(whole, BF))
        out_specs.append(full(whole))
    return pl.pallas_call(
        functools.partial(back_kernel, group, pairs, first, last),
        grid_spec=pltpu.PrefetchScalarGridSpec(
            num_scalar_prefetch=1, grid=(len(pairs),), in_specs=in_specs, out_specs=out_specs, scratch_shapes=scratch
        ),
        out_shape=out_shape,
        compiler_params=params(20), cost_estimate=cost(12),
        name="attend_back",
    )(own, *inputs)


def frames_kernel(pairs, last, w_ref, gx_in_ref, after_ref, *refs):
    n = len(pairs)
    dqs, dkvs = refs[:n], refs[n : 2 * n]
    refs = list(refs[2 * n :])
    dx_ref = refs.pop(0) if last else None
    gx_ref, *outs, wkv = refs
    j = pl.program_id(0)
    width = gx_ref.shape[1]
    flat = [p for call in pairs for p in call]

    @pl.when(j == 0)
    def _():
        for i, p in enumerate(flat):
            for t in range(2):
                start = (1 + t) * width + p * LANES
                wkv[:, (2 * i + t) * LANES : (2 * i + t + 1) * LANES] = w_ref[:, start : start + LANES]
        wq = jnp.concatenate([w_ref[:, p * LANES : (p + 1) * LANES] for p in flat], axis=1)
        dq = jnp.concatenate([r[...] for r in dqs], axis=1)
        gx_ref[...] = gx_in_ref[...] + dot_t(dq, wq)

    made = dot(wkv[...], jnp.concatenate([r[...] for r in dkvs], axis=0))
    if not last:
        outs[0][0] = made
        return
    made = made + dx_ref[0]

    @pl.when(j < 2)
    def _():
        outs[0][0] = made.astype(BF)

    @pl.when(j >= 2)
    def _():
        outs[1][0] = made


def frames_back(input_weight, gx, after, pairs, dqs, dkvs, dx=None):
    rows, width = gx.shape
    last = dx is not None
    count = 2 * sum(map(len, pairs))
    full = lambda a: pl.BlockSpec(a.shape, lambda j: (0,) * a.ndim)
    column = lambda a: pl.BlockSpec((a.shape[0], rows), lambda j: (0, turn(j)))
    block = lambda pick: pl.BlockSpec((1, width, rows), lambda j: (pick(j), 0, 0))
    if last:
        out_specs = [block(lambda j: jnp.minimum(j, 1)), block(lambda j: jnp.maximum(j - 2, 0))]
        out_shape = [jax.ShapeDtypeStruct((2, width, rows), BF), jax.ShapeDtypeStruct((2, width, rows), F32)]
    else:
        out_specs = [block(lambda j: j)]
        out_shape = [jax.ShapeDtypeStruct((4, width, rows), F32)]
    return pl.pallas_call(
        functools.partial(frames_kernel, pairs, last),
        grid=(4,),
        in_specs=[
            full(input_weight), full(gx), pl.BlockSpec(memory_space=pl.ANY), *map(full, dqs), *map(column, dkvs),
            *([block(lambda j: j)] if last else []),
        ],
        out_specs=[full(gx), *out_specs],
        out_shape=[jax.ShapeDtypeStruct((rows, width), F32), *out_shape],
        scratch_shapes=[pltpu.VMEM((width, count * LANES), BF)],
        compiler_params=params(16), cost_estimate=cost(4 if last else 8),
        name="frames_back",
    )(input_weight, gx, after, *dqs, *dkvs, *([dx] if last else []))


def frames_end_kernel(gx_ref, keep_ref, came_ref, out_ref, token_ref):
    token_ref[...] = jnp.zeros_like(token_ref)
    out_ref[...] = gx_ref[...] + (keep_ref[0] + came_ref[0].astype(F32)).T


def frames_end(gx, keep, came):
    rows, width = gx.shape
    across = pl.BlockSpec((rows, LANES), lambda p: (0, p))
    down = pl.BlockSpec((1, LANES, rows), lambda p: (0, p, 0))
    return pl.pallas_call(
        frames_end_kernel,
        grid=(width // LANES,), in_specs=[across, down, down],
        out_specs=[across, pl.BlockSpec((8, LANES), lambda p: (0, 0))],
        out_shape=[jax.ShapeDtypeStruct((rows, width), F32), jax.ShapeDtypeStruct((8, LANES), F32)], compiler_params=params(8), cost_estimate=cost(5), name="frames_end",
    )(gx, keep, came)


def gather_kernel(plan, *refs):
    start, out = 0, sum(n for n, _ in plan) + 1
    for n, outs in plan:
        ins = refs[start : start + n]
        start += n
        for parts in outs:
            for i, part in enumerate(parts):
                terms = [r[part].astype(F32) for r in ins]
                while len(terms) > 1:
                    terms = [terms[t] + terms[t + 1] for t in range(0, len(terms), 2)]
                refs[out][i] = terms[0].astype(refs[out].dtype)
            out += 1


def gather(sums, after, steps=2):
    inputs, in_specs, out_shape, out_specs, plan = [], [], [], [], []
    for arrays, count, outs in sums:
        cols = arrays[0].shape[-1]
        rows = arrays[0].size // cols // count
        plan.append((len(arrays), tuple(parts for parts, _ in outs)))
        for a in arrays:
            inputs.append(a.reshape(count, rows, cols))
            in_specs.append(pl.BlockSpec((count, rows // steps, cols), lambda i: (0, i, 0)))
        for parts, kind in outs:
            out_shape.append(jax.ShapeDtypeStruct((len(parts), rows, cols), kind))
            out_specs.append(pl.BlockSpec((len(parts), rows // steps, cols), lambda i: (0, i, 0)))
    outs = pl.pallas_call(
        functools.partial(gather_kernel, plan),
        grid=(steps,), in_specs=[*in_specs, pl.BlockSpec(memory_space=pl.ANY)], out_specs=out_specs,
        out_shape=out_shape, compiler_params=params(14), cost_estimate=cost(3), name="gather",
    )(*inputs, after)
    made = []
    for _, parts in plan:
        made.append(outs[: len(parts)])
        outs = outs[len(parts) :]
    return made


def finish_kernel(counts, own_ref, *refs):
    sums = []
    for n in counts:
        parts = [r[0].astype(F32) for r in refs[:n]]
        refs = refs[n:]
        while len(parts) > 1:
            parts = [parts[t] + parts[t + 1] for t in range(0, len(parts), 2)]
        sums.append(parts[0])
    inp_ref, out_ref, exp_ref, red_ref, vec_ref, sq_ref = refs[1:]
    red, exp, in1, in2 = sums
    rows = in1.shape[0]
    vec = in2[rows : rows + vec_ref.shape[0], : vec_ref.shape[1]]
    vec_ref[...] = vec
    in2 = in2[:rows]
    even = jnp.concatenate([in1[:, :128], in2[:, :128], in1[:, 128:], in2[:, 128:]], axis=1)
    odd = jnp.concatenate([in2[:, :128], in1[:, :256], in2[:, 128:], in1[:, 256:]], axis=1)
    odd = pltpu.roll(odd, odd.shape[1] - HD, axis=1)
    inp = jnp.where((own_ref[0] & 1) == 1, odd, even)[:, : inp_ref.shape[1]]
    tall = exp_ref.shape[0]
    out = exp[tall:, :]
    half = out_ref.shape[1]
    out = jnp.concatenate([out[:, :half], pltpu.roll(out, half, axis=1)[:, :half]], axis=0)
    inp_ref[...] = inp
    out_ref[...] = out
    exp_ref[...] = exp[:tall, :]
    red_ref[...] = red
    squares = jnp.zeros((1, 1), F32)
    for g in (inp, out, exp[:tall, :], red, vec):
        squares = squares + jnp.sum(jnp.sum(g * g, axis=0, keepdims=True), axis=1, keepdims=True)
    sq_ref[...] = jnp.broadcast_to(squares, sq_ref.shape)


def finish(own, red, exp, in1, in2, after):
    piece = in1[0].shape[1]
    tall = exp[0].shape[1] - piece // 2
    vmem = pl.BlockSpec(memory_space=pltpu.VMEM)
    inputs = [*red, *exp, *in1, *in2]
    return pl.pallas_call(
        functools.partial(finish_kernel, tuple(map(len, (red, exp, in1, in2)))),
        in_specs=[
            pl.BlockSpec(memory_space=pltpu.SMEM), *[vmem] * len(inputs), pl.BlockSpec(memory_space=pl.ANY)
        ],
        out_specs=[vmem] * 6,
        out_shape=[
            jax.ShapeDtypeStruct((piece, 9 * HD), F32),
            jax.ShapeDtypeStruct((piece, 3 * HD), F32),
            jax.ShapeDtypeStruct((tall, exp[0].shape[2]), F32),
            jax.ShapeDtypeStruct(red[0].shape[1:], F32),
            jax.ShapeDtypeStruct((3, piece), F32),
            jax.ShapeDtypeStruct((8, LANES), F32),
        ],
        compiler_params=params(8), cost_estimate=cost(3), name="finish",
    )(own, *inputs, after)


def adam_step(master, moment_one, moment_two, gradient, step_rate, decay_weight):
    new_one = 0.9 * moment_one + 0.1 * gradient
    new_two = 0.999 * moment_two + 0.001 * gradient * gradient
    corrected_one = new_one / (1.0 - 0.9**STEP)
    corrected_two = new_two / (1.0 - 0.999**STEP)
    new_master = master - step_rate * (
        corrected_one / (jnp.sqrt(corrected_two) + 1e-08) + decay_weight * master
    )
    return (new_one, new_two, new_master, new_master.astype(BF))


def adam_kernel(rates, turned, squares_ref, *refs):
    n = len(rates)
    ins, outs = refs[: 4 * n], refs[4 * n :]
    norm = jnp.sqrt(squares_ref[0:1, 0:1])
    outs[0][...] = norm
    factor = 1.0 / jnp.maximum(norm, 1.0)
    for a in range(n):
        master, one, two, grad = (r[...] for r in ins[4 * a : 4 * a + 4])
        if turned[a]:
            grad = grad.T
        made = adam_step(master, one, two, grad * factor, rates[a][0], rates[a][1])
        for b in range(4):
            outs[1 + 4 * a + b][...] = made[b]


def adam_all(squares, states, grads, rates, turned):
    inputs, out_shape = [squares], [jax.ShapeDtypeStruct((1, 1), F32)]
    for state, grad in zip(states, grads):
        inputs += [*state, grad]
        shape = state[0].shape
        out_shape += [jax.ShapeDtypeStruct(shape, F32)] * 3 + [jax.ShapeDtypeStruct(shape, BF)]
    vmem = pl.BlockSpec(memory_space=pltpu.VMEM)
    return pl.pallas_call(
        functools.partial(adam_kernel, rates, turned),
        in_specs=[vmem] * len(inputs), out_specs=[vmem] * len(out_shape), out_shape=out_shape,
        compiler_params=params(16), cost_estimate=cost(5), name="adam",
    )(*inputs)


def mover(dp, seq):
    def move(value, bits_d, bits_s):
        pairs = [(d * seq + s, (d ^ bits_d) * seq + (s ^ bits_s)) for d in range(dp) for s in range(seq)]
        return lax.ppermute(value, AXES, pairs)

    return move


def tree_sum(move, value, token):
    value = value + move(value, 0, 1)
    value = (value + move(value, 0, 2)) + (move(value, 1, 0) + move(value, 1, 2))
    return (value + move(value, 2, 0)) + (move(value, 4, 0) + move(value, 6, 0)) + token


def spread_out(move, parts):
    return [parts[0], *(move(parts[b], 2 * b, 0) for b in (1, 2, 3))]


def plane(move, parts):
    return [parts[0], move(parts[1], 1, 0), move(parts[2], 0, 2), move(parts[3], 1, 2)]


def scatter_plain(parts, dim):
    part = lax.psum_scatter(parts, "seq", scatter_dimension=0, tiled=True)[0].astype(F32)
    return lax.psum_scatter(part, "dp", scatter_dimension=dim, tiled=True)


def in_order(kept, sent):
    parts = jnp.stack([kept, sent], axis=1)
    rows, cols = parts.shape[-2:]
    return parts.reshape(4, 2, 4, rows, cols).swapaxes(1, 2).reshape(4, 8 * rows, cols)


HALVES = tuple((parts, BF) for parts in ((0, 2), (4, 6), (1, 5), (3, 7)))
PAIR = (((0,), BF), ((1,), BF))
QUARTERS = tuple(((part,), BF) for part in range(4))
ONE = (((0,), BF),)
Z_HALVES = (((0, 1), BF), ((2, 3), BF))


def both_ways(move, cut):
    y_keep, y_send, x_keep, x_send = cut
    return (y_keep, move(y_send, 0, 2)), (x_keep, move(x_send, 1, 0))


def turned_ways(move, y_cut, x_cut):
    return (y_cut[0], move(y_cut[1], 1, 0)), (x_cut[0], move(x_cut[1], 0, 2))


def reduce_fast(move, own, back, behind_of, input_weight, gbt, act, red_s, vec1):
    red_c = move(red_s, 0, 1)
    red_k = reduce_kept(own, gbt, act)
    (red,) = gather([((red_k, red_c), 8, HALVES)], red_k)
    red_y, red_x = both_ways(move, red)

    gf, grad_mixed, exp_s, exp_k, vec2 = behind_of(red[0])
    exp_c = move(exp_s, 0, 1)
    red_y, red_x = gather([(red_y, 2, PAIR), (red_x, 2, PAIR)], vec2)
    red_y, red_x = turned_ways(move, red_y, red_x)

    dq0, dkv0, vb0, gw = back(0, CALLS[0], grad_mixed, red_y[0], last=False)
    (red_k,), (red_s,), exp = gather([(red_y, 1, ONE), (red_x, 1, ONE), ((exp_k, exp_c), 8, HALVES)], vb0)
    red = red_k, move(red_s, 4, 0)
    exp_y, exp_x = both_ways(move, exp)

    dq1, dkv1, vb1, in_s1, in_k1 = back(0, CALLS[1], grad_mixed, red_k, gw=gw)
    in_c1 = move(in_s1, 0, 1)
    (red_k, red_s), exp_y, exp_x = gather([(red, 2, PAIR), (exp_y, 2, PAIR), (exp_x, 2, PAIR)], vb1)
    red = red_k, move(red_s, 2, 0)
    exp_y, exp_x = turned_ways(move, exp_y, exp_x)

    gx, dx = frames_back(input_weight, gf, red_k, CALLS[:2], (dq0, dq1), (dkv0, dkv1))
    (exp_k,), (exp_s,), in1 = gather([(exp_y, 1, ONE), (exp_x, 1, ONE), ((in_k1, in_c1), 4, QUARTERS)], gx)
    exp = exp_k, move(exp_s, 4, 0)
    in1 = plane(move, in1)

    dq2, dkv2, vb2, in_s2, in_k2 = back(1, CALLS[2], grad_mixed, exp_k, vecs=(vec1, vec2, vb0, vb1))
    in_c2 = move(in_s2, 0, 1)
    (exp_k, exp_s), (in1_k, in1_s) = gather([(exp, 2, PAIR), (in1, 4, Z_HALVES)], vb2, 1)
    in1 = in1_k, move(in1_s, 4, 0)
    (in2,) = gather([((in_k2, in_c2), 4, QUARTERS)], exp_k, 1)
    in2 = plane(move, in2)

    gx, dx_s, dx_k = frames_back(input_weight, gx, in2[0], CALLS[2:], (dq2,), (dkv2,), dx)
    dx_c = move(dx_s, 0, 1)
    in2, (in1_k, in1_s) = gather([(in2, 4, QUARTERS), (in1, 2, PAIR)], gx, 1)
    in2 = spread_out(move, in2)
    in1 = in1_k, move(in1_s, 2, 0)
    exp = exp_k, move(exp_s, 2, 0)
    ((dx_k, dx_s),) = gather([((dx_k, dx_c), 2, (((0,), F32), ((1,), BF)))], in1_k)
    return red, exp, in1, in2, gx, (dx_k, move(dx_s, 0, 2))


def reduce_plain(move, own, back, behind_of, input_weight, gbt, act, red_s, vec1):
    red_k = reduce_kept(own, gbt, act)
    gf, grad_mixed, exp_s, exp_k, vec2 = behind_of(red_k)
    dq0, dkv0, vb0, gw = back(0, CALLS[0], grad_mixed, vec2, last=False)
    dq1, dkv1, vb1, in_s1, in_k1 = back(0, CALLS[1], grad_mixed, vb0, gw=gw)
    dq2, dkv2, vb2, in_s2, in_k2 = back(1, CALLS[2], grad_mixed, vb1, vecs=(vec1, vec2, vb0, vb1))
    gx, dx = frames_back(input_weight, gf, vb2, CALLS[:2], (dq0, dq1), (dkv0, dkv1))
    gx, dx_s, dx_k = frames_back(input_weight, gx, vb2, CALLS[2:], (dq2,), (dkv2,), dx)
    ((dx_keep, dx_send),) = gather([((dx_k, move(dx_s, 0, 1)), 2, (((0,), F32), ((1,), BF)))], vb2)
    dx = dx_keep, move(dx_send, 0, 2)
    red = scatter_plain(in_order(red_k, red_s), 0)
    in1 = scatter_plain(in_order(in_k1, in_s1), 0)
    both = in_order(in_k2, in_s2)
    both = both.reshape(4, 8, -1, both.shape[-1])
    piece = in_k1.shape[2]
    in2 = scatter_plain(both[:, :, :piece].reshape(4, 8 * piece, -1), 0)
    vec = scatter_plain(both[:, :, piece : piece + 3, :piece].swapaxes(1, 2).reshape(4, 3, -1), 1)
    both = jnp.stack([exp_k, exp_s], axis=1).transpose(0, 1, 3, 2, 4, 5)
    tall, wide = both.shape[-2] - piece // 2, both.shape[-1]
    both = both.reshape(4, 8, -1, wide)
    exp = scatter_plain(both[:, :, :tall].swapaxes(1, 2).reshape(4, tall, 8 * wide), 1)
    out = both[:, :, tall:].reshape(4, 8, piece // 2, 2, wide // 2).swapaxes(2, 3)
    out = scatter_plain(out.reshape(4, 8 * piece, wide // 2), 0)
    even = jnp.concatenate([in1[:, :128], in2[:, :128], in1[:, 128:], in2[:, 128:192]], axis=1)
    odd = jnp.concatenate([in2[:, 64:128], in1[:, :256], in2[:, 128:], in1[:, 256:]], axis=1)
    inp = jnp.where(lax.axis_index("seq") % 2 == 1, odd, even)
    squares = sum(jnp.sum(g * g) for g in (inp, out, exp, red, vec))
    squares = lax.psum(jnp.full((8, LANES), squares, F32), AXES)
    return inp, out, exp, red, vec, squares, gx, dx


def local(
    frames, cotangent, lengths,
    input_weight, output_weight, expand_weight, reduce_weight, vector_copy,
    *states,
):
    rows, width = frames.shape
    seq, dp = lax.axis_size("seq"), lax.axis_size("dp")
    move = mover(dp, seq)
    own_s, own_d = lax.axis_index("seq"), lax.axis_index("dp")
    fast = dp == 8

    near = move(frames, 0, 1)
    across = move(frames, 0, 2)
    own = jnp.stack([own_s, own_d]).astype(jnp.int32) if fast else jnp.zeros((2,), jnp.int32)

    e0, k0, v0, xt0, q, *stats, qhot, vectors = attend(lengths, (frames, near), input_weight, vector_copy)
    across = pass_on(across, stats[0])
    far = move(across, 0, 1)
    rest = qhot, q, *stats, *project(across, input_weight, vectors, stats[0])
    e1, k1, v1, xt1, mixed, rinv0, rinv1 = attend(lengths, (far,), input_weight, vectors, rest)
    halves = (e0, k0, v0, rinv0, xt0), (e1, k1, v1, rinv1, xt1)
    layer, act, slope, norm1, inv1, hlt, mt, gs, gb, gbt, red_s, vec1 = ahead(
        own, mixed, frames, cotangent, qhot, output_weight, expand_weight, reduce_weight, vectors
    )

    def behind_of(after):
        return behind(
            own, slope, gb, gs, norm1, inv1, hlt, mt, output_weight, expand_weight, reduce_weight, vectors, after
        )

    def back(group, pairs, grad_mixed, after, **more):
        return attend_back(group, pairs, own, q, grad_mixed, mixed, halves, after, **more)

    if fast:
        red, exp, in1, in2, gx, dx = reduce_fast(move, own, back, behind_of, input_weight, gbt, act, red_s, vec1)
        inp, out, exp, red, vec, squares = finish(own, red, exp, in1, in2, dx[0])
        frames_gradient, token = frames_end(gx, *dx)
        squares = tree_sum(move, squares, token)
    else:
        inp, out, exp, red, vec, squares, gx, dx = reduce_plain(
            move, own, back, behind_of, input_weight, gbt, act, red_s, vec1
        )
        frames_gradient, token = frames_end(gx, *dx)
        squares = squares + token

    grads = [inp, out, exp, red, vec]
    masters, firsts, seconds = (list(states[i : i + 5]) for i in (0, 5, 10))
    for group in (masters, firsts, seconds):
        group[3] = group[3].T
    hidden = expand_weight.shape[1]
    wide, narrow = 2.0 * width**-0.5, 2.0 * hidden**-0.5
    norm, *made = adam_all(
        squares, list(zip(masters, firsts, seconds)), grads,
        ((wide, 0.01), (wide, 0.01), (wide, 0.01), (narrow, 0.01), (0.5, 0.0)),
        (False, True, False, False, False),
    )
    made[12:16] = [m.T for m in made[12:16]]
    return (layer, frames_gradient, norm.reshape(()), *made)


def solution(mesh):
    tokens, whole = P(("dp", "seq"), None), P()
    state = (P("dp", "seq"), *(P("seq", "dp"),) * 4)
    outs = tuple(s for s in state for _ in range(4))
    return jax.shard_map(
        local,
        mesh=mesh,
        in_specs=(tokens, tokens, P("dp", None), *(whole,) * 5, *state * 3),
        out_specs=(tokens, tokens, whole, *outs),
        check_vma=False,
    )
```

```python
import functools

import jax
import jax.numpy as jnp
from jax import lax
from jax.experimental import pallas as pl
from jax.experimental.pallas import tpu as pltpu
from jax.sharding import PartitionSpec as P

HD = 64
STEP = 10
LANES = 128
NORM_EPS = 1e-05
MASK = -float(2**30)
BF = jnp.bfloat16
F32 = jnp.float32
AXES = ("dp", "seq")

PLACES = (
    {
        0: ((0, 0, 0), (1, 1, 1), (2, 2, 2)),
        2: ((0, 0, 1), (1, 1, 2), (2, 3, 0)),
        3: ((0, 0, 2), (1, 2, 0), (2, 3, 1)),
        5: ((0, 1, 0), (1, 2, 1), (2, 3, 2)),
    },
    {
        1: ((0, 0, 0), (1, 1, 1), (2, 2, 1), (2, 3, 0)),
        4: ((0, 0, 1), (0, 1, 0), (1, 2, 0), (2, 3, 1)),
    },
)
WIDTHS = (3 * LANES, 2 * LANES)
CALLS = ((0, 2), (3, 5), (1, 4))


def params(mebibytes):
    return pltpu.CompilerParams(vmem_limit_bytes=mebibytes * 2**20)


def cost(microseconds):
    return pl.CostEstimate(flops=int(microseconds * 4.4e9), bytes_accessed=0, transcendentals=0)


def in_hbm(array):
    return pltpu.with_memory_space_constraint(array, pltpu.HBM)


def dot(a, b):
    return lax.dot_general(a, b, (((1,), (0,)), ((), ())), preferred_element_type=F32)


def dot_t(a, b):
    return lax.dot_general(a, b, (((1,), (1,)), ((), ())), preferred_element_type=F32)


def softmax_half(q, k, v, kmask, qhot, e_ref):
    rows, wide = q.shape
    pairs = wide // LANES
    low = lax.broadcasted_iota(jnp.int32, (rows, LANES), 1) < HD
    part = lambda a, p: a[:, p * LANES : (p + 1) * LANES]
    keys = [jnp.concatenate([part(k, p), kmask], axis=1) for p in range(pairs)]
    values = [jnp.concatenate([part(v, p), jnp.ones((v.shape[0], LANES), BF)], axis=1) for p in range(pairs)]

    def score(head):
        qh = part(q, head // 2)
        qh = jnp.where(low if head % 2 == 0 else jnp.logical_not(low), qh, jnp.zeros_like(qh))
        return dot_t(jnp.concatenate([qh, qhot], axis=1), keys[head // 2])

    following = score(0)
    done, results = [], []
    for head in range(2 * pairs):
        scores = following
        if head + 1 < 2 * pairs:
            following = score(head + 1)
        top = jnp.max(scores, axis=1, keepdims=True)
        e = jnp.exp(scores - top).astype(BF)
        e_ref[head] = e
        both = dot(e, values[head // 2])
        done.append((top, both[:, LANES:], both[:, :LANES]))
        if head % 2 == 1:
            results.append([jnp.where(low, a, b) for a, b in zip(*done[-2:])])
    return results


def segment_of(lengths_ref, rows, first):
    own = lax.axis_index("seq")
    at = lax.broadcasted_iota(jnp.int32, (rows, LANES), 0)
    half = rows // 2
    place = jnp.where(at < half, (first ^ own) * half + at, ((first + 1) ^ own) * half + at - half)
    segments, end = jnp.zeros((rows, LANES), jnp.int32), 0
    for n in range(lengths_ref.shape[1]):
        end = end + lengths_ref[0, n]
        segments = segments + (place >= end).astype(jnp.int32)
    return segments


def key_mask(lengths_ref, rows, first):
    lanes = lax.broadcasted_iota(jnp.int32, (rows, LANES), 1)
    segments = segment_of(lengths_ref, rows, first)
    return jnp.where((segments == lanes) | (lanes > 3), 0.0, MASK).astype(BF)


def project_half(x_ref, blocks, wk_ref, wv_ref, vec_ref, k_ref, v_ref, xt_ref):
    step = pl.program_id(0)
    wide = wk_ref.shape[1]
    rows = blocks[0].shape[0]

    @pl.when(step == 0)
    def _():
        for i, ref in enumerate(blocks):
            x_ref[i * rows : (i + 1) * rows, :] = ref[...]

    xt_ref[...] = x_ref[:, pl.ds(pl.multiple_of(step * wide, LANES), wide)].T
    k = dot(x_ref[...], wk_ref[...]).astype(BF)
    v = (dot(x_ref[...], wv_ref[...]) + vec_ref[1:2, :].astype(F32)).astype(BF)
    k_ref[...] = k
    v_ref[...] = v
    return k, v


def attend_near_kernel(
    lengths_ref, x0_ref, x1_ref, wk_ref, wv_ref, vec_ref, wq_ref,
    e_ref, k_ref, v_ref, xt_ref, q_ref, top_ref, sum_ref, out_ref, qhot_ref, wide_ref, x_ref, kmask,
):
    rows, slab = q_ref.shape[0], x_ref.shape[0]

    @pl.when(pl.program_id(0) == 0)
    def _():
        kmask[...] = key_mask(lengths_ref, slab, 0)
        lanes = lax.broadcasted_iota(jnp.int32, (rows, LANES), 1)
        qhot_ref[...] = (segment_of(lengths_ref, slab, 0)[:rows] == lanes).astype(F32).astype(BF)

    wide_ref[...] = vec_ref[...].astype(F32)
    k, v = project_half(x_ref, (x0_ref, x1_ref), wk_ref, wv_ref, vec_ref, k_ref, v_ref, xt_ref)
    q = (dot(x_ref[:rows, :], wq_ref[...]) + vec_ref[0:1, :].astype(F32)).astype(BF)
    q = q * jnp.asarray(HD**-0.5, BF)
    q_ref[...] = q
    for p, made in enumerate(softmax_half(q, k, v, kmask[...], qhot_ref[...], e_ref)):
        for ref, value in zip((top_ref, sum_ref, out_ref), made):
            ref[:, p * LANES : (p + 1) * LANES] = value


def pass_kernel(x_ref, _, out_ref):
    out_ref[...] = x_ref[...]


def pass_on(x, after):
    whole = pl.BlockSpec(x.shape, lambda i: (0, 0))
    return pl.pallas_call(
        pass_kernel,
        grid=(1,), in_specs=[whole, pl.BlockSpec(memory_space=pl.ANY)], out_specs=whole,
        out_shape=jax.ShapeDtypeStruct(x.shape, x.dtype),
        compiler_params=params(6), cost_estimate=cost(1), name="pass_on",
    )(x, after)


def project_kernel(x_ref, xp_ref, wk_ref, wv_ref, vec_ref, _, k_ref, v_ref, xt_ref):
    xt_ref[...] = xp_ref[...].T
    k_ref[...] = dot(x_ref[...], wk_ref[...]).astype(BF)
    v_ref[...] = (dot(x_ref[...], wv_ref[...]) + vec_ref[1:2, :]).astype(BF)


def project(x, input_weight, vectors, after):
    rows, width = x.shape
    wide = 3 * LANES
    steps = width // wide
    weight = in_hbm(input_weight)
    cols = lambda r, off=0: pl.BlockSpec((r, wide), lambda p: (0, p + off))
    down = pl.BlockSpec((wide, rows), lambda p: (p, 0))
    return pl.pallas_call(
        project_kernel,
        grid=(steps,),
        in_specs=[
            pl.BlockSpec((rows, width), lambda p: (0, 0)), cols(rows), cols(width, steps), cols(width, 2 * steps),
            cols(vectors.shape[0]), pl.BlockSpec(memory_space=pl.ANY),
        ],
        out_specs=[cols(rows), cols(rows), down],
        out_shape=[jax.ShapeDtypeStruct((rows, width), BF)] * 2 + [jax.ShapeDtypeStruct((width, rows), BF)],
        compiler_params=params(12), cost_estimate=cost(5),
        name="project",
    )(x, x, weight, weight, vectors, after)


def attend_far_kernel(
    lengths_ref, x0_ref, wk_ref, wv_ref, vec_ref, qhot_ref, q_ref, top_ref, sum_ref, out_ref, k0_ref, v0_ref, xt0_ref,
    e_ref, k_ref, v_ref, xt_ref, mixed_ref, near_ref, far_ref, x_ref, kmask,
):
    rows = x0_ref.shape[0]

    @pl.when(pl.program_id(0) == 0)
    def _():
        kmask[...] = key_mask(lengths_ref, 2 * rows, 2)

    project_half(
        x_ref, (x0_ref,), wk_ref, wv_ref, vec_ref, k_ref.at[rows:, :], v_ref.at[rows:, :], xt_ref.at[:, rows:]
    )
    k_ref[:rows, :] = k0_ref[...]
    v_ref[:rows, :] = v0_ref[...]
    xt_ref[:, :rows] = xt0_ref[...]
    k, v = k_ref[...], v_ref[...]
    for p, (top, total, out) in enumerate(softmax_half(q_ref[...], k, v, kmask[...], qhot_ref[...], e_ref)):
        span = slice(p * LANES, (p + 1) * LANES)
        both = jnp.maximum(top, top_ref[:, span])
        near, far = jnp.exp(top_ref[:, span] - both), jnp.exp(top - both)
        rinv = 1.0 / (near * sum_ref[:, span] + far * total)
        near, far = near * rinv, far * rinv
        near_ref[:, span] = near
        far_ref[:, span] = far
        mixed_ref[:, span] = (out_ref[:, span] * near + out * far).astype(BF)


def attend(lengths, blocks, input_weight, vectors, near=()):
    rows, width = blocks[0].shape
    slab = 2 * rows
    wide = 2 * LANES
    steps = width // wide
    weight = in_hbm(input_weight)
    full = lambda shape: pl.BlockSpec(shape, lambda p: (0,) * len(shape))
    cols = lambda r, off=0: pl.BlockSpec((r, wide), lambda p: (0, p + off))
    down = lambda c: pl.BlockSpec((wide, c), lambda p: (p, 0))
    inputs = [lengths, *blocks, weight, weight, vectors]
    in_specs = [
        pl.BlockSpec(memory_space=pltpu.SMEM), *(full(b.shape) for b in blocks), cols(width, steps), cols(width, 2 * steps), cols(vectors.shape[0]),
    ]
    out_specs = [
        pl.BlockSpec((wide // HD, rows, slab), lambda p: (p, 0, 0)), cols(slab), cols(slab), down(slab),
    ]
    out_shape = [
        pltpu.HBM((width // HD, rows, slab), BF), pltpu.HBM((slab, width), BF), pltpu.HBM((slab, width), BF),
        pltpu.HBM((width, slab), BF),
    ]
    if near:
        inputs += near
        in_specs += [full((rows, LANES)), *[cols(rows)] * 6, down(rows)]
        out_specs += [cols(rows)] * 3
        out_shape += [jax.ShapeDtypeStruct((rows, width), BF), *[pltpu.HBM((rows, width), F32)] * 2]
    else:
        inputs[1] = in_hbm(inputs[1])
        inputs.append(weight)
        in_specs.append(cols(width))
        out_specs += [*[cols(rows)] * 4, full((rows, LANES)), cols(vectors.shape[0])]
        out_shape += [
            jax.ShapeDtypeStruct((rows, width), BF), *[jax.ShapeDtypeStruct((rows, width), F32)] * 3,
            jax.ShapeDtypeStruct((rows, LANES), BF), jax.ShapeDtypeStruct(vectors.shape, F32),
        ]
    return pl.pallas_call(
        attend_far_kernel if near else attend_near_kernel,
        grid=(steps,), in_specs=in_specs, out_specs=out_specs,
        scratch_shapes=[pltpu.VMEM((rows * len(blocks), width), BF), pltpu.VMEM((slab, LANES), BF)],
        out_shape=out_shape,
        compiler_params=params(28), cost_estimate=cost(11),
        name="attend",
    )(*inputs)


def spot(d, own_d):
    rel = d ^ own_d
    return (rel & 1) * 4 + (rel >> 1)


def turn(j):
    return jnp.where(j < 2, 2 * j + 1, 2 * (j - 2))


def by_rows(rows, body, blocks=4):
    block = rows // blocks

    def step(i, carry):
        body(pl.ds(pl.multiple_of(i * block, block), block))
        return carry

    lax.fori_loop(0, blocks, step, 0)


def store_rows(ref, block, own_d):
    piece = block.shape[0] // 8
    for d in range(8):
        ref[0, spot(d, own_d)] = block[d * piece : (d + 1) * piece, :]


def reduce_kernel(own_ref, gbt_ref, act_ref, hl_ref, mixed_ref, rk_ref, hlt_ref, mt_ref):
    store_rows(rk_ref, dot(gbt_ref[...], act_ref[0]).astype(BF), own_ref[1])

    @pl.when(pl.program_id(0) == 0)
    def _():
        hlt_ref[...] = hl_ref[...].T
        mt_ref[...] = mixed_ref[...].T


def reduce_kept(own, gbt, act, hl, mixed):
    width, rows = gbt.shape
    chunks, _, cut = act.shape
    full = lambda a: pl.BlockSpec(a, lambda j, own: (0, 0))
    return pl.pallas_call(
        reduce_kernel,
        grid_spec=pltpu.PrefetchScalarGridSpec(
            num_scalar_prefetch=1,
            grid=(2,),
            in_specs=[
                full((width, rows)), pl.BlockSpec((1, rows, cut), lambda j, own: (j + 2, 0, 0)),
                full((rows, width)), full((rows, width)),
            ],
            out_specs=[
                pl.BlockSpec((1, 8, width // 8, cut), lambda j, own: (j, 0, 0, 0)), full((width, rows)),
                full((width, rows)),
            ],
        ),
        out_shape=[
            jax.ShapeDtypeStruct((2, 8, width // 8, cut), BF),
            jax.ShapeDtypeStruct((width, rows), BF), jax.ShapeDtypeStruct((width, rows), BF),
        ],
        compiler_params=params(12), cost_estimate=cost(5),
        name="reduce_kept",
    )(own, gbt, act, hl, mixed)


def ahead_kernel(
    own_ref, mixed_ref, x_ref, cot_ref, qhot_ref, wo_ref, we_ref, wr_ref, vec_ref,
    layer_ref, act_ref, slope_ref, norm1_ref, inv1_ref, hl, gs_ref, gb_ref, gbt, rs_ref, vg_ref,
    act, hid, acc,
):
    step = pl.program_id(0)
    own_s, own_d = own_ref[0], own_ref[1]
    rows, width = x_ref.shape
    chunks = act.shape[0]
    j = lax.rem(step, chunks)
    shard = turn(j) ^ own_s
    row = lambda i: vec_ref[i : i + 1, :]

    @pl.when(step == 0)
    def _():
        acc[...] = dot(mixed_ref[...], wo_ref[...])

        def first_norm(at):
            z = x_ref[at, :].astype(F32) + acc[at, :] + row(2)
            center = z - jnp.mean(z, axis=1, keepdims=True)
            inverse = lax.rsqrt(jnp.mean(center * center, axis=1, keepdims=True) + NORM_EPS)
            normed = center * inverse
            hidden = normed * row(3) + row(4)
            hid[at, :] = hidden
            norm1_ref[at, :] = normed
            inv1_ref[at, :] = jnp.broadcast_to(inverse, (z.shape[0], LANES))
            hl[at, :] = hidden.astype(BF)

        by_rows(rows, first_norm, 2)
        vg_ref[...] = jnp.zeros_like(vg_ref)

    @pl.when(step < chunks)
    def _():
        pre = dot(hl[...], we_ref[...]) + vec_ref[pl.ds(8 + shard, 1), :]
        cdf = 0.5 * (1.0 + lax.erf(pre * 0.7071067811865476))
        density = jnp.exp(-0.5 * pre * pre) * 0.3989422804014327
        low = (pre * cdf).astype(BF)
        act[j] = low
        act_ref[0] = low
        slope_ref[0] = cdf + pre * density
        part = dot(low, wr_ref[...])

        @pl.when(step == 0)
        def _():
            acc[...] = part

        @pl.when(step > 0)
        def _():
            acc[...] += part

    @pl.when(step == chunks - 1)
    def _():
        def second_norm(at):
            z = hid[at, :] + acc[at, :] + row(5)
            center = z - jnp.mean(z, axis=1, keepdims=True)
            inverse = lax.rsqrt(jnp.mean(center * center, axis=1, keepdims=True) + NORM_EPS)
            normed = center * inverse
            valid = 1.0 - qhot_ref[at, :][:, 3:4].astype(F32)
            layer_ref[at, :] = ((normed * row(6) + row(7)) * valid).astype(BF)
            gy = cot_ref[at, :].astype(F32) * valid
            e = gy * row(6)
            grad = e - jnp.mean(e, axis=1, keepdims=True)
            grad = (grad - normed * jnp.mean(e * normed, axis=1, keepdims=True)) * inverse
            low = grad.astype(BF)
            vg_ref[5:6, :] += jnp.sum(low.astype(F32), axis=0, keepdims=True)
            vg_ref[6:7, :] += jnp.sum(gy * normed, axis=0, keepdims=True)
            vg_ref[7:8, :] += jnp.sum(gy, axis=0, keepdims=True)
            gb_ref[at, :] = low
            gs_ref[at, :] = grad

        by_rows(rows, second_norm, 2)
        gbt[...] = gb_ref[...].T

    @pl.when(step >= chunks)
    def _():
        store_rows(rs_ref, dot(gbt[...], act[j]).astype(BF), own_d)


def ahead(own, mixed, frames, cotangent, qhot, output_weight, expand_weight, reduce_weight, vectors):
    rows, width = frames.shape
    hidden = expand_weight.shape[1]
    chunks = 4
    cut = hidden // chunks
    piece = width // 8
    first = lambda s: jnp.minimum(s, chunks - 1)
    shard_of = lambda s, own: turn(first(s)) ^ own[0]
    full = lambda shape: pl.BlockSpec(shape, lambda s, own: (0,) * len(shape))
    chunk = pl.BlockSpec((1, rows, cut), lambda s, own: (first(s), 0, 0))
    return pl.pallas_call(
        ahead_kernel,
        grid_spec=pltpu.PrefetchScalarGridSpec(
            num_scalar_prefetch=1,
            grid=(chunks + 2,),
            in_specs=[
                full(mixed.shape), full(frames.shape), full(cotangent.shape), full(qhot.shape),
                full(output_weight.shape),
                pl.BlockSpec((width, cut), lambda s, own: (0, shard_of(s, own))),
                pl.BlockSpec((cut, width), lambda s, own: (shard_of(s, own), 0)),
                full(vectors.shape),
            ],
            out_specs=[
                full((rows, width)), chunk, chunk, full((rows, width)), full((rows, LANES)),
                full((rows, width)), full((rows, width)), full((rows, width)), full((width, rows)),
                pl.BlockSpec((1, 8, piece, cut), lambda s, own: (jnp.maximum(s - chunks, 0), 0, 0, 0)),
                full((16, width)),
            ],
            scratch_shapes=[
                pltpu.VMEM((chunks, rows, cut), BF),
                pltpu.VMEM((rows, width), F32),
                pltpu.VMEM((rows, width), F32),
            ],
        ),
        out_shape=[
            jax.ShapeDtypeStruct((rows, width), BF),
            jax.ShapeDtypeStruct((chunks, rows, cut), BF),
            jax.ShapeDtypeStruct((chunks, rows, cut), F32),
            jax.ShapeDtypeStruct((rows, width), F32),
            jax.ShapeDtypeStruct((rows, LANES), F32),
            jax.ShapeDtypeStruct((rows, width), BF),
            jax.ShapeDtypeStruct((rows, width), F32),
            jax.ShapeDtypeStruct((rows, width), BF),
            jax.ShapeDtypeStruct((width, rows), BF),
            jax.ShapeDtypeStruct((2, 8, piece, cut), BF),
            jax.ShapeDtypeStruct((16, width), F32),
        ],
        compiler_params=params(22), cost_estimate=cost(20),
        name="ahead",
    )(own, mixed, frames, cotangent, qhot, output_weight, expand_weight, reduce_weight, vectors)


def behind_kernel(
    own_ref, slope_ref, gb_ref, gs_ref, norm1_ref, inv1_ref, hlt_ref, mt_ref, wo_ref, we_ref, wr_ref, vec_ref, _,
    gf_ref, gm_ref, es_ref, ek_ref, vg_ref,
    acc, tmp, ga,
):
    j = pl.program_id(0)
    own_s, own_d = own_ref[0], own_ref[1]
    rows, width = gb_ref.shape
    shard = turn(j) ^ own_s
    row = lambda i: vec_ref[i : i + 1, :]
    piece, fourth = width // 8, width // 4

    @pl.when(j == 0)
    def _():
        acc[...] = gs_ref[...]
        vg_ref[...] = jnp.zeros_like(vg_ref)

    grad_act = dot_t(gb_ref[...], wr_ref[...])
    low = (grad_act * slope_ref[0]).astype(BF)
    vg_ref[pl.ds(8 + shard, 1), :] = jnp.sum(low.astype(F32), axis=0, keepdims=True)
    acc[...] += dot_t(low, we_ref[...])
    grad_e = dot(hlt_ref[...], low).astype(BF)
    tmp[...] = grad_e.reshape(tmp.shape)
    half = grad_e.shape[1] // 2
    rz = shard ^ (own_d >> 1)
    for part, ref in ((1, es_ref), (0, ek_ref)):
        for ry in range(2):
            for t in range(2):
                block = tmp[own_s ^ (2 * ry + part), :, t * half : (t + 1) * half]
                ref[ry, t ^ (own_d & 1), rz, :fourth, :] = block

    @pl.when(j == pl.num_programs(0) - 1)
    def _():
        def first_back(at):
            gy = acc[at, :]
            normed = norm1_ref[at, :]
            e = gy * row(3)
            grad = e - jnp.mean(e, axis=1, keepdims=True)
            grad = (grad - normed * jnp.mean(e * normed, axis=1, keepdims=True)) * inv1_ref[at, :][:, :1]
            gf_ref[at, :] = grad
            rounded = grad.astype(BF)
            vg_ref[2:3, :] += jnp.sum(rounded.astype(F32), axis=0, keepdims=True)
            vg_ref[3:4, :] += jnp.sum(gy * normed, axis=0, keepdims=True)
            vg_ref[4:5, :] += jnp.sum(gy, axis=0, keepdims=True)
            ga[at, :] = rounded

        by_rows(rows, first_back)
        gm_ref[...] = dot_t(ga[...], wo_ref[...]).astype(BF)
        gat = ga[...].T
        for part, ref in ((1, es_ref), (0, ek_ref)):
            for ry in range(2):
                start = pl.multiple_of((own_s ^ (2 * ry + part)) * fourth, fourth)
                out = dot_t(gat, mt_ref[pl.ds(start, fourth), :]).astype(BF)
                for d in range(8):
                    block = out[d * piece : (d + 1) * piece, :]
                    block = jnp.concatenate([block[: piece // 2], block[piece // 2 :]], axis=1)
                    ref[ry, (d & 1) ^ (own_d & 1), (d >> 1) ^ (own_d >> 1), fourth:, :] = block


def behind(own, slope, gb, gs, norm1, inv1, hlt, mt, output_weight, expand_weight, reduce_weight, vectors, after):
    rows, width = gb.shape
    hidden = expand_weight.shape[1]
    chunks = 4
    cut = hidden // chunks
    fourth, eighth = width // 4, hidden // 8
    shard_of = lambda s, own: turn(s) ^ own[0]
    full = lambda shape: pl.BlockSpec(shape, lambda s, own: (0,) * len(shape))
    spread = (2, 2, 4, fourth + width // 16, eighth)
    return pl.pallas_call(
        behind_kernel,
        grid_spec=pltpu.PrefetchScalarGridSpec(
            num_scalar_prefetch=1,
            grid=(chunks,),
            in_specs=[
                pl.BlockSpec((1, rows, cut), lambda s, own: (s, 0, 0)),
                full(gb.shape), full(gs.shape), full(norm1.shape), full(inv1.shape), full(hlt.shape), full(mt.shape),
                full(output_weight.shape),
                pl.BlockSpec((width, cut), lambda s, own: (0, shard_of(s, own))),
                pl.BlockSpec((cut, width), lambda s, own: (shard_of(s, own), 0)),
                full(vectors.shape), pl.BlockSpec(memory_space=pl.ANY),
            ],
            out_specs=[full((rows, width)), full((rows, width)), full(spread), full(spread), full((16, width))],
            scratch_shapes=[
                pltpu.VMEM((rows, width), F32), pltpu.VMEM((4, fourth, cut), BF), pltpu.VMEM((rows, width), BF),
            ],
        ),
        out_shape=[
            jax.ShapeDtypeStruct((rows, width), F32),
            jax.ShapeDtypeStruct((rows, width), BF),
            jax.ShapeDtypeStruct(spread, BF),
            jax.ShapeDtypeStruct(spread, BF),
            jax.ShapeDtypeStruct((16, width), F32),
        ],
        compiler_params=params(20), cost_estimate=cost(18),
        name="behind",
    )(own, slope, gb, gs, norm1, inv1, hlt, mt, output_weight, expand_weight, reduce_weight, vectors, after)


def back_kernel(group, pairs, first, last, own_ref, q_ref, gm_ref, mixed_ref, *rest):
    halves, rest = (rest[:5], rest[5:10]), list(rest[11:])
    gw_in_ref = None if first else rest.pop(0)
    vec_in = [rest.pop(0) for _ in range(4)] if group == 1 else []
    dq_ref, dkv_ref, vb_ref = rest[:3]
    rest = rest[3:]
    if last:
        gs_ref, gk_ref, gw, *vecs = rest
    else:
        (gw,) = rest
    i = pl.program_id(0)
    own_s, own_d = own_ref[0], own_ref[1]
    rows = q_ref.shape[0]
    q_t = q_ref[...].T
    low = lax.broadcasted_iota(jnp.int32, (rows, LANES), 1) < HD
    dqs, dkvs = [0.0, 0.0], []
    for e_ref, k_ref, v_ref, rinv_ref, _ in halves:
        k, v = k_ref[...], v_ref[...]
        gm = gm_ref[...].astype(F32) * rinv_ref[...]
        both = gm * mixed_ref[...].astype(F32)
        gm_low = gm.astype(BF)
        gm_t = gm_low.T
        dks, dvs = [], []
        for head in range(2):
            own = low if head == 0 else jnp.logical_not(low)
            span = slice(head * HD, (head + 1) * HD)
            e = e_ref[head]
            inner = jnp.sum(jnp.where(own, both, 0.0), axis=1, keepdims=True)
            grad_e = dot_t(jnp.where(own, gm_low, jnp.zeros_like(gm_low)), v)
            ds = (e.astype(F32) * (grad_e - inner)).astype(BF)
            dqs[head] = dqs[head] + dot(ds, k)
            dks.append(dot(q_t[span, :], ds))
            dvs.append(dot(gm_t[span, :], e))
        dkvs.append(jnp.concatenate([*dks, *dvs], axis=0).astype(BF))
    dq = (jnp.where(low, dqs[0], dqs[1]) * HD**-0.5).astype(BF)
    dkv = jnp.concatenate(dkvs, axis=1)
    dq_ref[...] = dq
    dkv_ref[...] = dkv
    ones = jnp.ones((8, dkv.shape[1]), BF)
    bias = jnp.concatenate(
        [jnp.sum(dq.astype(F32), axis=0, keepdims=True), dot_t(ones, dkv[LANES:, :])[0:1, :]], axis=0
    )
    vb_ref[0:2, :] = bias

    if group == 1:

        @pl.when(i == 0)
        def _():
            vecs[0][...] = vec_in[0][...] + vec_in[1][...]
            for call, ref in zip(CALLS, vec_in[2:]):
                for n, p in enumerate(call):
                    vecs[0][0:2, p * LANES : (p + 1) * LANES] = ref[0:2, n * LANES : (n + 1) * LANES]

    if not first:

        @pl.when(i == 0)
        def _():
            gw[...] = gw_in_ref[...]

    grad_q = dot(halves[0][4][:, :rows], dq).astype(BF)
    grad_kv = sum(dot_t(half[4][...], part) for half, part in zip(halves, dkvs)).astype(BF)
    piece = grad_q.shape[0] // 8
    blocks = [b.reshape(8, piece, LANES) for b in (grad_q, grad_kv[:, :LANES], grad_kv[:, LANES:])]
    for n, pair in enumerate(pairs):

        @pl.when(i == n)
        def _():
            for which, shard, place in PLACES[group][pair]:
                gw[shard, :, :piece, place * LANES : (place + 1) * LANES] = blocks[which]
            if group == 1:
                vecs[0][0:2, pair * LANES : (pair + 1) * LANES] = bias

    if last:

        @pl.when(i == len(pairs) - 1)
        def _():
            if group == 1:
                vec, tall = vecs[0][...], vecs[0].shape[1]
                for d in range(8):
                    turned = pltpu.roll(vec, (tall - piece * d) % tall, axis=1)[:, : gw.shape[3]]
                    for shard in range(4):
                        block = pltpu.roll(turned, (16 - 3 * shard) % 16, axis=0) if shard else turned
                        gw[shard, d, piece:, :] = block.astype(BF)
            for ref, part in ((gs_ref, 1), (gk_ref, 0)):
                for ry in range(2):
                    for d in range(8):
                        ref[ry, spot(d, own_d)] = gw[own_s ^ (2 * ry + part), d]


def attend_back(group, pairs, own, q, grad_mixed, mixed, halves, after, gw=None, last=True, vecs=(), time=12):
    first = gw is None
    rows, width = q.shape
    half = halves[0][1].shape[0]
    slab = 2 * half
    piece = width // 8
    span = WIDTHS[group]
    pair_of = lambda i: jnp.where(i == 0, pairs[0], pairs[1])
    full = lambda shape: pl.BlockSpec(shape, lambda i, own: (0,) * len(shape))
    cols = lambda r: pl.BlockSpec((r, LANES), lambda i, own: (0, pair_of(i)))
    inputs = [q, grad_mixed, mixed]
    in_specs = [cols(rows)] * 3
    for e, k, v, rinv, x_t in halves:
        inputs += [in_hbm(e), k, v, rinv, x_t]
        in_specs += [
            pl.BlockSpec((2, rows, half), lambda i, own: (pair_of(i), 0, 0)),
            cols(half), cols(half), cols(rows), full(x_t.shape),
        ]
    inputs.append(after)
    in_specs.append(pl.BlockSpec(memory_space=pl.ANY))
    out_shape = [
        jax.ShapeDtypeStruct((rows, len(pairs) * LANES), BF),
        jax.ShapeDtypeStruct((len(pairs) * 2 * LANES, slab), BF),
        jax.ShapeDtypeStruct((8, len(pairs) * LANES), F32),
    ]
    out_specs = [
        pl.BlockSpec((rows, LANES), lambda i, own: (0, i)),
        pl.BlockSpec((2 * LANES, slab), lambda i, own: (i, 0)),
        pl.BlockSpec((8, LANES), lambda i, own: (0, i)),
    ]
    scratch = []
    whole = (4, 8, piece + (16 if vecs else 0), span)
    if not first:
        inputs.append(gw)
        in_specs.append(full(whole))
    inputs += vecs
    in_specs += [full(a.shape) for a in vecs]
    if last:
        out_shape += [jax.ShapeDtypeStruct((2, *whole[1:]), BF)] * 2
        out_specs += [full((2, *whole[1:]))] * 2
        scratch.append(pltpu.VMEM(whole, BF))
        if vecs:
            scratch.append(pltpu.VMEM((16, width), F32))
    else:
        out_shape.append(jax.ShapeDtypeStruct(whole, BF))
        out_specs.append(full(whole))
    return pl.pallas_call(
        functools.partial(back_kernel, group, pairs, first, last),
        grid_spec=pltpu.PrefetchScalarGridSpec(
            num_scalar_prefetch=1, grid=(len(pairs),), in_specs=in_specs, out_specs=out_specs, scratch_shapes=scratch
        ),
        out_shape=out_shape,
        compiler_params=params(20), cost_estimate=cost(time),
        name="attend_back",
    )(own, *inputs)


def frames_kernel(pairs, last, w_ref, gx_in_ref, after_ref, *refs):
    n = len(pairs)
    dqs, dkvs = refs[:n], refs[n : 2 * n]
    refs = list(refs[2 * n :])
    dx_ref = refs.pop(0) if last else None
    gx_ref, *outs, wkv = refs
    j = pl.program_id(0)
    width = gx_ref.shape[1]
    flat = [p for call in pairs for p in call]

    @pl.when(j == 0)
    def _():
        for i, p in enumerate(flat):
            for t in range(2):
                start = (1 + t) * width + p * LANES
                wkv[:, (2 * i + t) * LANES : (2 * i + t + 1) * LANES] = w_ref[:, start : start + LANES]
        wq = jnp.concatenate([w_ref[:, p * LANES : (p + 1) * LANES] for p in flat], axis=1)
        dq = jnp.concatenate([r[...] for r in dqs], axis=1)
        gx_ref[...] = gx_in_ref[...] + dot_t(dq, wq)

    made = dot(wkv[...], jnp.concatenate([r[...] for r in dkvs], axis=0))
    if not last:
        outs[0][0] = made
        return
    made = made + dx_ref[0]

    @pl.when(j < 2)
    def _():
        outs[0][0] = made.astype(BF)

    @pl.when(j >= 2)
    def _():
        outs[1][0] = made


def frames_back(input_weight, gx, after, pairs, dqs, dkvs, dx=None):
    rows, width = gx.shape
    last = dx is not None
    count = 2 * sum(map(len, pairs))
    full = lambda a: pl.BlockSpec(a.shape, lambda j: (0,) * a.ndim)
    column = lambda a: pl.BlockSpec((a.shape[0], rows), lambda j: (0, turn(j)))
    block = lambda pick: pl.BlockSpec((1, width, rows), lambda j: (pick(j), 0, 0))
    if last:
        out_specs = [block(lambda j: jnp.minimum(j, 1)), block(lambda j: jnp.maximum(j - 2, 0))]
        out_shape = [jax.ShapeDtypeStruct((2, width, rows), BF), jax.ShapeDtypeStruct((2, width, rows), F32)]
    else:
        out_specs = [block(lambda j: j)]
        out_shape = [jax.ShapeDtypeStruct((4, width, rows), F32)]
    return pl.pallas_call(
        functools.partial(frames_kernel, pairs, last),
        grid=(4,),
        in_specs=[
            full(input_weight), full(gx), pl.BlockSpec(memory_space=pl.ANY), *map(full, dqs), *map(column, dkvs),
            *([block(lambda j: j)] if last else []),
        ],
        out_specs=[full(gx), *out_specs],
        out_shape=[jax.ShapeDtypeStruct((rows, width), F32), *out_shape],
        scratch_shapes=[pltpu.VMEM((width, count * LANES), BF)],
        compiler_params=params(16), cost_estimate=cost(4 if last else 8),
        name="frames_back",
    )(input_weight, gx, after, *dqs, *dkvs, *([dx] if last else []))


def frames_end_kernel(gx_ref, keep_ref, came_ref, out_ref, token_ref):
    token_ref[...] = jnp.zeros_like(token_ref)
    out_ref[...] = gx_ref[...] + (keep_ref[0] + came_ref[0].astype(F32)).T


def frames_end(gx, keep, came):
    rows, width = gx.shape
    across = pl.BlockSpec((rows, LANES), lambda p: (0, p))
    down = pl.BlockSpec((1, LANES, rows), lambda p: (0, p, 0))
    return pl.pallas_call(
        frames_end_kernel,
        grid=(width // LANES,), in_specs=[across, down, down],
        out_specs=[across, pl.BlockSpec((8, LANES), lambda p: (0, 0))],
        out_shape=[jax.ShapeDtypeStruct((rows, width), F32), jax.ShapeDtypeStruct((8, LANES), F32)], compiler_params=params(8), cost_estimate=cost(5), name="frames_end",
    )(gx, keep, came)


def gather_kernel(plan, *refs):
    start, out = 0, sum(n for n, _ in plan) + 1
    for n, outs in plan:
        ins = refs[start : start + n]
        start += n
        for parts in outs:
            for i, part in enumerate(parts):
                terms = [r[part].astype(F32) for r in ins]
                while len(terms) > 1:
                    terms = [terms[t] + terms[t + 1] for t in range(0, len(terms), 2)]
                refs[out][i] = terms[0].astype(refs[out].dtype)
            out += 1


def gather(sums, after, steps=2, time=3):
    inputs, in_specs, out_shape, out_specs, plan = [], [], [], [], []
    for arrays, count, outs in sums:
        cols = arrays[0].shape[-1]
        rows = arrays[0].size // cols // count
        plan.append((len(arrays), tuple(parts for parts, _ in outs)))
        for a in arrays:
            inputs.append(a.reshape(count, rows, cols))
            in_specs.append(pl.BlockSpec((count, rows // steps, cols), lambda i: (0, i, 0)))
        for parts, kind in outs:
            out_shape.append(jax.ShapeDtypeStruct((len(parts), rows, cols), kind))
            out_specs.append(pl.BlockSpec((len(parts), rows // steps, cols), lambda i: (0, i, 0)))
    outs = pl.pallas_call(
        functools.partial(gather_kernel, plan),
        grid=(steps,), in_specs=[*in_specs, pl.BlockSpec(memory_space=pl.ANY)], out_specs=out_specs,
        out_shape=out_shape, compiler_params=params(14), cost_estimate=cost(time), name="gather",
    )(*inputs, after)
    made = []
    for _, parts in plan:
        made.append(outs[: len(parts)])
        outs = outs[len(parts) :]
    return made


def join_kernel(a_ref, a_came_ref, b_ref, b_came_ref, _, a_keep_ref, b_keep_ref, send_ref):
    start = 0
    for ref, came_ref, keep_ref in ((a_ref, a_came_ref, a_keep_ref), (b_ref, b_came_ref, b_keep_ref)):
        total = ref[...].astype(F32) + came_ref[...].astype(F32)
        rows = total.shape[1]
        keep_ref[...] = total[0]
        send_ref[start : start + rows, :] = total[1].astype(BF)
        start += rows


def join(a, b, after):
    inputs, out_shape = [], []
    for arrays in (a, b):
        cols = arrays[0].shape[-1]
        rows = arrays[0].size // cols // 2
        inputs += [r.reshape(2, rows, cols) for r in arrays]
        out_shape.append(jax.ShapeDtypeStruct((rows, cols), F32))
    out_shape.append(jax.ShapeDtypeStruct((sum(o.shape[0] for o in out_shape), cols), BF))
    vmem = pl.BlockSpec(memory_space=pltpu.VMEM)
    return pl.pallas_call(
        join_kernel,
        in_specs=[*[vmem] * 4, pl.BlockSpec(memory_space=pl.ANY)], out_specs=[vmem] * 3, out_shape=out_shape,
        compiler_params=params(8), cost_estimate=cost(3), name="join",
    )(*inputs, after)


def finish_kernel(own_ref, *refs):
    read = lambda ref: ref[0].astype(F32)
    exp_ref, in1_ref, both_ref = refs[2:5]
    tall = exp_ref.shape[0]
    red = read(refs[0]) + read(refs[1])
    exp = exp_ref[...] + both_ref[:tall, :].astype(F32)
    in1 = in1_ref[...] + both_ref[tall:, :].astype(F32)
    in2 = (read(refs[5]) + read(refs[6])) + (read(refs[7]) + read(refs[8]))
    refs = refs[9:]
    inp_ref, out_ref, exp_ref, red_ref, vec_ref, sq_ref = refs[1:]
    rows = in1.shape[0]
    vec = in2[rows : rows + vec_ref.shape[0], : vec_ref.shape[1]]
    vec_ref[...] = vec
    in2 = in2[:rows]
    even = jnp.concatenate([in1[:, :128], in2[:, :128], in1[:, 128:], in2[:, 128:]], axis=1)
    odd = jnp.concatenate([in2[:, :128], in1[:, :256], in2[:, 128:], in1[:, 256:]], axis=1)
    odd = pltpu.roll(odd, odd.shape[1] - HD, axis=1)
    inp = jnp.where((own_ref[0] & 1) == 1, odd, even)[:, : inp_ref.shape[1]]
    tall = exp_ref.shape[0]
    out = exp[tall:, :]
    half = out_ref.shape[1]
    out = jnp.concatenate([out[:, :half], pltpu.roll(out, half, axis=1)[:, :half]], axis=0)
    inp_ref[...] = inp
    out_ref[...] = out
    exp_ref[...] = exp[:tall, :]
    red_ref[...] = red
    squares = jnp.zeros((1, 1), F32)
    for g in (inp, out, exp[:tall, :], red, vec):
        squares = squares + jnp.sum(jnp.sum(g * g, axis=0, keepdims=True), axis=1, keepdims=True)
    sq_ref[...] = jnp.broadcast_to(squares, sq_ref.shape)


def finish(own, red, others, in2, after):
    piece = others[1].shape[0]
    tall = others[0].shape[0] - piece // 2
    vmem = pl.BlockSpec(memory_space=pltpu.VMEM)
    inputs = [*red, *others, *in2]
    return pl.pallas_call(
        finish_kernel,
        in_specs=[
            pl.BlockSpec(memory_space=pltpu.SMEM), *[vmem] * len(inputs), pl.BlockSpec(memory_space=pl.ANY)
        ],
        out_specs=[vmem] * 6,
        out_shape=[
            jax.ShapeDtypeStruct((piece, 9 * HD), F32),
            jax.ShapeDtypeStruct((piece, 3 * HD), F32),
            jax.ShapeDtypeStruct((tall, others[0].shape[1]), F32),
            jax.ShapeDtypeStruct(red[0].shape[1:], F32),
            jax.ShapeDtypeStruct((3, piece), F32),
            jax.ShapeDtypeStruct((8, LANES), F32),
        ],
        compiler_params=params(8), cost_estimate=cost(3), name="finish",
    )(own, *inputs, after)


def adam_step(master, moment_one, moment_two, gradient, step_rate, decay_weight):
    new_one = 0.9 * moment_one + 0.1 * gradient
    new_two = 0.999 * moment_two + 0.001 * gradient * gradient
    corrected_one = new_one / (1.0 - 0.9**STEP)
    corrected_two = new_two / (1.0 - 0.999**STEP)
    new_master = master - step_rate * (
        corrected_one / (jnp.sqrt(corrected_two) + 1e-08) + decay_weight * master
    )
    return (new_one, new_two, new_master, new_master.astype(BF))


def adam_kernel(rates, turned, squares_ref, *refs):
    n = len(rates)
    ins, outs = refs[: 4 * n], refs[4 * n :]
    norm = jnp.sqrt(squares_ref[0:1, 0:1])
    outs[0][...] = norm
    factor = 1.0 / jnp.maximum(norm, 1.0)
    for a in range(n):
        master, one, two, grad = (r[...] for r in ins[4 * a : 4 * a + 4])
        if turned[a]:
            grad = grad.T
        made = adam_step(master, one, two, grad * factor, rates[a][0], rates[a][1])
        for b in range(4):
            outs[1 + 4 * a + b][...] = made[b]


def adam_all(squares, states, grads, rates, turned):
    inputs, out_shape = [squares], [jax.ShapeDtypeStruct((1, 1), F32)]
    for state, grad in zip(states, grads):
        inputs += [*state, grad]
        shape = state[0].shape
        out_shape += [jax.ShapeDtypeStruct(shape, F32)] * 3 + [jax.ShapeDtypeStruct(shape, BF)]
    vmem = pl.BlockSpec(memory_space=pltpu.VMEM)
    return pl.pallas_call(
        functools.partial(adam_kernel, rates, turned),
        in_specs=[vmem] * len(inputs), out_specs=[vmem] * len(out_shape), out_shape=out_shape,
        compiler_params=params(16), cost_estimate=cost(5), name="adam",
    )(*inputs)


def mover(dp, seq):
    def move(value, bits_d, bits_s):
        pairs = [(d * seq + s, (d ^ bits_d) * seq + (s ^ bits_s)) for d in range(dp) for s in range(seq)]
        return lax.ppermute(value, AXES, pairs)

    return move


def tree_sum(move, value, token):
    value = value + move(value, 0, 1)
    value = (value + move(value, 2, 0)) + (move(value, 4, 0) + move(value, 6, 0))
    return (value + move(value, 0, 2)) + (move(value, 1, 0) + move(value, 1, 2)) + token


def spread_out(move, parts):
    return [parts[0], *(move(parts[b], 2 * b, 0) for b in (1, 2, 3))]


def plane(move, parts):
    return [parts[0], move(parts[1], 1, 0), move(parts[2], 0, 2), move(parts[3], 1, 2)]


def scatter_plain(parts, dim):
    part = lax.psum_scatter(parts, "seq", scatter_dimension=0, tiled=True)[0].astype(F32)
    return lax.psum_scatter(part, "dp", scatter_dimension=dim, tiled=True)


def in_order(kept, sent):
    parts = jnp.stack([kept, sent], axis=1)
    rows, cols = parts.shape[-2:]
    return parts.reshape(4, 2, 4, rows, cols).swapaxes(1, 2).reshape(4, 8 * rows, cols)


HALVES = tuple((parts, BF) for parts in ((0, 2), (4, 6), (1, 5), (3, 7)))
PAIR = (((0,), BF), ((1,), BF))
QUARTERS = tuple(((part,), BF) for part in range(4))
ONE = (((0,), BF),)
Z_HALVES = (((0, 1), BF), ((2, 3), BF))


def both_ways(move, cut):
    y_keep, y_send, x_keep, x_send = cut
    return (y_keep, move(y_send, 0, 2)), (x_keep, move(x_send, 1, 0))


def turned_ways(move, y_cut, x_cut):
    return (y_cut[0], move(y_cut[1], 1, 0)), (x_cut[0], move(x_cut[1], 0, 2))


def reduce_fast(move, kept_of, back, behind_of, input_weight, red_s, vec1):
    red_c = move(red_s, 0, 1)
    red_k, *turned = kept_of()
    (red,) = gather([((red_k, red_c), 8, HALVES)], red_k)
    red_y, red_x = both_ways(move, red)

    gf, grad_mixed, exp_s, exp_k, vec2 = behind_of(red[0], turned)
    exp_c = move(exp_s, 0, 1)
    red_y, red_x = gather([(red_y, 2, PAIR), (red_x, 2, PAIR)], vec2, time=12)
    red_y, red_x = turned_ways(move, red_y, red_x)
    (exp,) = gather([((exp_k, exp_c), 8, HALVES)], red_y[0])
    exp_y, exp_x = both_ways(move, exp)

    dq0, dkv0, vb0, gw = back(0, CALLS[0], grad_mixed, exp[0], last=False)
    (red_k,), (red_s,) = gather([(red_y, 1, ONE), (red_x, 1, ONE)], vb0)
    red = red_k, move(red_s, 4, 0)

    dq1, dkv1, vb1, in_s1, in_k1 = back(0, CALLS[1], grad_mixed, red_k, gw=gw, time=1)
    in_c1 = move(in_s1, 0, 1)
    exp_y, exp_x = gather([(exp_y, 2, PAIR), (exp_x, 2, PAIR)], vb1)
    exp_y, exp_x = turned_ways(move, exp_y, exp_x)

    gx, dx = frames_back(input_weight, gf, exp_y[0], CALLS[:2], (dq0, dq1), (dkv0, dkv1))
    (exp_k,), (exp_s,), in1, (red_k, red_s) = gather(
        [(exp_y, 1, ONE), (exp_x, 1, ONE), ((in_k1, in_c1), 4, QUARTERS), (red, 2, PAIR)], gx
    )
    exp = exp_k, move(exp_s, 4, 0)
    in1 = plane(move, in1)
    red = red_k, move(red_s, 2, 0)

    dq2, dkv2, vb2, in_s2, in_k2 = back(1, CALLS[2], grad_mixed, exp_k, vecs=(vec1, vec2, vb0, vb1))
    in_c2 = move(in_s2, 0, 1)
    ((in1_k, in1_s),) = gather([(in1, 4, Z_HALVES)], vb2, 1)
    in1 = in1_k, move(in1_s, 4, 0)
    (in2,) = gather([((in_k2, in_c2), 4, QUARTERS)], in1_k, 1)
    in2 = plane(move, in2)

    gx, dx_s, dx_k = frames_back(input_weight, gx, in2[0], CALLS[2:], (dq2,), (dkv2,), dx)
    dx_c = move(dx_s, 0, 1)
    exp_k, in1_k, both_s = join(exp, in1, gx)
    both_c = move(both_s, 2, 0)
    (in2,) = gather([(in2, 4, QUARTERS)], exp_k, 1)
    in2 = spread_out(move, in2)
    ((dx_k, dx_s),) = gather([((dx_k, dx_c), 2, (((0,), F32), ((1,), BF)))], in2[0])
    return red, (exp_k, in1_k, both_c), in2, gx, (dx_k, move(dx_s, 0, 2))


def reduce_plain(move, kept_of, back, behind_of, input_weight, red_s, vec1):
    red_k, *turned = kept_of()
    gf, grad_mixed, exp_s, exp_k, vec2 = behind_of(red_k, turned)
    dq0, dkv0, vb0, gw = back(0, CALLS[0], grad_mixed, vec2, last=False)
    dq1, dkv1, vb1, in_s1, in_k1 = back(0, CALLS[1], grad_mixed, vb0, gw=gw)
    dq2, dkv2, vb2, in_s2, in_k2 = back(1, CALLS[2], grad_mixed, vb1, vecs=(vec1, vec2, vb0, vb1))
    gx, dx = frames_back(input_weight, gf, vb2, CALLS[:2], (dq0, dq1), (dkv0, dkv1))
    gx, dx_s, dx_k = frames_back(input_weight, gx, vb2, CALLS[2:], (dq2,), (dkv2,), dx)
    ((dx_keep, dx_send),) = gather([((dx_k, move(dx_s, 0, 1)), 2, (((0,), F32), ((1,), BF)))], vb2)
    dx = dx_keep, move(dx_send, 0, 2)
    red = scatter_plain(in_order(red_k, red_s), 0)
    in1 = scatter_plain(in_order(in_k1, in_s1), 0)
    both = in_order(in_k2, in_s2)
    both = both.reshape(4, 8, -1, both.shape[-1])
    piece = in_k1.shape[2]
    in2 = scatter_plain(both[:, :, :piece].reshape(4, 8 * piece, -1), 0)
    vec = scatter_plain(both[:, :, piece : piece + 3, :piece].swapaxes(1, 2).reshape(4, 3, -1), 1)
    both = jnp.stack([exp_k, exp_s], axis=1).transpose(0, 1, 3, 2, 4, 5)
    tall, wide = both.shape[-2] - piece // 2, both.shape[-1]
    both = both.reshape(4, 8, -1, wide)
    exp = scatter_plain(both[:, :, :tall].swapaxes(1, 2).reshape(4, tall, 8 * wide), 1)
    out = both[:, :, tall:].reshape(4, 8, piece // 2, 2, wide // 2).swapaxes(2, 3)
    out = scatter_plain(out.reshape(4, 8 * piece, wide // 2), 0)
    even = jnp.concatenate([in1[:, :128], in2[:, :128], in1[:, 128:], in2[:, 128:192]], axis=1)
    odd = jnp.concatenate([in2[:, 64:128], in1[:, :256], in2[:, 128:], in1[:, 256:]], axis=1)
    inp = jnp.where(lax.axis_index("seq") % 2 == 1, odd, even)
    squares = sum(jnp.sum(g * g) for g in (inp, out, exp, red, vec))
    squares = lax.psum(jnp.full((8, LANES), squares, F32), AXES)
    return inp, out, exp, red, vec, squares, gx, dx


def local(
    frames, cotangent, lengths,
    input_weight, output_weight, expand_weight, reduce_weight, vector_copy,
    *states,
):
    rows, width = frames.shape
    seq, dp = lax.axis_size("seq"), lax.axis_size("dp")
    move = mover(dp, seq)
    own_s, own_d = lax.axis_index("seq"), lax.axis_index("dp")
    fast = dp == 8

    across = move(frames, 0, 2)
    near = move(frames, 0, 1)
    own = jnp.stack([own_s, own_d]).astype(jnp.int32) if fast else jnp.zeros((2,), jnp.int32)

    e0, k0, v0, xt0, q, *stats, qhot, vectors = attend(lengths, (frames, near), input_weight, vector_copy)
    across = pass_on(across, stats[0])
    far = move(across, 0, 1)
    rest = qhot, q, *stats, *project(across, input_weight, vectors, stats[0])
    e1, k1, v1, xt1, mixed, rinv0, rinv1 = attend(lengths, (far,), input_weight, vectors, rest)
    halves = (e0, k0, v0, rinv0, xt0), (e1, k1, v1, rinv1, xt1)
    layer, act, slope, norm1, inv1, hl, gs, gb, gbt, red_s, vec1 = ahead(
        own, mixed, frames, cotangent, qhot, output_weight, expand_weight, reduce_weight, vectors
    )

    def kept_of():
        return reduce_kept(own, gbt, act, hl, mixed)

    def behind_of(after, turned):
        return behind(
            own, slope, gb, gs, norm1, inv1, *turned, output_weight, expand_weight, reduce_weight, vectors, after
        )

    def back(group, pairs, grad_mixed, after, **more):
        return attend_back(group, pairs, own, q, grad_mixed, mixed, halves, after, **more)

    if fast:
        red, others, in2, gx, dx = reduce_fast(move, kept_of, back, behind_of, input_weight, red_s, vec1)
        inp, out, exp, red, vec, squares = finish(own, red, others, in2, dx[0])
        frames_gradient, token = frames_end(gx, *dx)
        squares = tree_sum(move, squares, token)
    else:
        inp, out, exp, red, vec, squares, gx, dx = reduce_plain(
            move, kept_of, back, behind_of, input_weight, red_s, vec1
        )
        frames_gradient, token = frames_end(gx, *dx)
        squares = squares + token

    grads = [inp, out, exp, red, vec]
    masters, firsts, seconds = (list(states[i : i + 5]) for i in (0, 5, 10))
    for group in (masters, firsts, seconds):
        group[3] = group[3].T
    hidden = expand_weight.shape[1]
    wide, narrow = 2.0 * width**-0.5, 2.0 * hidden**-0.5
    norm, *made = adam_all(
        squares, list(zip(masters, firsts, seconds)), grads,
        ((wide, 0.01), (wide, 0.01), (wide, 0.01), (narrow, 0.01), (0.5, 0.0)),
        (False, True, False, False, False),
    )
    made[12:16] = [m.T for m in made[12:16]]
    return (layer, frames_gradient, norm.reshape(()), *made)


def solution(mesh):
    tokens, whole = P(("dp", "seq"), None), P()
    state = (P("dp", "seq"), *(P("seq", "dp"),) * 4)
    outs = tuple(s for s in state for _ in range(4))
    return jax.shard_map(
        local,
        mesh=mesh,
        in_specs=(tokens, tokens, P("dp", None), *(whole,) * 5, *state * 3),
        out_specs=(tokens, tokens, whole, *outs),
        check_vma=False,
    )
```

```python
import functools

import jax
import jax.numpy as jnp
from jax import lax
from jax.experimental import pallas as pl
from jax.experimental.pallas import tpu as pltpu
from jax.sharding import PartitionSpec as P

HD = 64
STEP = 10
LANES = 128
NORM_EPS = 1e-05
MASK = -float(2**30)
BF = jnp.bfloat16
F32 = jnp.float32
AXES = ("dp", "seq")

PLACES = (
    {
        0: ((0, 0, 0), (1, 1, 1), (2, 2, 2)),
        2: ((0, 0, 1), (1, 1, 2), (2, 3, 0)),
        3: ((0, 0, 2), (1, 2, 0), (2, 3, 1)),
        5: ((0, 1, 0), (1, 2, 1), (2, 3, 2)),
    },
    {
        1: ((0, 0, 0), (1, 1, 1), (2, 2, 1), (2, 3, 0)),
        4: ((0, 0, 1), (0, 1, 0), (1, 2, 0), (2, 3, 1)),
    },
)
WIDTHS = (3 * LANES, 2 * LANES)
CALLS = ((0, 2), (3, 5), (1, 4))


def params(mebibytes):
    return pltpu.CompilerParams(vmem_limit_bytes=mebibytes * 2**20)


def cost(microseconds):
    return pl.CostEstimate(flops=int(microseconds * 4.4e9), bytes_accessed=0, transcendentals=0)


def in_hbm(array):
    return pltpu.with_memory_space_constraint(array, pltpu.HBM)


def dot(a, b):
    return lax.dot_general(a, b, (((1,), (0,)), ((), ())), preferred_element_type=F32)


def dot_t(a, b):
    return lax.dot_general(a, b, (((1,), (1,)), ((), ())), preferred_element_type=F32)


def softmax_half(q, k, v, kmask, qhot, e_ref):
    rows, wide = q.shape
    pairs = wide // LANES
    low = lax.broadcasted_iota(jnp.int32, (rows, LANES), 1) < HD
    part = lambda a, p: a[:, p * LANES : (p + 1) * LANES]
    keys = [jnp.concatenate([part(k, p), kmask], axis=1) for p in range(pairs)]
    values = [jnp.concatenate([part(v, p), jnp.ones((v.shape[0], LANES), BF)], axis=1) for p in range(pairs)]

    def score(head):
        qh = part(q, head // 2)
        qh = jnp.where(low if head % 2 == 0 else jnp.logical_not(low), qh, jnp.zeros_like(qh))
        return dot_t(jnp.concatenate([qh, qhot], axis=1), keys[head // 2])

    following = score(0)
    done, results = [], []
    for head in range(2 * pairs):
        scores = following
        if head + 1 < 2 * pairs:
            following = score(head + 1)
        top = jnp.max(scores, axis=1, keepdims=True)
        e = jnp.exp(scores - top).astype(BF)
        e_ref[head] = e
        both = dot(e, values[head // 2])
        done.append((top, both[:, LANES:], both[:, :LANES]))
        if head % 2 == 1:
            results.append([jnp.where(low, a, b) for a, b in zip(*done[-2:])])
    return results


def segment_of(lengths_ref, rows, first):
    own = lax.axis_index("seq")
    at = lax.broadcasted_iota(jnp.int32, (rows, LANES), 0)
    half = rows // 2
    place = jnp.where(at < half, (first ^ own) * half + at, ((first + 1) ^ own) * half + at - half)
    segments, end = jnp.zeros((rows, LANES), jnp.int32), 0
    for n in range(lengths_ref.shape[1]):
        end = end + lengths_ref[0, n]
        segments = segments + (place >= end).astype(jnp.int32)
    return segments


def key_mask(lengths_ref, rows, first):
    lanes = lax.broadcasted_iota(jnp.int32, (rows, LANES), 1)
    segments = segment_of(lengths_ref, rows, first)
    return jnp.where((segments == lanes) | (lanes > 3), 0.0, MASK).astype(BF)


def project_half(x_ref, blocks, wk_ref, wv_ref, vec_ref, k_ref, v_ref, xt_ref):
    step = pl.program_id(0)
    wide = wk_ref.shape[1]
    rows = blocks[0].shape[0]

    @pl.when(step == 0)
    def _():
        for i, ref in enumerate(blocks):
            x_ref[i * rows : (i + 1) * rows, :] = ref[...]

    xt_ref[...] = x_ref[:, pl.ds(pl.multiple_of(step * wide, LANES), wide)].T
    k = dot(x_ref[...], wk_ref[...]).astype(BF)
    v = (dot(x_ref[...], wv_ref[...]) + vec_ref[1:2, :].astype(F32)).astype(BF)
    k_ref[...] = k
    v_ref[...] = v
    return k, v


def attend_near_kernel(
    lengths_ref, x0_ref, x1_ref, wk_ref, wv_ref, vec_ref, wq_ref,
    e_ref, k_ref, v_ref, xt_ref, q_ref, top_ref, sum_ref, out_ref, qhot_ref, wide_ref, x_ref, kmask,
):
    rows, slab = q_ref.shape[0], x_ref.shape[0]

    @pl.when(pl.program_id(0) == 0)
    def _():
        kmask[...] = key_mask(lengths_ref, slab, 0)
        lanes = lax.broadcasted_iota(jnp.int32, (rows, LANES), 1)
        qhot_ref[...] = (segment_of(lengths_ref, slab, 0)[:rows] == lanes).astype(F32).astype(BF)

    wide_ref[...] = vec_ref[...].astype(F32)
    k, v = project_half(x_ref, (x0_ref, x1_ref), wk_ref, wv_ref, vec_ref, k_ref, v_ref, xt_ref)
    q = (dot(x_ref[:rows, :], wq_ref[...]) + vec_ref[0:1, :].astype(F32)).astype(BF)
    q = q * jnp.asarray(HD**-0.5, BF)
    q_ref[...] = q
    for p, made in enumerate(softmax_half(q, k, v, kmask[...], qhot_ref[...], e_ref)):
        for ref, value in zip((top_ref, sum_ref, out_ref), made):
            ref[:, p * LANES : (p + 1) * LANES] = value


def pass_kernel(x_ref, _, out_ref):
    out_ref[...] = x_ref[...]


def pass_on(x, after):
    whole = pl.BlockSpec(x.shape, lambda i: (0, 0))
    return pl.pallas_call(
        pass_kernel,
        grid=(1,), in_specs=[whole, pl.BlockSpec(memory_space=pl.ANY)], out_specs=whole,
        out_shape=jax.ShapeDtypeStruct(x.shape, x.dtype),
        compiler_params=params(6), cost_estimate=cost(1), name="pass_on",
    )(x, after)


def project_kernel(x_ref, xp_ref, wk_ref, wv_ref, vec_ref, _, k_ref, v_ref, xt_ref):
    xt_ref[...] = xp_ref[...].T
    k_ref[...] = dot(x_ref[...], wk_ref[...]).astype(BF)
    v_ref[...] = (dot(x_ref[...], wv_ref[...]) + vec_ref[1:2, :]).astype(BF)


def project(x, input_weight, vectors, after):
    rows, width = x.shape
    wide = 3 * LANES
    steps = width // wide
    weight = in_hbm(input_weight)
    cols = lambda r, off=0: pl.BlockSpec((r, wide), lambda p: (0, p + off))
    down = pl.BlockSpec((wide, rows), lambda p: (p, 0))
    return pl.pallas_call(
        project_kernel,
        grid=(steps,),
        in_specs=[
            pl.BlockSpec((rows, width), lambda p: (0, 0)), cols(rows), cols(width, steps), cols(width, 2 * steps),
            cols(vectors.shape[0]), pl.BlockSpec(memory_space=pl.ANY),
        ],
        out_specs=[cols(rows), cols(rows), down],
        out_shape=[jax.ShapeDtypeStruct((rows, width), BF)] * 2 + [jax.ShapeDtypeStruct((width, rows), BF)],
        compiler_params=params(12), cost_estimate=cost(5),
        name="project",
    )(x, x, weight, weight, vectors, after)


def attend_far_kernel(
    lengths_ref, x0_ref, wk_ref, wv_ref, vec_ref, qhot_ref, q_ref, top_ref, sum_ref, out_ref, k0_ref, v0_ref, xt0_ref,
    e_ref, k_ref, v_ref, xt_ref, mixed_ref, near_ref, far_ref, x_ref, kmask,
):
    rows = x0_ref.shape[0]

    @pl.when(pl.program_id(0) == 0)
    def _():
        kmask[...] = key_mask(lengths_ref, 2 * rows, 2)

    project_half(
        x_ref, (x0_ref,), wk_ref, wv_ref, vec_ref, k_ref.at[rows:, :], v_ref.at[rows:, :], xt_ref.at[:, rows:]
    )
    k_ref[:rows, :] = k0_ref[...]
    v_ref[:rows, :] = v0_ref[...]
    xt_ref[:, :rows] = xt0_ref[...]
    k, v = k_ref[...], v_ref[...]
    for p, (top, total, out) in enumerate(softmax_half(q_ref[...], k, v, kmask[...], qhot_ref[...], e_ref)):
        span = slice(p * LANES, (p + 1) * LANES)
        both = jnp.maximum(top, top_ref[:, span])
        near, far = jnp.exp(top_ref[:, span] - both), jnp.exp(top - both)
        rinv = 1.0 / (near * sum_ref[:, span] + far * total)
        near, far = near * rinv, far * rinv
        near_ref[:, span] = near
        far_ref[:, span] = far
        mixed_ref[:, span] = (out_ref[:, span] * near + out * far).astype(BF)


def attend(lengths, blocks, input_weight, vectors, near=()):
    rows, width = blocks[0].shape
    slab = 2 * rows
    wide = 2 * LANES
    steps = width // wide
    weight = in_hbm(input_weight)
    full = lambda shape: pl.BlockSpec(shape, lambda p: (0,) * len(shape))
    cols = lambda r, off=0: pl.BlockSpec((r, wide), lambda p: (0, p + off))
    down = lambda c: pl.BlockSpec((wide, c), lambda p: (p, 0))
    inputs = [lengths, *blocks, weight, weight, vectors]
    in_specs = [
        pl.BlockSpec(memory_space=pltpu.SMEM), *(full(b.shape) for b in blocks), cols(width, steps), cols(width, 2 * steps), cols(vectors.shape[0]),
    ]
    out_specs = [
        pl.BlockSpec((wide // HD, rows, slab), lambda p: (p, 0, 0)), cols(slab), cols(slab), down(slab),
    ]
    out_shape = [
        pltpu.HBM((width // HD, rows, slab), BF), pltpu.HBM((slab, width), BF), pltpu.HBM((slab, width), BF),
        pltpu.HBM((width, slab), BF),
    ]
    if near:
        inputs += near
        in_specs += [full((rows, LANES)), *[cols(rows)] * 6, down(rows)]
        out_specs += [cols(rows)] * 3
        out_shape += [jax.ShapeDtypeStruct((rows, width), BF), *[pltpu.HBM((rows, width), F32)] * 2]
    else:
        inputs[1] = in_hbm(inputs[1])
        inputs.append(weight)
        in_specs.append(cols(width))
        out_specs += [*[cols(rows)] * 4, full((rows, LANES)), cols(vectors.shape[0])]
        out_shape += [
            jax.ShapeDtypeStruct((rows, width), BF), *[jax.ShapeDtypeStruct((rows, width), F32)] * 3,
            jax.ShapeDtypeStruct((rows, LANES), BF), jax.ShapeDtypeStruct(vectors.shape, F32),
        ]
    return pl.pallas_call(
        attend_far_kernel if near else attend_near_kernel,
        grid=(steps,), in_specs=in_specs, out_specs=out_specs,
        scratch_shapes=[pltpu.VMEM((rows * len(blocks), width), BF), pltpu.VMEM((slab, LANES), BF)],
        out_shape=out_shape,
        compiler_params=params(28), cost_estimate=cost(11),
        name="attend",
    )(*inputs)


def spot(d, own_d):
    rel = d ^ own_d
    return (rel & 1) * 4 + (rel >> 1)


def turn(j):
    return jnp.where(j < 2, 2 * j + 1, 2 * (j - 2))


def by_rows(rows, body, blocks=4):
    block = rows // blocks

    def step(i, carry):
        body(pl.ds(pl.multiple_of(i * block, block), block))
        return carry

    lax.fori_loop(0, blocks, step, 0)


def store_rows(ref, block, own_d):
    piece = block.shape[0] // 8
    for d in range(8):
        ref[0, spot(d, own_d)] = block[d * piece : (d + 1) * piece, :]


def reduce_kernel(own_ref, gbt_ref, act_ref, hl_ref, mixed_ref, rk_ref, hlt_ref, mt_ref):
    store_rows(rk_ref, dot(gbt_ref[...], act_ref[0]).astype(BF), own_ref[1])

    @pl.when(pl.program_id(0) == 0)
    def _():
        hlt_ref[...] = hl_ref[...].T
        mt_ref[...] = mixed_ref[...].T


def reduce_kept(own, gbt, act, hl, mixed):
    width, rows = gbt.shape
    chunks, _, cut = act.shape
    full = lambda a: pl.BlockSpec(a, lambda j, own: (0, 0))
    return pl.pallas_call(
        reduce_kernel,
        grid_spec=pltpu.PrefetchScalarGridSpec(
            num_scalar_prefetch=1,
            grid=(2,),
            in_specs=[
                full((width, rows)), pl.BlockSpec((1, rows, cut), lambda j, own: (j + 2, 0, 0)),
                full((rows, width)), full((rows, width)),
            ],
            out_specs=[
                pl.BlockSpec((1, 8, width // 8, cut), lambda j, own: (j, 0, 0, 0)), full((width, rows)),
                full((width, rows)),
            ],
        ),
        out_shape=[
            jax.ShapeDtypeStruct((2, 8, width // 8, cut), BF),
            jax.ShapeDtypeStruct((width, rows), BF), jax.ShapeDtypeStruct((width, rows), BF),
        ],
        compiler_params=params(12), cost_estimate=cost(5),
        name="reduce_kept",
    )(own, gbt, act, hl, mixed)


def ahead_kernel(
    own_ref, mixed_ref, x_ref, cot_ref, qhot_ref, wo_ref, we_ref, wr_ref, vec_ref,
    layer_ref, act_ref, slope_ref, norm1_ref, inv1_ref, hl, gs_ref, gb_ref, gbt, rs_ref, vg_ref,
    act, hid, acc,
):
    step = pl.program_id(0)
    own_s, own_d = own_ref[0], own_ref[1]
    rows, width = x_ref.shape
    chunks = act.shape[0]
    j = lax.rem(step, chunks)
    shard = turn(j) ^ own_s
    row = lambda i: vec_ref[i : i + 1, :]

    @pl.when(step == 0)
    def _():
        acc[...] = dot(mixed_ref[...], wo_ref[...])

        def first_norm(at):
            z = x_ref[at, :].astype(F32) + acc[at, :] + row(2)
            center = z - jnp.mean(z, axis=1, keepdims=True)
            inverse = lax.rsqrt(jnp.mean(center * center, axis=1, keepdims=True) + NORM_EPS)
            normed = center * inverse
            hidden = normed * row(3) + row(4)
            hid[at, :] = hidden
            norm1_ref[at, :] = normed
            inv1_ref[at, :] = jnp.broadcast_to(inverse, (z.shape[0], LANES))
            hl[at, :] = hidden.astype(BF)

        by_rows(rows, first_norm, 2)
        vg_ref[...] = jnp.zeros_like(vg_ref)

    @pl.when(step < chunks)
    def _():
        pre = dot(hl[...], we_ref[...]) + vec_ref[pl.ds(8 + shard, 1), :]
        cdf = 0.5 * (1.0 + lax.erf(pre * 0.7071067811865476))
        density = jnp.exp(-0.5 * pre * pre) * 0.3989422804014327
        low = (pre * cdf).astype(BF)
        act[j] = low
        act_ref[0] = low
        slope_ref[0] = cdf + pre * density
        part = dot(low, wr_ref[...])

        @pl.when(step == 0)
        def _():
            acc[...] = part

        @pl.when(step > 0)
        def _():
            acc[...] += part

    @pl.when(step == chunks - 1)
    def _():
        def second_norm(at):
            z = hid[at, :] + acc[at, :] + row(5)
            center = z - jnp.mean(z, axis=1, keepdims=True)
            inverse = lax.rsqrt(jnp.mean(center * center, axis=1, keepdims=True) + NORM_EPS)
            normed = center * inverse
            valid = 1.0 - qhot_ref[at, :][:, 3:4].astype(F32)
            layer_ref[at, :] = ((normed * row(6) + row(7)) * valid).astype(BF)
            gy = cot_ref[at, :].astype(F32) * valid
            e = gy * row(6)
            grad = e - jnp.mean(e, axis=1, keepdims=True)
            grad = (grad - normed * jnp.mean(e * normed, axis=1, keepdims=True)) * inverse
            low = grad.astype(BF)
            vg_ref[5:6, :] += jnp.sum(low.astype(F32), axis=0, keepdims=True)
            vg_ref[6:7, :] += jnp.sum(gy * normed, axis=0, keepdims=True)
            vg_ref[7:8, :] += jnp.sum(gy, axis=0, keepdims=True)
            gb_ref[at, :] = low
            gs_ref[at, :] = grad

        by_rows(rows, second_norm, 2)
        gbt[...] = gb_ref[...].T

    @pl.when(step >= chunks)
    def _():
        store_rows(rs_ref, dot(gbt[...], act[j]).astype(BF), own_d)


def ahead(own, mixed, frames, cotangent, qhot, output_weight, expand_weight, reduce_weight, vectors):
    rows, width = frames.shape
    hidden = expand_weight.shape[1]
    chunks = 4
    cut = hidden // chunks
    piece = width // 8
    first = lambda s: jnp.minimum(s, chunks - 1)
    shard_of = lambda s, own: turn(first(s)) ^ own[0]
    full = lambda shape: pl.BlockSpec(shape, lambda s, own: (0,) * len(shape))
    chunk = pl.BlockSpec((1, rows, cut), lambda s, own: (first(s), 0, 0))
    return pl.pallas_call(
        ahead_kernel,
        grid_spec=pltpu.PrefetchScalarGridSpec(
            num_scalar_prefetch=1,
            grid=(chunks + 2,),
            in_specs=[
                full(mixed.shape), full(frames.shape), full(cotangent.shape), full(qhot.shape),
                full(output_weight.shape),
                pl.BlockSpec((width, cut), lambda s, own: (0, shard_of(s, own))),
                pl.BlockSpec((cut, width), lambda s, own: (shard_of(s, own), 0)),
                full(vectors.shape),
            ],
            out_specs=[
                full((rows, width)), chunk, chunk, full((rows, width)), full((rows, LANES)),
                full((rows, width)), full((rows, width)), full((rows, width)), full((width, rows)),
                pl.BlockSpec((1, 8, piece, cut), lambda s, own: (jnp.maximum(s - chunks, 0), 0, 0, 0)),
                full((16, width)),
            ],
            scratch_shapes=[
                pltpu.VMEM((chunks, rows, cut), BF),
                pltpu.VMEM((rows, width), F32),
                pltpu.VMEM((rows, width), F32),
            ],
        ),
        out_shape=[
            jax.ShapeDtypeStruct((rows, width), BF),
            jax.ShapeDtypeStruct((chunks, rows, cut), BF),
            jax.ShapeDtypeStruct((chunks, rows, cut), F32),
            jax.ShapeDtypeStruct((rows, width), F32),
            jax.ShapeDtypeStruct((rows, LANES), F32),
            jax.ShapeDtypeStruct((rows, width), BF),
            jax.ShapeDtypeStruct((rows, width), F32),
            jax.ShapeDtypeStruct((rows, width), BF),
            jax.ShapeDtypeStruct((width, rows), BF),
            jax.ShapeDtypeStruct((2, 8, piece, cut), BF),
            jax.ShapeDtypeStruct((16, width), F32),
        ],
        compiler_params=params(22), cost_estimate=cost(20),
        name="ahead",
    )(own, mixed, frames, cotangent, qhot, output_weight, expand_weight, reduce_weight, vectors)


def behind_kernel(
    own_ref, slope_ref, gb_ref, gs_ref, norm1_ref, inv1_ref, hlt_ref, mt_ref, wo_ref, we_ref, wr_ref, vec_ref, _,
    gf_ref, gm_ref, es_ref, ek_ref, vg_ref,
    acc, tmp, ga,
):
    j = pl.program_id(0)
    own_s, own_d = own_ref[0], own_ref[1]
    rows, width = gb_ref.shape
    shard = turn(j) ^ own_s
    row = lambda i: vec_ref[i : i + 1, :]
    piece, fourth = width // 8, width // 4

    @pl.when(j == 0)
    def _():
        acc[...] = gs_ref[...]
        vg_ref[...] = jnp.zeros_like(vg_ref)

    grad_act = dot_t(gb_ref[...], wr_ref[...])
    low = (grad_act * slope_ref[0]).astype(BF)
    vg_ref[pl.ds(8 + shard, 1), :] = jnp.sum(low.astype(F32), axis=0, keepdims=True)
    acc[...] += dot_t(low, we_ref[...])
    grad_e = dot(hlt_ref[...], low).astype(BF)
    tmp[...] = grad_e.reshape(tmp.shape)
    half = grad_e.shape[1] // 2
    rz = shard ^ (own_d >> 1)
    for part, ref in ((1, es_ref), (0, ek_ref)):
        for ry in range(2):
            for t in range(2):
                block = tmp[own_s ^ (2 * ry + part), :, t * half : (t + 1) * half]
                ref[ry, t ^ (own_d & 1), rz, :fourth, :] = block

    @pl.when(j == pl.num_programs(0) - 1)
    def _():
        def first_back(at):
            gy = acc[at, :]
            normed = norm1_ref[at, :]
            e = gy * row(3)
            grad = e - jnp.mean(e, axis=1, keepdims=True)
            grad = (grad - normed * jnp.mean(e * normed, axis=1, keepdims=True)) * inv1_ref[at, :][:, :1]
            gf_ref[at, :] = grad
            rounded = grad.astype(BF)
            vg_ref[2:3, :] += jnp.sum(rounded.astype(F32), axis=0, keepdims=True)
            vg_ref[3:4, :] += jnp.sum(gy * normed, axis=0, keepdims=True)
            vg_ref[4:5, :] += jnp.sum(gy, axis=0, keepdims=True)
            ga[at, :] = rounded

        by_rows(rows, first_back)
        gm_ref[...] = dot_t(ga[...], wo_ref[...]).astype(BF)
        gat = ga[...].T
        for part, ref in ((1, es_ref), (0, ek_ref)):
            for ry in range(2):
                start = pl.multiple_of((own_s ^ (2 * ry + part)) * fourth, fourth)
                out = dot_t(gat, mt_ref[pl.ds(start, fourth), :]).astype(BF)
                for d in range(8):
                    block = out[d * piece : (d + 1) * piece, :]
                    block = jnp.concatenate([block[: piece // 2], block[piece // 2 :]], axis=1)
                    ref[ry, (d & 1) ^ (own_d & 1), (d >> 1) ^ (own_d >> 1), fourth:, :] = block


def behind(own, slope, gb, gs, norm1, inv1, hlt, mt, output_weight, expand_weight, reduce_weight, vectors, after):
    rows, width = gb.shape
    hidden = expand_weight.shape[1]
    chunks = 4
    cut = hidden // chunks
    fourth, eighth = width // 4, hidden // 8
    shard_of = lambda s, own: turn(s) ^ own[0]
    full = lambda shape: pl.BlockSpec(shape, lambda s, own: (0,) * len(shape))
    spread = (2, 2, 4, fourth + width // 16, eighth)
    return pl.pallas_call(
        behind_kernel,
        grid_spec=pltpu.PrefetchScalarGridSpec(
            num_scalar_prefetch=1,
            grid=(chunks,),
            in_specs=[
                pl.BlockSpec((1, rows, cut), lambda s, own: (s, 0, 0)),
                full(gb.shape), full(gs.shape), full(norm1.shape), full(inv1.shape), full(hlt.shape), full(mt.shape),
                full(output_weight.shape),
                pl.BlockSpec((width, cut), lambda s, own: (0, shard_of(s, own))),
                pl.BlockSpec((cut, width), lambda s, own: (shard_of(s, own), 0)),
                full(vectors.shape), pl.BlockSpec(memory_space=pl.ANY),
            ],
            out_specs=[full((rows, width)), full((rows, width)), full(spread), full(spread), full((16, width))],
            scratch_shapes=[
                pltpu.VMEM((rows, width), F32), pltpu.VMEM((4, fourth, cut), BF), pltpu.VMEM((rows, width), BF),
            ],
        ),
        out_shape=[
            jax.ShapeDtypeStruct((rows, width), F32),
            jax.ShapeDtypeStruct((rows, width), BF),
            jax.ShapeDtypeStruct(spread, BF),
            jax.ShapeDtypeStruct(spread, BF),
            jax.ShapeDtypeStruct((16, width), F32),
        ],
        compiler_params=params(20), cost_estimate=cost(18),
        name="behind",
    )(own, slope, gb, gs, norm1, inv1, hlt, mt, output_weight, expand_weight, reduce_weight, vectors, after)


def back_kernel(group, pairs, first, last, own_ref, q_ref, gm_ref, mixed_ref, *rest):
    halves, rest = (rest[:5], rest[5:10]), list(rest[11:])
    gw_in_ref = None if first else rest.pop(0)
    vec_in = [rest.pop(0) for _ in range(4)] if group == 1 else []
    dq_ref, dkv_ref, vb_ref = rest[:3]
    rest = rest[3:]
    if last:
        gs_ref, gk_ref, gw, *vecs = rest
    else:
        (gw,) = rest
    i = pl.program_id(0)
    own_s, own_d = own_ref[0], own_ref[1]
    rows = q_ref.shape[0]
    q_t = q_ref[...].T
    low = lax.broadcasted_iota(jnp.int32, (rows, LANES), 1) < HD
    dqs, dkvs = [0.0, 0.0], []
    for e_ref, k_ref, v_ref, rinv_ref, _ in halves:
        k, v = k_ref[...], v_ref[...]
        gm = gm_ref[...].astype(F32) * rinv_ref[...]
        both = gm * mixed_ref[...].astype(F32)
        gm_low = gm.astype(BF)
        gm_t = gm_low.T
        dks, dvs = [], []
        for head in range(2):
            own = low if head == 0 else jnp.logical_not(low)
            span = slice(head * HD, (head + 1) * HD)
            e = e_ref[head]
            inner = jnp.sum(jnp.where(own, both, 0.0), axis=1, keepdims=True)
            grad_e = dot_t(jnp.where(own, gm_low, jnp.zeros_like(gm_low)), v)
            ds = (e.astype(F32) * (grad_e - inner)).astype(BF)
            dqs[head] = dqs[head] + dot(ds, k)
            dks.append(dot(q_t[span, :], ds))
            dvs.append(dot(gm_t[span, :], e))
        dkvs.append(jnp.concatenate([*dks, *dvs], axis=0).astype(BF))
    dq = (jnp.where(low, dqs[0], dqs[1]) * HD**-0.5).astype(BF)
    dkv = jnp.concatenate(dkvs, axis=1)
    dq_ref[...] = dq
    dkv_ref[...] = dkv
    ones = jnp.ones((8, dkv.shape[1]), BF)
    bias = jnp.concatenate(
        [jnp.sum(dq.astype(F32), axis=0, keepdims=True), dot_t(ones, dkv[LANES:, :])[0:1, :]], axis=0
    )
    vb_ref[0:2, :] = bias

    if group == 1:

        @pl.when(i == 0)
        def _():
            vecs[0][...] = vec_in[0][...] + vec_in[1][...]
            for call, ref in zip(CALLS, vec_in[2:]):
                for n, p in enumerate(call):
                    vecs[0][0:2, p * LANES : (p + 1) * LANES] = ref[0:2, n * LANES : (n + 1) * LANES]

    if not first:

        @pl.when(i == 0)
        def _():
            gw[...] = gw_in_ref[...]

    grad_q = dot(halves[0][4][:, :rows], dq).astype(BF)
    grad_kv = sum(dot_t(half[4][...], part) for half, part in zip(halves, dkvs)).astype(BF)
    piece = grad_q.shape[0] // 8
    blocks = [b.reshape(8, piece, LANES) for b in (grad_q, grad_kv[:, :LANES], grad_kv[:, LANES:])]
    for n, pair in enumerate(pairs):

        @pl.when(i == n)
        def _():
            for which, shard, place in PLACES[group][pair]:
                gw[shard, :, :piece, place * LANES : (place + 1) * LANES] = blocks[which]
            if group == 1:
                vecs[0][0:2, pair * LANES : (pair + 1) * LANES] = bias

    if last:

        @pl.when(i == len(pairs) - 1)
        def _():
            if group == 1:
                vec, tall = vecs[0][...], vecs[0].shape[1]
                for d in range(8):
                    turned = pltpu.roll(vec, (tall - piece * d) % tall, axis=1)[:, : gw.shape[3]]
                    for shard in range(4):
                        block = pltpu.roll(turned, (16 - 3 * shard) % 16, axis=0) if shard else turned
                        gw[shard, d, piece:, :] = block.astype(BF)
            for ref, part in ((gs_ref, 1), (gk_ref, 0)):
                for ry in range(2):
                    for d in range(8):
                        ref[ry, spot(d, own_d)] = gw[own_s ^ (2 * ry + part), d]


def attend_back(group, pairs, own, q, grad_mixed, mixed, halves, after, gw=None, last=True, vecs=(), time=12):
    first = gw is None
    rows, width = q.shape
    half = halves[0][1].shape[0]
    slab = 2 * half
    piece = width // 8
    span = WIDTHS[group]
    pair_of = lambda i: jnp.where(i == 0, pairs[0], pairs[1])
    full = lambda shape: pl.BlockSpec(shape, lambda i, own: (0,) * len(shape))
    cols = lambda r: pl.BlockSpec((r, LANES), lambda i, own: (0, pair_of(i)))
    inputs = [q, grad_mixed, mixed]
    in_specs = [cols(rows)] * 3
    for e, k, v, rinv, x_t in halves:
        inputs += [in_hbm(e), k, v, rinv, x_t]
        in_specs += [
            pl.BlockSpec((2, rows, half), lambda i, own: (pair_of(i), 0, 0)),
            cols(half), cols(half), cols(rows), full(x_t.shape),
        ]
    inputs.append(after)
    in_specs.append(pl.BlockSpec(memory_space=pl.ANY))
    out_shape = [
        jax.ShapeDtypeStruct((rows, len(pairs) * LANES), BF),
        jax.ShapeDtypeStruct((len(pairs) * 2 * LANES, slab), BF),
        jax.ShapeDtypeStruct((8, len(pairs) * LANES), F32),
    ]
    out_specs = [
        pl.BlockSpec((rows, LANES), lambda i, own: (0, i)),
        pl.BlockSpec((2 * LANES, slab), lambda i, own: (i, 0)),
        pl.BlockSpec((8, LANES), lambda i, own: (0, i)),
    ]
    scratch = []
    whole = (4, 8, piece + (16 if vecs else 0), span)
    if not first:
        inputs.append(gw)
        in_specs.append(full(whole))
    inputs += vecs
    in_specs += [full(a.shape) for a in vecs]
    if last:
        out_shape += [jax.ShapeDtypeStruct((2, *whole[1:]), BF)] * 2
        out_specs += [full((2, *whole[1:]))] * 2
        scratch.append(pltpu.VMEM(whole, BF))
        if vecs:
            scratch.append(pltpu.VMEM((16, width), F32))
    else:
        out_shape.append(jax.ShapeDtypeStruct(whole, BF))
        out_specs.append(full(whole))
    return pl.pallas_call(
        functools.partial(back_kernel, group, pairs, first, last),
        grid_spec=pltpu.PrefetchScalarGridSpec(
            num_scalar_prefetch=1, grid=(len(pairs),), in_specs=in_specs, out_specs=out_specs, scratch_shapes=scratch
        ),
        out_shape=out_shape,
        compiler_params=params(20), cost_estimate=cost(time),
        name="attend_back",
    )(own, *inputs)


def frames_kernel(pairs, last, w_ref, gx_in_ref, after_ref, *refs):
    n = len(pairs)
    dqs, dkvs = refs[:n], refs[n : 2 * n]
    refs = list(refs[2 * n :])
    dx_ref = refs.pop(0) if last else None
    gx_ref, *outs, wkv = refs
    j = pl.program_id(0)
    width = gx_ref.shape[1]
    flat = [p for call in pairs for p in call]

    @pl.when(j == 0)
    def _():
        for i, p in enumerate(flat):
            for t in range(2):
                start = (1 + t) * width + p * LANES
                wkv[:, (2 * i + t) * LANES : (2 * i + t + 1) * LANES] = w_ref[:, start : start + LANES]
        wq = jnp.concatenate([w_ref[:, p * LANES : (p + 1) * LANES] for p in flat], axis=1)
        dq = jnp.concatenate([r[...] for r in dqs], axis=1)
        gx_ref[...] = gx_in_ref[...] + dot_t(dq, wq)

    made = dot(wkv[...], jnp.concatenate([r[...] for r in dkvs], axis=0))
    if not last:
        outs[0][0] = made
        return
    made = made + dx_ref[0]

    @pl.when(j < 2)
    def _():
        outs[0][0] = made.astype(BF)

    @pl.when(j >= 2)
    def _():
        outs[1][0] = made


def frames_back(input_weight, gx, after, pairs, dqs, dkvs, dx=None):
    rows, width = gx.shape
    last = dx is not None
    count = 2 * sum(map(len, pairs))
    full = lambda a: pl.BlockSpec(a.shape, lambda j: (0,) * a.ndim)
    column = lambda a: pl.BlockSpec((a.shape[0], rows), lambda j: (0, turn(j)))
    block = lambda pick: pl.BlockSpec((1, width, rows), lambda j: (pick(j), 0, 0))
    if last:
        out_specs = [block(lambda j: jnp.minimum(j, 1)), block(lambda j: jnp.maximum(j - 2, 0))]
        out_shape = [jax.ShapeDtypeStruct((2, width, rows), BF), jax.ShapeDtypeStruct((2, width, rows), F32)]
    else:
        out_specs = [block(lambda j: j)]
        out_shape = [jax.ShapeDtypeStruct((4, width, rows), F32)]
    return pl.pallas_call(
        functools.partial(frames_kernel, pairs, last),
        grid=(4,),
        in_specs=[
            full(input_weight), full(gx), pl.BlockSpec(memory_space=pl.ANY), *map(full, dqs), *map(column, dkvs),
            *([block(lambda j: j)] if last else []),
        ],
        out_specs=[full(gx), *out_specs],
        out_shape=[jax.ShapeDtypeStruct((rows, width), F32), *out_shape],
        scratch_shapes=[pltpu.VMEM((width, count * LANES), BF)],
        compiler_params=params(16), cost_estimate=cost(4 if last else 8),
        name="frames_back",
    )(input_weight, gx, after, *dqs, *dkvs, *([dx] if last else []))


def frames_end_kernel(gx_ref, keep_ref, came_ref, out_ref, token_ref):
    token_ref[...] = jnp.zeros_like(token_ref)
    out_ref[...] = gx_ref[...] + (keep_ref[0] + came_ref[0].astype(F32)).T


def frames_end(gx, keep, came):
    rows, width = gx.shape
    wide = 3 * LANES
    across = pl.BlockSpec((rows, wide), lambda p: (0, p))
    down = pl.BlockSpec((1, wide, rows), lambda p: (0, p, 0))
    return pl.pallas_call(
        frames_end_kernel,
        grid=(width // wide,), in_specs=[across, down, down],
        out_specs=[across, pl.BlockSpec((8, LANES), lambda p: (0, 0))],
        out_shape=[jax.ShapeDtypeStruct((rows, width), F32), jax.ShapeDtypeStruct((8, LANES), F32)], compiler_params=params(8), cost_estimate=cost(5), name="frames_end",
    )(gx, keep, came)


def gather_kernel(plan, *refs):
    start, out = 0, sum(n for n, _ in plan) + 1
    for n, outs in plan:
        ins = refs[start : start + n]
        start += n
        for parts in outs:
            for i, part in enumerate(parts):
                terms = [r[part].astype(F32) for r in ins]
                while len(terms) > 1:
                    terms = [terms[t] + terms[t + 1] for t in range(0, len(terms), 2)]
                refs[out][i] = terms[0].astype(refs[out].dtype)
            out += 1


def gather(sums, after, steps=2, time=3):
    inputs, in_specs, out_shape, out_specs, plan = [], [], [], [], []
    for arrays, count, outs in sums:
        cols = arrays[0].shape[-1]
        rows = arrays[0].size // cols // count
        plan.append((len(arrays), tuple(parts for parts, _ in outs)))
        for a in arrays:
            inputs.append(a.reshape(count, rows, cols))
            in_specs.append(pl.BlockSpec((count, rows // steps, cols), lambda i: (0, i, 0)))
        for parts, kind in outs:
            out_shape.append(jax.ShapeDtypeStruct((len(parts), rows, cols), kind))
            out_specs.append(pl.BlockSpec((len(parts), rows // steps, cols), lambda i: (0, i, 0)))
    outs = pl.pallas_call(
        functools.partial(gather_kernel, plan),
        grid=(steps,), in_specs=[*in_specs, pl.BlockSpec(memory_space=pl.ANY)], out_specs=out_specs,
        out_shape=out_shape, compiler_params=params(14), cost_estimate=cost(time), name="gather",
    )(*inputs, after)
    made = []
    for _, parts in plan:
        made.append(outs[: len(parts)])
        outs = outs[len(parts) :]
    return made


def join_kernel(a_ref, a_came_ref, b_ref, b_came_ref, _, a_keep_ref, b_keep_ref, send_ref):
    start = 0
    for ref, came_ref, keep_ref in ((a_ref, a_came_ref, a_keep_ref), (b_ref, b_came_ref, b_keep_ref)):
        total = ref[...].astype(F32) + came_ref[...].astype(F32)
        rows = total.shape[1]
        keep_ref[...] = total[0]
        send_ref[start : start + rows, :] = total[1].astype(BF)
        start += rows


def join(a, b, after):
    inputs, out_shape = [], []
    for arrays in (a, b):
        cols = arrays[0].shape[-1]
        rows = arrays[0].size // cols // 2
        inputs += [r.reshape(2, rows, cols) for r in arrays]
        out_shape.append(jax.ShapeDtypeStruct((rows, cols), F32))
    out_shape.append(jax.ShapeDtypeStruct((sum(o.shape[0] for o in out_shape), cols), BF))
    vmem = pl.BlockSpec(memory_space=pltpu.VMEM)
    return pl.pallas_call(
        join_kernel,
        in_specs=[*[vmem] * 4, pl.BlockSpec(memory_space=pl.ANY)], out_specs=[vmem] * 3, out_shape=out_shape,
        compiler_params=params(8), cost_estimate=cost(3), name="join",
    )(*inputs, after)


def finish_kernel(own_ref, *refs):
    read = lambda ref: ref[0].astype(F32)
    exp_ref, in1_ref, both_ref = refs[2:5]
    tall = exp_ref.shape[0]
    red = read(refs[0]) + read(refs[1])
    exp = exp_ref[...] + both_ref[:tall, :].astype(F32)
    in1 = in1_ref[...] + both_ref[tall:, :].astype(F32)
    in2 = (read(refs[5]) + read(refs[6])) + (read(refs[7]) + read(refs[8]))
    refs = refs[9:]
    inp_ref, out_ref, exp_ref, red_ref, vec_ref, sq_ref = refs[1:]
    rows = in1.shape[0]
    vec = in2[rows : rows + vec_ref.shape[0], : vec_ref.shape[1]]
    vec_ref[...] = vec
    in2 = in2[:rows]
    even = jnp.concatenate([in1[:, :128], in2[:, :128], in1[:, 128:], in2[:, 128:]], axis=1)
    odd = jnp.concatenate([in2[:, :128], in1[:, :256], in2[:, 128:], in1[:, 256:]], axis=1)
    odd = pltpu.roll(odd, odd.shape[1] - HD, axis=1)
    inp = jnp.where((own_ref[0] & 1) == 1, odd, even)[:, : inp_ref.shape[1]]
    tall = exp_ref.shape[0]
    out = exp[tall:, :]
    half = out_ref.shape[1]
    out = jnp.concatenate([out[:, :half], pltpu.roll(out, half, axis=1)[:, :half]], axis=0)
    inp_ref[...] = inp
    out_ref[...] = out
    exp_ref[...] = exp[:tall, :]
    red_ref[...] = red
    squares = jnp.zeros((1, 1), F32)
    for g in (inp, out, exp[:tall, :], red, vec):
        squares = squares + jnp.sum(jnp.sum(g * g, axis=0, keepdims=True), axis=1, keepdims=True)
    sq_ref[...] = jnp.broadcast_to(squares, sq_ref.shape)


def finish(own, red, others, in2, after):
    piece = others[1].shape[0]
    tall = others[0].shape[0] - piece // 2
    vmem = pl.BlockSpec(memory_space=pltpu.VMEM)
    inputs = [*red, *others, *in2]
    return pl.pallas_call(
        finish_kernel,
        in_specs=[
            pl.BlockSpec(memory_space=pltpu.SMEM), *[vmem] * len(inputs), pl.BlockSpec(memory_space=pl.ANY)
        ],
        out_specs=[vmem] * 6,
        out_shape=[
            jax.ShapeDtypeStruct((piece, 9 * HD), F32),
            jax.ShapeDtypeStruct((piece, 3 * HD), F32),
            jax.ShapeDtypeStruct((tall, others[0].shape[1]), F32),
            jax.ShapeDtypeStruct(red[0].shape[1:], F32),
            jax.ShapeDtypeStruct((3, piece), F32),
            jax.ShapeDtypeStruct((8, LANES), F32),
        ],
        compiler_params=params(8), cost_estimate=cost(3), name="finish",
    )(own, *inputs, after)


def adam_step(master, moment_one, moment_two, gradient, step_rate, decay_weight):
    new_one = 0.9 * moment_one + 0.1 * gradient
    new_two = 0.999 * moment_two + 0.001 * gradient * gradient
    corrected_one = new_one / (1.0 - 0.9**STEP)
    corrected_two = new_two / (1.0 - 0.999**STEP)
    new_master = master - step_rate * (
        corrected_one / (jnp.sqrt(corrected_two) + 1e-08) + decay_weight * master
    )
    return (new_one, new_two, new_master, new_master.astype(BF))


def adam_kernel(rates, turned, squares_ref, *refs):
    n = len(rates)
    ins, outs = refs[: 4 * n], refs[4 * n :]
    norm = jnp.sqrt(squares_ref[0:1, 0:1])
    outs[0][...] = norm
    factor = 1.0 / jnp.maximum(norm, 1.0)
    for a in range(n):
        master, one, two, grad = (r[...] for r in ins[4 * a : 4 * a + 4])
        if turned[a]:
            grad = grad.T
        made = adam_step(master, one, two, grad * factor, rates[a][0], rates[a][1])
        for b in range(4):
            outs[1 + 4 * a + b][...] = made[b]


def adam_all(squares, states, grads, rates, turned):
    inputs, out_shape = [squares], [jax.ShapeDtypeStruct((1, 1), F32)]
    for state, grad in zip(states, grads):
        inputs += [*state, grad]
        shape = state[0].shape
        out_shape += [jax.ShapeDtypeStruct(shape, F32)] * 3 + [jax.ShapeDtypeStruct(shape, BF)]
    vmem = pl.BlockSpec(memory_space=pltpu.VMEM)
    return pl.pallas_call(
        functools.partial(adam_kernel, rates, turned),
        in_specs=[vmem] * len(inputs), out_specs=[vmem] * len(out_shape), out_shape=out_shape,
        compiler_params=params(16), cost_estimate=cost(5), name="adam",
    )(*inputs)


def mover(dp, seq):
    def move(value, bits_d, bits_s):
        pairs = [(d * seq + s, (d ^ bits_d) * seq + (s ^ bits_s)) for d in range(dp) for s in range(seq)]
        return lax.ppermute(value, AXES, pairs)

    return move


def tree_sum(move, value, token):
    value = value + move(value, 0, 1)
    value = (value + move(value, 2, 0)) + (move(value, 4, 0) + move(value, 6, 0))
    return (value + move(value, 0, 2)) + (move(value, 1, 0) + move(value, 1, 2)) + token


def spread_out(move, parts):
    return [parts[0], *(move(parts[b], 2 * b, 0) for b in (1, 2, 3))]


def plane(move, parts):
    return [parts[0], move(parts[1], 1, 0), move(parts[2], 0, 2), move(parts[3], 1, 2)]


def scatter_plain(parts, dim):
    part = lax.psum_scatter(parts, "seq", scatter_dimension=0, tiled=True)[0].astype(F32)
    return lax.psum_scatter(part, "dp", scatter_dimension=dim, tiled=True)


def in_order(kept, sent):
    parts = jnp.stack([kept, sent], axis=1)
    rows, cols = parts.shape[-2:]
    return parts.reshape(4, 2, 4, rows, cols).swapaxes(1, 2).reshape(4, 8 * rows, cols)


HALVES = tuple((parts, BF) for parts in ((0, 2), (4, 6), (1, 5), (3, 7)))
PAIR = (((0,), BF), ((1,), BF))
QUARTERS = tuple(((part,), BF) for part in range(4))
ONE = (((0,), BF),)
Z_HALVES = (((0, 1), BF), ((2, 3), BF))


def both_ways(move, cut):
    y_keep, y_send, x_keep, x_send = cut
    return (y_keep, move(y_send, 0, 2)), (x_keep, move(x_send, 1, 0))


def turned_ways(move, y_cut, x_cut):
    return (y_cut[0], move(y_cut[1], 1, 0)), (x_cut[0], move(x_cut[1], 0, 2))


def reduce_fast(move, kept_of, back, behind_of, input_weight, red_s, vec1):
    red_c = move(red_s, 0, 1)
    red_k, *turned = kept_of()
    (red,) = gather([((red_k, red_c), 8, HALVES)], red_k, 3)
    red_y, red_x = both_ways(move, red)

    gf, grad_mixed, exp_s, exp_k, vec2 = behind_of(red[0], turned)
    exp_c = move(exp_s, 0, 1)
    red_y, red_x = gather([(red_y, 2, PAIR), (red_x, 2, PAIR)], vec2, time=12)
    red_y, red_x = turned_ways(move, red_y, red_x)
    (exp,) = gather([((exp_k, exp_c), 8, HALVES)], red_y[0], 3)
    exp_y, exp_x = both_ways(move, exp)

    dq0, dkv0, vb0, gw = back(0, CALLS[0], grad_mixed, exp[0], last=False)
    (red_k,), (red_s,) = gather([(red_y, 1, ONE), (red_x, 1, ONE)], vb0)
    red = red_k, move(red_s, 4, 0)

    dq1, dkv1, vb1, in_s1, in_k1 = back(0, CALLS[1], grad_mixed, red_k, gw=gw, time=1)
    in_c1 = move(in_s1, 0, 1)
    exp_y, exp_x = gather([(exp_y, 2, PAIR), (exp_x, 2, PAIR)], vb1)
    exp_y, exp_x = turned_ways(move, exp_y, exp_x)

    gx, dx = frames_back(input_weight, gf, exp_y[0], CALLS[:2], (dq0, dq1), (dkv0, dkv1))
    (exp_k,), (exp_s,), in1, (red_k, red_s) = gather(
        [(exp_y, 1, ONE), (exp_x, 1, ONE), ((in_k1, in_c1), 4, QUARTERS), (red, 2, PAIR)], gx
    )
    exp = exp_k, move(exp_s, 4, 0)
    in1 = plane(move, in1)
    red = red_k, move(red_s, 2, 0)

    dq2, dkv2, vb2, in_s2, in_k2 = back(1, CALLS[2], grad_mixed, exp_k, vecs=(vec1, vec2, vb0, vb1))
    in_c2 = move(in_s2, 0, 1)
    ((in1_k, in1_s),) = gather([(in1, 4, Z_HALVES)], vb2, 1)
    in1 = in1_k, move(in1_s, 4, 0)
    (in2,) = gather([((in_k2, in_c2), 4, QUARTERS)], in1_k, 1)
    in2 = plane(move, in2)

    gx, dx_s, dx_k = frames_back(input_weight, gx, in2[0], CALLS[2:], (dq2,), (dkv2,), dx)
    dx_c = move(dx_s, 0, 1)
    exp_k, in1_k, both_s = join(exp, in1, gx)
    both_c = move(both_s, 2, 0)
    (in2,) = gather([(in2, 4, QUARTERS)], exp_k, 1)
    in2 = spread_out(move, in2)
    ((dx_k, dx_s),) = gather([((dx_k, dx_c), 2, (((0,), F32), ((1,), BF)))], in2[0])
    return red, (exp_k, in1_k, both_c), in2, gx, (dx_k, move(dx_s, 0, 2))


def reduce_plain(move, kept_of, back, behind_of, input_weight, red_s, vec1):
    red_k, *turned = kept_of()
    gf, grad_mixed, exp_s, exp_k, vec2 = behind_of(red_k, turned)
    dq0, dkv0, vb0, gw = back(0, CALLS[0], grad_mixed, vec2, last=False)
    dq1, dkv1, vb1, in_s1, in_k1 = back(0, CALLS[1], grad_mixed, vb0, gw=gw)
    dq2, dkv2, vb2, in_s2, in_k2 = back(1, CALLS[2], grad_mixed, vb1, vecs=(vec1, vec2, vb0, vb1))
    gx, dx = frames_back(input_weight, gf, vb2, CALLS[:2], (dq0, dq1), (dkv0, dkv1))
    gx, dx_s, dx_k = frames_back(input_weight, gx, vb2, CALLS[2:], (dq2,), (dkv2,), dx)
    ((dx_keep, dx_send),) = gather([((dx_k, move(dx_s, 0, 1)), 2, (((0,), F32), ((1,), BF)))], vb2)
    dx = dx_keep, move(dx_send, 0, 2)
    red = scatter_plain(in_order(red_k, red_s), 0)
    in1 = scatter_plain(in_order(in_k1, in_s1), 0)
    both = in_order(in_k2, in_s2)
    both = both.reshape(4, 8, -1, both.shape[-1])
    piece = in_k1.shape[2]
    in2 = scatter_plain(both[:, :, :piece].reshape(4, 8 * piece, -1), 0)
    vec = scatter_plain(both[:, :, piece : piece + 3, :piece].swapaxes(1, 2).reshape(4, 3, -1), 1)
    both = jnp.stack([exp_k, exp_s], axis=1).transpose(0, 1, 3, 2, 4, 5)
    tall, wide = both.shape[-2] - piece // 2, both.shape[-1]
    both = both.reshape(4, 8, -1, wide)
    exp = scatter_plain(both[:, :, :tall].swapaxes(1, 2).reshape(4, tall, 8 * wide), 1)
    out = both[:, :, tall:].reshape(4, 8, piece // 2, 2, wide // 2).swapaxes(2, 3)
    out = scatter_plain(out.reshape(4, 8 * piece, wide // 2), 0)
    even = jnp.concatenate([in1[:, :128], in2[:, :128], in1[:, 128:], in2[:, 128:192]], axis=1)
    odd = jnp.concatenate([in2[:, 64:128], in1[:, :256], in2[:, 128:], in1[:, 256:]], axis=1)
    inp = jnp.where(lax.axis_index("seq") % 2 == 1, odd, even)
    squares = sum(jnp.sum(g * g) for g in (inp, out, exp, red, vec))
    squares = lax.psum(jnp.full((8, LANES), squares, F32), AXES)
    return inp, out, exp, red, vec, squares, gx, dx


def local(
    frames, cotangent, lengths,
    input_weight, output_weight, expand_weight, reduce_weight, vector_copy,
    *states,
):
    rows, width = frames.shape
    seq, dp = lax.axis_size("seq"), lax.axis_size("dp")
    move = mover(dp, seq)
    own_s, own_d = lax.axis_index("seq"), lax.axis_index("dp")
    fast = dp == 8

    across = move(frames, 0, 2)
    near = move(frames, 0, 1)
    own = jnp.stack([own_s, own_d]).astype(jnp.int32) if fast else jnp.zeros((2,), jnp.int32)

    e0, k0, v0, xt0, q, *stats, qhot, vectors = attend(lengths, (frames, near), input_weight, vector_copy)
    across = pass_on(across, stats[0])
    far = move(across, 0, 1)
    rest = qhot, q, *stats, *project(across, input_weight, vectors, stats[0])
    e1, k1, v1, xt1, mixed, rinv0, rinv1 = attend(lengths, (far,), input_weight, vectors, rest)
    halves = (e0, k0, v0, rinv0, xt0), (e1, k1, v1, rinv1, xt1)
    layer, act, slope, norm1, inv1, hl, gs, gb, gbt, red_s, vec1 = ahead(
        own, mixed, frames, cotangent, qhot, output_weight, expand_weight, reduce_weight, vectors
    )

    def kept_of():
        return reduce_kept(own, gbt, act, hl, mixed)

    def behind_of(after, turned):
        return behind(
            own, slope, gb, gs, norm1, inv1, *turned, output_weight, expand_weight, reduce_weight, vectors, after
        )

    def back(group, pairs, grad_mixed, after, **more):
        return attend_back(group, pairs, own, q, grad_mixed, mixed, halves, after, **more)

    if fast:
        red, others, in2, gx, dx = reduce_fast(move, kept_of, back, behind_of, input_weight, red_s, vec1)
        inp, out, exp, red, vec, squares = finish(own, red, others, in2, dx[0])
        frames_gradient, token = frames_end(gx, *dx)
        squares = tree_sum(move, squares, token)
    else:
        inp, out, exp, red, vec, squares, gx, dx = reduce_plain(
            move, kept_of, back, behind_of, input_weight, red_s, vec1
        )
        frames_gradient, token = frames_end(gx, *dx)
        squares = squares + token

    grads = [inp, out, exp, red, vec]
    masters, firsts, seconds = (list(states[i : i + 5]) for i in (0, 5, 10))
    for group in (masters, firsts, seconds):
        group[3] = group[3].T
    hidden = expand_weight.shape[1]
    wide, narrow = 2.0 * width**-0.5, 2.0 * hidden**-0.5
    norm, *made = adam_all(
        squares, list(zip(masters, firsts, seconds)), grads,
        ((wide, 0.01), (wide, 0.01), (wide, 0.01), (narrow, 0.01), (0.5, 0.0)),
        (False, True, False, False, False),
    )
    made[12:16] = [m.T for m in made[12:16]]
    return (layer, frames_gradient, norm.reshape(()), *made)


def solution(mesh):
    tokens, whole = P(("dp", "seq"), None), P()
    state = (P("dp", "seq"), *(P("seq", "dp"),) * 4)
    outs = tuple(s for s in state for _ in range(4))
    return jax.shard_map(
        local,
        mesh=mesh,
        in_specs=(tokens, tokens, P("dp", None), *(whole,) * 5, *state * 3),
        out_specs=(tokens, tokens, whole, *outs),
        check_vma=False,
    )
```
